32 devices in a mesh: grp: 4 (over x, core), mem: 8 (over z, y).
Axes of the slice: x: 2, y: 2, z: 4, core: 2. Of those that a mesh axis runs over, the one named last changes fastest.
Arguments:
- embeddings: bfloat16 [32768, 768], P(('grp', 'mem'))
- cluster: int32 [32768], P(('grp', 'mem')), may hold values from -1 to 7, as said below
- rank: int32 [32768], P(('grp', 'mem')), may hold values from -1 to 4095, as said below
Outputs:
- best_match: float32 [32768], P(('grp', 'mem'))
The draws below stay inside these ranges and needn't reach their ends.
Inputs may be any that keep to these rules, and one draw needn't show every extreme that they name: cluster is -1 exactly where rank is -1. Ranks are distinct within a cluster; among the rows of one device, at most 16 have the same cluster // 2 and the same rank // 256, and every device reaches 16 for some such pair.
All inputs are finite; a program needn't handle non-finite values.
Results may differ from the reference program's by a relative error of at most 0.0004.
Values may be sent and summed in bfloat16 or wider, within the bound.
No kernel may reach another device: no remote copies, remote signals or barrier semaphores. Data moves between devices by JAX's collectives and lax.ppermute only.
A program may use at most 128 MiB of HBM per device.

```python
import math
import jax
import jax.numpy as jnp
from jax import lax

D = 768
CLUS_GRP = 2
ROWS_DEV = 1024
ROWS = 32768
CLUSTERS = 8
CAP = 4096
HALF = 256
QH = 16
PROTOS = 512
N_GRP = 4
N_MEM = 8
DEVICES = 32


def layout_draw(key):
    base = jax.random.fold_in(key, 7)
    keys = jax.random.split(base, 5)
    units = N_GRP * 2 * N_MEM
    unit_slots = CLUS_GRP * HALF
    counts = jax.random.randint(keys[0], (DEVICES, units), QH - QH // 2, QH + 1)
    sources = jnp.arange(DEVICES)
    first = jax.random.randint(keys[1], (DEVICES,), 0, DEVICES)
    unit_a = first // N_MEM * 2 * N_MEM + 2 * (first % N_MEM)
    counts = counts.at[sources, unit_a].set(QH)
    counts = counts.at[sources, unit_a + 1].set(QH)
    second = jax.random.randint(keys[2], (DEVICES,), 0, DEVICES)
    unit_c = second // N_MEM * 2 * N_MEM + second % N_MEM
    unit_d = second // N_MEM * 2 * N_MEM + 2 * N_MEM - 1 - second % N_MEM
    counts = counts.at[sources, unit_c].set(QH)
    counts = counts.at[sources, unit_d].set(QH)
    inclusive = jnp.cumsum(counts, axis=1)
    exclusive = inclusive - counts
    spots = jnp.arange(ROWS_DEV)
    target = jnp.sum((inclusive[:, None, :] <= spots[None, :, None]).astype(jnp.int32), axis=2)
    alive = target < units
    clipped = jnp.minimum(target, units - 1)
    within = spots[None, :] - jnp.take_along_axis(exclusive, clipped, axis=1)
    arrival = jnp.cumsum(counts, axis=0) - counts
    order = jnp.take_along_axis(arrival, clipped, axis=1) + within
    slot = jnp.clip(order, 0, unit_slots - 1)
    group_id = clipped // (2 * N_MEM)
    half_id = clipped % (2 * N_MEM)
    cluster = group_id * CLUS_GRP + slot // HALF
    rank = half_id * HALF + slot % HALF
    cluster = jnp.where(alive, cluster, -1)
    rank = jnp.where(alive, rank, -1)
    mixing = jax.vmap(lambda k: jax.random.permutation(k, ROWS_DEV))(jax.random.split(keys[4], DEVICES))
    cluster = jnp.take_along_axis(cluster, mixing, axis=1).reshape(-1)
    rank = jnp.take_along_axis(rank, mixing, axis=1).reshape(-1)
    return (cluster.astype(jnp.int32), rank.astype(jnp.int32))


def draw_cluster(key, part):
    return layout_draw(key)[0]


def draw_rank(key, part):
    return layout_draw(key)[1]


def draw_embeddings(key, part):
    cluster, rank = layout_draw(key)
    keys = jax.random.split(jax.random.fold_in(key, 11), 6)
    safe = jnp.maximum(cluster, 0)
    centers = jax.random.normal(keys[0], (CLUSTERS, D), jnp.float32)
    protos = jax.random.normal(keys[1], (CLUSTERS, PROTOS, D), jnp.float32)
    which = jax.random.randint(keys[2], (ROWS,), 0, PROTOS)
    noise = jax.random.normal(keys[3], (ROWS, D), jnp.float32)
    spread = jnp.exp(jax.random.uniform(keys[4], (ROWS, 1), jnp.float32, jnp.log(0.15), jnp.log(0.8)))
    size = jnp.exp(jax.random.uniform(keys[5], (ROWS, 1), jnp.float32, jnp.log(0.5), jnp.log(4.0)))
    values = (0.5 * centers[safe] + protos[safe, which] + spread * noise) * size
    return values.astype(jnp.bfloat16)


def setup_inputs(seed: int = 0) -> dict:
    key_list = jax.random.split(jax.random.key(seed), 4)
    return {
        "embeddings": draw_embeddings(jax.random.fold_in(key_list[3], 71), 0),
        "cluster": draw_cluster(jax.random.fold_in(key_list[3], 71), 0),
        "rank": draw_rank(jax.random.fold_in(key_list[3], 71), 0),
    }


def unit_rows(embeddings):
    wide = embeddings.astype(jnp.float32)
    total = lax.optimization_barrier(jnp.sum(wide * wide, axis=1, keepdims=True))
    return (wide * lax.rsqrt(total + 1e-06)).astype(jnp.bfloat16)

def reference(embeddings, cluster, rank):
    unit = unit_rows(embeddings)
    alive = cluster >= 0
    flat = jnp.where(alive, jnp.maximum(cluster, 0) * CAP + jnp.maximum(rank, 0), CLUSTERS * CAP).astype(jnp.int32)
    grid = jnp.zeros((CLUSTERS * CAP + 1, D), jnp.bfloat16).at[flat].set(unit)[:-1].reshape(CLUSTERS, CAP, D)
    present = jnp.zeros((CLUSTERS * CAP + 1,), jnp.int32).at[flat].set(1)[:-1].reshape(CLUSTERS, CAP)
    block = math.gcd(CAP, 512)

    def per_cluster(operands):
        table, live = operands

        def per_block(index):
            rows = lax.dynamic_slice_in_dim(table, index * block, block, 0)
            sims = jnp.dot(rows, table.T, preferred_element_type=jnp.float32)
            row_rank = index * block + jnp.arange(block, dtype=jnp.int32)
            col_rank = jnp.arange(CAP, dtype=jnp.int32)
            keep = (col_rank[None, :] < row_rank[:, None]) & (live[None, :] > 0)
            return lax.optimization_barrier(jnp.max(jnp.where(keep, sims, jnp.float32(-1.0)), axis=1))
        return lax.map(per_block, jnp.arange(CAP // block, dtype=jnp.int32)).reshape(CAP)
    best = lax.map(per_cluster, (grid, present)).reshape(-1)
    picked = best[jnp.minimum(flat, CLUSTERS * CAP - 1)]
    return jnp.where(alive, picked, jnp.float32(-1.0))
```

```python
import functools

import jax
import jax.numpy as jnp
from jax import lax
from jax.experimental import pallas as pl
from jax.experimental.pallas import tpu as pltpu
from jax.sharding import PartitionSpec as P

CLUS_GRP = 2
TILES = 4
LABEL_ROWS = 16
FAR = 1.0e9
NT = (((1,), (1,)), ((), ()))


def cover(members):
    bits = [1 << i for i in range(members.bit_length() - 1)]
    offsets = [0] + bits

    def missing(held):
        return set(range(members)) - {a ^ b for a in held for b in held}

    while missing(offsets):
        offsets.append(
            min(
                (d for d in range(members) if d not in offsets),
                key=lambda d: (len(missing(offsets + [d])), bin(d).count("1"), -d),
            )
        )
    pairs = {}
    for delta in range(members):
        pairs[delta] = min(
            (a, a ^ delta) for a in offsets if a ^ delta in offsets
        )
    return offsets, pairs


def pack_kernel(sizes, block_ref, emb_ref, cluster_ref, rank_ref, *out_refs):
    groups, halves, half, cap, blk = sizes
    dest_ref, sends = out_refs[0], out_refs[1:]
    rows = emb_ref.shape[0]
    cluster = cluster_ref[...]
    rank = rank_ref[...]
    alive = cluster >= 0
    pair = lax.shift_right_logical(jnp.maximum(cluster, 0), 1)
    parity = jnp.maximum(cluster, 0) - 2 * pair
    safe_rank = jnp.maximum(rank, 0)
    which = safe_rank // half
    units = groups * halves
    unit_id = jnp.where(alive, (pair ^ block_ref[0]) * halves + which, -1)
    step = 256
    before_rows = lax.broadcasted_iota(jnp.int32, (step, step), 0)
    before_cols = lax.broadcasted_iota(jnp.int32, (step, step), 1)
    upper = (before_rows < before_cols).astype(jnp.float32).astype(jnp.bfloat16)
    unit_iota = lax.broadcasted_iota(jnp.int32, (units, step), 0)
    carry = jnp.zeros((units, 1), jnp.float32)
    places = []
    for j in range(rows // step):
        mine = unit_id[:, j * step : (j + 1) * step]
        hit = (unit_iota == mine).astype(jnp.float32)
        before = jnp.dot(hit.astype(jnp.bfloat16), upper, preferred_element_type=jnp.float32) + carry
        position = jnp.sum(hit * before, axis=0, keepdims=True)
        carry = carry + jnp.sum(hit, axis=1, keepdims=True)
        places.append(jnp.where(mine >= 0, mine * cap + position.astype(jnp.int32), -1))
    dest = jnp.concatenate(places, axis=1)
    dest_ref[...] = dest

    wide = emb_ref[...].astype(jnp.float32)
    total = jnp.sum(wide * wide, axis=1, keepdims=True)
    unit = (wide * lax.rsqrt(total + 1e-06)).astype(jnp.bfloat16)

    field = lax.broadcasted_iota(jnp.int32, (LABEL_ROWS, rows), 0)
    labels = jnp.where(
        field == 0, safe_rank - which * half, jnp.where(field == 1, parity + 1, 0)
    )
    labels = jnp.where(alive, labels, 0).astype(jnp.float32).astype(jnp.bfloat16)
    per_tile = blk // TILES
    wide_tile = groups * per_tile
    spread = (
        lax.broadcasted_iota(jnp.int32, (blk, wide_tile), 0) % per_tile
        == lax.broadcasted_iota(jnp.int32, (blk, wide_tile), 1) % per_tile
    )
    spread = spread.astype(jnp.float32).astype(jnp.bfloat16)
    own_tile = lax.broadcasted_iota(jnp.int32, (LABEL_ROWS, blk), 0) == lax.div(
        lax.broadcasted_iota(jnp.int32, (LABEL_ROWS, blk), 1), per_tile
    )
    slot = lax.broadcasted_iota(jnp.int32, (blk, rows), 0)
    for k in range(groups):
        pick = (slot + k * blk == dest).astype(jnp.float32).astype(jnp.bfloat16)
        sends[k][0:blk, :] = jnp.dot(pick, unit, preferred_element_type=jnp.float32).astype(
            jnp.bfloat16
        )
        mine = lax.dot_general(labels, pick, NT, preferred_element_type=jnp.float32)
        parts = []
        for f in range(2):
            line = jnp.where(own_tile, mine[f : f + 1, :], 0.0).astype(jnp.bfloat16)
            parts.append(jnp.dot(line, spread, preferred_element_type=jnp.float32))
        width = sends[k].shape[1]
        parts.append(jnp.zeros((LABEL_ROWS, width - 2 * wide_tile), jnp.float32))
        sends[k][blk : blk + LABEL_ROWS, :] = jnp.concatenate(parts, axis=1).astype(jnp.bfloat16)


def pack(block, embeddings, cluster, rank, sizes):
    groups, halves, half, cap, blk = sizes
    rows, width = embeddings.shape
    vmem = pl.BlockSpec(memory_space=pltpu.VMEM)
    out_shape = [jax.ShapeDtypeStruct((1, rows), jnp.int32)]
    out_shape += [jax.ShapeDtypeStruct((blk + LABEL_ROWS, width), jnp.bfloat16)] * groups
    return pl.pallas_call(
        functools.partial(pack_kernel, sizes),
        out_shape=out_shape,
        in_specs=[pl.BlockSpec(memory_space=pltpu.SMEM), vmem, vmem, vmem],
        out_specs=[vmem] * len(out_shape),
        compiler_params=pltpu.CompilerParams(vmem_limit_bytes=48 * 1024 * 1024),
    )(block, embeddings, cluster.reshape(1, rows), rank.reshape(1, rows))


def compare_kernel(sizes, plan, n_sets, *refs):
    groups, halves, half, cap, blk = sizes
    blocks = [refs[i * groups : (i + 1) * groups] for i in range(n_sets)]
    n_out = len(plan)
    outs = refs[n_sets * groups : n_sets * groups + n_out]
    table, key_col, key_row, low_row, best, sems = refs[n_sets * groups + n_out :]
    rows = groups * blk
    per_tile = blk // TILES
    tile = rows // TILES

    for i in range(n_sets):
        for t in range(TILES):
            for k in range(groups):
                pltpu.make_async_copy(
                    blocks[i][k].at[pl.ds(t * per_tile, per_tile)],
                    table.at[pl.ds(i * rows + t * tile + k * per_tile, per_tile)],
                    sems.at[i],
                ).start()

    lane = lax.broadcasted_iota(jnp.int32, (LABEL_ROWS, tile), 1)
    line = lax.broadcasted_iota(jnp.int32, (LABEL_ROWS, tile), 0)
    from_block = lax.div(lane, per_tile)
    which = line * (halves // TILES) + lax.div(lane - from_block * per_tile, cap)
    for i in range(n_sets):
        rest = jnp.zeros((LABEL_ROWS, tile), jnp.float32)
        code = jnp.zeros((LABEL_ROWS, tile), jnp.float32)
        for k in range(groups):
            label = blocks[i][k][blk : blk + LABEL_ROWS, 0 : 2 * tile].astype(jnp.float32)
            rest = jnp.where(from_block == k, label[:, :tile], rest)
            code = jnp.where(from_block == k, label[:, tile:], code)
        cap_all = float(halves * half)
        low = (code - 1.0) * cap_all
        key = low + (which * half).astype(jnp.float32) + rest
        live = code > 0.5
        key = jnp.where(live, key, FAR)
        key_row[i] = key[0:8]
        low_row[i] = low[0:8]
        for t in range(TILES):
            for part in range(tile // 128):
                square = jnp.broadcast_to(key[t : t + 1, part * 128 : (part + 1) * 128], (128, 128))
                key_col[pl.ds(i * rows + t * tile + part * 128, 128), :] = square.T

    for i in range(n_sets):
        here = table.at[pl.ds(i * rows, rows)]
        pltpu.make_async_copy(here, here, sems.at[i]).wait()

    for o, (a, cols) in enumerate(plan):

        def one_tile(t, _, a=a, cols=cols, o=o):
            queries = table[pl.ds(pl.multiple_of(a * rows + t * tile, tile), tile), :]
            mine = key_row[a, pl.ds(t, 1), :]
            floor = low_row[a, pl.ds(t, 1), :]

            def one_col(s, acc):
                for b in cols:
                    at = pl.multiple_of(b * rows + s * tile, tile)
                    sims = lax.dot_general(
                        table[pl.ds(at, tile), :], queries, NT, preferred_element_type=jnp.float32
                    )
                    theirs = key_col[pl.ds(at, tile), :]
                    theirs = jnp.concatenate([theirs] * (tile // 128), axis=1)
                    keep = (theirs >= floor) & (theirs < mine)
                    sims = jnp.where(keep, sims, -1.0)
                    acc = jnp.maximum(acc, jnp.max(sims.reshape(tile // 8, 8, tile), axis=0))
                return acc

            acc = lax.fori_loop(0, t + 1, one_col, jnp.full((8, tile), -1.0, jnp.float32))
            best[o, pl.ds(t, 1), :] = jnp.max(acc, axis=0, keepdims=True)
            return 0

        lax.fori_loop(0, TILES, one_tile, 0)

    lane = lax.broadcasted_iota(jnp.int32, (8, tile), 1)
    for o in range(n_out):
        found = best[o]
        for k in range(groups):
            total = jnp.full((1, tile), -1.0, jnp.float32)
            for t in range(TILES):
                turn = ((t - k) * per_tile) % tile
                moved = pltpu.roll(found, turn, 1) if turn else found
                total = jnp.where(lax.div(lane, per_tile)[0:1] == t, moved[t : t + 1], total)
            outs[o][k : k + 1, :] = total[:, :blk]


def compare(sets, plan, sizes):
    groups, halves, half, cap, blk = sizes
    n_sets = len(sets)
    flat = [piece for one in sets for piece in one]
    rows, width = groups * blk, flat[0].shape[1]
    tile = rows // TILES
    vmem = pl.BlockSpec(memory_space=pltpu.VMEM)
    combos = sum(len(cols) for _, cols in plan) * TILES * (TILES + 1) // 2
    return pl.pallas_call(
        functools.partial(compare_kernel, sizes, plan, n_sets),
        out_shape=[jax.ShapeDtypeStruct((groups, blk), jnp.float32)] * len(plan),
        in_specs=[vmem] * len(flat),
        out_specs=[vmem] * len(plan),
        scratch_shapes=[
            pltpu.VMEM((n_sets * rows, width), jnp.bfloat16),
            pltpu.VMEM((n_sets * rows, 128), jnp.float32),
            pltpu.VMEM((n_sets, 8, tile), jnp.float32),
            pltpu.VMEM((n_sets, 8, tile), jnp.float32),
            pltpu.VMEM((len(plan), 8, tile), jnp.float32),
            pltpu.SemaphoreType.DMA((n_sets,)),
        ],
        compiler_params=pltpu.CompilerParams(vmem_limit_bytes=48 * 1024 * 1024),
        cost_estimate=pl.CostEstimate(
            flops=2 * combos * tile * tile * width, bytes_accessed=2 * n_sets * rows * width, transcendentals=0
        ),
    )(*flat)


def unpack_kernel(sizes, dest_ref, *refs):
    groups, halves, half, cap, blk = sizes
    out_ref = refs[-1]
    pieces = refs[:-1]
    rows = dest_ref.shape[1]
    dest = dest_ref[...]
    slot = lax.broadcasted_iota(jnp.int32, (blk, rows), 0)
    field = lax.broadcasted_iota(jnp.int32, (LABEL_ROWS, blk), 0)
    total = jnp.zeros((LABEL_ROWS, rows), jnp.float32)
    for k in range(groups):
        value = pieces[k][...]
        for more in range(k + groups, len(pieces), groups):
            value = jnp.maximum(value, pieces[more][...])
        top = value.astype(jnp.bfloat16).astype(jnp.float32)
        rest = value - top
        mid = rest.astype(jnp.bfloat16).astype(jnp.float32)
        low = rest - mid
        stack = jnp.where(field == 0, top, jnp.where(field == 1, mid, jnp.where(field == 2, low, 0.0)))
        pick = (slot + k * blk == dest).astype(jnp.float32).astype(jnp.bfloat16)
        total = total + jnp.dot(stack.astype(jnp.bfloat16), pick, preferred_element_type=jnp.float32)
    value = (total[0:1] + total[1:2]) + total[2:3]
    out_ref[...] = jnp.where(dest >= 0, value, -1.0)


def unpack(dest, pieces, sizes):
    vmem = pl.BlockSpec(memory_space=pltpu.VMEM)
    return pl.pallas_call(
        functools.partial(unpack_kernel, sizes),
        out_shape=jax.ShapeDtypeStruct(dest.shape, jnp.float32),
        in_specs=[vmem] * (1 + len(pieces)),
        out_specs=vmem,
        compiler_params=pltpu.CompilerParams(vmem_limit_bytes=48 * 1024 * 1024),
    )(dest, *pieces)


def on_device(embeddings, cluster, rank):
    rows_dev, width = embeddings.shape
    groups = lax.axis_size("grp")
    members = lax.axis_size("mem")
    devices = groups * members
    halves = 2 * members
    half = rows_dev // CLUS_GRP // 2
    blk = rows_dev // groups
    cap = blk // halves
    sizes = (groups, halves, half, cap, blk)
    side = members // groups

    def swap(value, block_step, member_step):
        mask = member_step // side * members + block_step * side + member_step % side
        if mask == 0:
            return value
        return lax.ppermute(value, ("grp", "mem"), [(i, i ^ mask) for i in range(devices)])

    offsets, pairs = cover(members)
    block = (lax.axis_index("mem") // side).astype(jnp.int32).reshape(1)
    packed = pack(block, embeddings, cluster, rank, sizes)
    dest, sends = packed[0], packed[1:]

    held = {0: [swap(sends[k], k, 0) for k in range(groups)]}
    for d in offsets[1:]:
        via = next((e for e in held if bin(d ^ e).count("1") == 1 and (e == 0 or d ^ e > 1)), 0)
        held[d] = [swap(piece, 0, d ^ via) for piece in held[via]]

    index = {d: i for i, d in enumerate(offsets)}
    starts = sorted({a for a, _ in pairs.values()})
    plan = [(index[a], [index[b] for _, (e, b) in sorted(pairs.items()) if e == a]) for a in starts]
    found = compare([held[d] for d in offsets], plan, sizes)

    best = {}
    for a, value in zip(starts, found):
        near = a % side
        value = swap(value, 0, a - near)
        best[near] = jnp.maximum(best[near], value) if near in best else value

    pieces = []
    for near in sorted(best):
        for k in range(groups):
            pieces.append(swap(best[near][k : k + 1], k, near))
    return unpack(dest, pieces, sizes).reshape(rows_dev)


def solution(mesh):
    in_specs = (P(("grp", "mem"), None), P(("grp", "mem")), P(("grp", "mem")))
    out_specs = P(("grp", "mem"))
    return jax.shard_map(
        on_device, mesh=mesh, in_specs=in_specs, out_specs=out_specs, check_vma=False
    )
```

```python
import functools

import jax
import jax.numpy as jnp
from jax import lax
from jax.experimental import pallas as pl
from jax.experimental.pallas import tpu as pltpu
from jax.sharding import PartitionSpec as P

CLUS_GRP = 2
TILES = 4
LABEL_ROWS = 16
FAR = 1.0e9
NT = (((1,), (1,)), ((), ()))
TN = (((0,), (0,)), ((), ()))


def cover(members):
    bits = [1 << i for i in range(members.bit_length() - 1)]
    offsets = [0] + bits

    def missing(held):
        return set(range(members)) - {a ^ b for a in held for b in held}

    while missing(offsets):
        offsets.append(
            min(
                (d for d in range(members) if d not in offsets),
                key=lambda d: (len(missing(offsets + [d])), bin(d).count("1"), -d),
            )
        )
    pairs = {}
    for delta in range(members):
        pairs[delta] = min(
            (a, a ^ delta) for a in offsets if a ^ delta in offsets
        )
    return offsets, pairs


def pack_kernel(sizes, place_ref, emb_hbm, cluster_hbm, rank_hbm, *refs):
    groups, halves, half, cap, blk = sizes
    dest_ref, sends = refs[0], refs[1 : 1 + groups]
    emb_ref, cluster_ref, rank_ref, sems = refs[1 + groups :]
    rows = emb_ref.shape[0]
    step = 256
    loads = [
        pltpu.make_async_copy(cluster_hbm, cluster_ref, sems.at[0]),
        pltpu.make_async_copy(rank_hbm, rank_ref, sems.at[1]),
    ]
    for j in range(rows // step):
        at = pl.ds(j * step, step)
        loads.append(pltpu.make_async_copy(emb_hbm.at[at], emb_ref.at[at], sems.at[2 + j]))
    for load in loads:
        load.start()
    for load in loads[:2]:
        load.wait()
    cluster = cluster_ref[...]
    rank = rank_ref[...]
    alive = cluster >= 0
    pair = lax.shift_right_logical(jnp.maximum(cluster, 0), 1)
    parity = jnp.maximum(cluster, 0) - 2 * pair
    safe_rank = jnp.maximum(rank, 0)
    which = safe_rank // half
    units = groups * halves
    unit_id = jnp.where(alive, pair * halves + which, -1)
    before_rows = lax.broadcasted_iota(jnp.int32, (step, step), 0)
    before_cols = lax.broadcasted_iota(jnp.int32, (step, step), 1)
    upper = (before_rows < before_cols).astype(jnp.float32).astype(jnp.bfloat16)
    unit_iota = lax.broadcasted_iota(jnp.int32, (units, step), 0)
    carry = jnp.zeros((units, 1), jnp.float32)
    places = []
    for j in range(rows // step):
        mine = unit_id[:, j * step : (j + 1) * step]
        hit = (unit_iota == mine).astype(jnp.float32)
        before = jnp.dot(hit.astype(jnp.bfloat16), upper, preferred_element_type=jnp.float32) + carry
        position = jnp.sum(hit * before, axis=0, keepdims=True)
        carry = carry + jnp.sum(hit, axis=1, keepdims=True)
        places.append(jnp.where(mine >= 0, mine * cap + position.astype(jnp.int32), -1))
    dest = jnp.concatenate(places, axis=1)
    dest_ref[...] = dest
    dest = jnp.where(dest >= 0, dest ^ (place_ref[0] * blk), -1)

    units_of = []
    for j in range(rows // step):
        loads[2 + j].wait()
        wide = emb_ref[j * step : (j + 1) * step, :].astype(jnp.float32)
        total = jnp.sum(wide * wide, axis=1, keepdims=True)
        units_of.append((wide * lax.rsqrt(total + 1e-06)).astype(jnp.bfloat16))
    unit = jnp.concatenate(units_of, axis=0)

    field = lax.broadcasted_iota(jnp.int32, (LABEL_ROWS, rows), 0)
    labels = jnp.where(
        field == 0, safe_rank - which * half, jnp.where(field == 1, parity + 1, 0)
    )
    labels = jnp.where(alive, labels, 0).astype(jnp.float32).astype(jnp.bfloat16)
    per_tile = blk // TILES
    wide_tile = groups * per_tile
    spread = (
        lax.broadcasted_iota(jnp.int32, (blk, wide_tile), 0) % per_tile
        == lax.broadcasted_iota(jnp.int32, (blk, wide_tile), 1) % per_tile
    )
    spread = spread.astype(jnp.float32).astype(jnp.bfloat16)
    label_row = lax.broadcasted_iota(jnp.int32, (LABEL_ROWS, blk), 0)
    label_col = lax.broadcasted_iota(jnp.int32, (LABEL_ROWS, blk), 1)
    own_tile = label_row == lax.div(label_col, per_tile)
    unit_col = lax.div(label_col, cap).astype(jnp.float32)
    slot = lax.broadcasted_iota(jnp.int32, (blk, rows), 0)
    width = sends[0].shape[1]
    for k in range(groups):
        pick = (slot + k * blk == dest).astype(jnp.float32).astype(jnp.bfloat16)
        sends[k][0:blk, :] = jnp.dot(pick, unit, preferred_element_type=jnp.float32).astype(
            jnp.bfloat16
        )
        mine = lax.dot_general(labels, pick, NT, preferred_element_type=jnp.float32)
        plain = jnp.where(label_row == 2, unit_col, mine)
        parts = [plain] + [jnp.zeros_like(plain)] * ((wide_tile - blk) // blk)
        for f in range(2):
            line = jnp.where(own_tile, mine[f : f + 1, :], 0.0).astype(jnp.bfloat16)
            parts.append(jnp.dot(line, spread, preferred_element_type=jnp.float32))
        if width > 3 * wide_tile:
            parts.append(jnp.zeros((LABEL_ROWS, width - 3 * wide_tile), jnp.float32))
        sends[k][blk : blk + LABEL_ROWS, :] = jnp.concatenate(parts, axis=1).astype(jnp.bfloat16)


def pack(place, embeddings, cluster, rank, sizes):
    groups, halves, half, cap, blk = sizes
    rows, width = embeddings.shape
    vmem = pl.BlockSpec(memory_space=pltpu.VMEM)
    hbm = pl.BlockSpec(memory_space=pltpu.HBM)
    out_shape = [jax.ShapeDtypeStruct((1, rows), jnp.int32)]
    out_shape += [jax.ShapeDtypeStruct((blk + LABEL_ROWS, width), jnp.bfloat16)] * groups
    return pl.pallas_call(
        functools.partial(pack_kernel, sizes),
        out_shape=out_shape,
        in_specs=[pl.BlockSpec(memory_space=pltpu.SMEM), hbm, hbm, hbm],
        out_specs=[vmem] * len(out_shape),
        scratch_shapes=[
            pltpu.VMEM((rows, width), jnp.bfloat16),
            pltpu.VMEM((1, rows), jnp.int32),
            pltpu.VMEM((1, rows), jnp.int32),
            pltpu.SemaphoreType.DMA((2 + rows // 256,)),
        ],
        compiler_params=pltpu.CompilerParams(vmem_limit_bytes=48 * 1024 * 1024),
    )(place, embeddings, cluster.reshape(1, rows), rank.reshape(1, rows))


def compare_kernel(sizes, plan, n_sets, joined, place_ref, *refs):
    groups, halves, half, cap, blk = sizes
    blocks = [refs[i * groups : (i + 1) * groups] for i in range(n_sets)]
    n_out = 1 if joined else len(plan)
    outs = refs[n_sets * groups : n_sets * groups + n_out]
    key_col, key_row, low_row, turned, best = refs[n_sets * groups + n_out :]
    rows = groups * blk
    per_tile = blk // TILES
    tile = rows // TILES
    cap_all = float(halves * half)

    lane = lax.broadcasted_iota(jnp.int32, (LABEL_ROWS, tile), 1)
    line = lax.broadcasted_iota(jnp.int32, (LABEL_ROWS, tile), 0)
    from_block = lax.div(lane, per_tile)
    which = line * (halves // TILES) + lax.div(lane - from_block * per_tile, cap)
    weight_row = lax.broadcasted_iota(jnp.int32, (LABEL_ROWS, 128), 0)
    weights = jnp.where(
        weight_row == 0,
        1.0,
        jnp.where(weight_row == 1, cap_all, jnp.where(weight_row == 2, float(half), 0.0)),
    ).astype(jnp.bfloat16)
    for i in range(n_sets):
        for k in range(groups):
            key_col[pl.ds((i * groups + k) * blk, blk), :] = lax.dot_general(
                blocks[i][k][blk : blk + LABEL_ROWS, 0:blk], weights, TN, preferred_element_type=jnp.float32
            )
    for o, (a, _) in enumerate(plan):
        rest = jnp.zeros((LABEL_ROWS, tile), jnp.float32)
        code = jnp.zeros((LABEL_ROWS, tile), jnp.float32)
        for k in range(groups):
            label = blocks[a][k][blk : blk + LABEL_ROWS, tile : 3 * tile].astype(jnp.float32)
            rest = jnp.where(from_block == k, label[:, :tile], rest)
            code = jnp.where(from_block == k, label[:, tile:], code)
        low = code * cap_all
        key = low + (which * half).astype(jnp.float32) + rest
        low = jnp.where(code > 0.5, low, FAR)
        key_row[o] = key[0:8]
        low_row[o] = low[0:8]

    def tile_of(i, t):
        at = pl.ds(pl.multiple_of(t * per_tile, per_tile), per_tile)
        return [blocks[i][k][at, :] for k in range(groups)]

    for o, (a, cols) in enumerate(plan):

        def one_tile(t, _, a=a, cols=cols, o=o):
            turned[...] = jnp.concatenate(tile_of(a, t), axis=0).T
            mine = key_row[o, pl.ds(t, 1), :]
            floor = low_row[o, pl.ds(t, 1), :]

            def one_col(s, acc):
                theirs = []
                pieces = []
                for b in cols:
                    pieces += tile_of(b, s)
                    for k in range(groups):
                        at = pl.multiple_of((b * groups + k) * blk + s * per_tile, per_tile)
                        theirs.append(key_col[pl.ds(at, per_tile), :])
                theirs = jnp.concatenate(theirs, axis=0)
                theirs = jnp.concatenate([theirs] * (tile // 128), axis=1)
                sims = jnp.dot(
                    jnp.concatenate(pieces, axis=0), turned[...], preferred_element_type=jnp.float32
                )
                keep = (theirs >= floor) & (theirs < mine)
                sims = jnp.where(keep, sims, -1.0)
                top = jnp.max(sims.reshape(len(cols) * tile // 8, 8, tile), axis=0)
                return jnp.maximum(acc, top)

            acc = lax.fori_loop(0, t + 1, one_col, jnp.full((8, tile), -1.0, jnp.float32))
            best[o, pl.ds(t, 1), :] = jnp.max(acc, axis=0, keepdims=True)
            return 0

        lax.fori_loop(0, TILES, one_tile, 0)

    lane = lax.broadcasted_iota(jnp.int32, (1, tile), 1)
    for o, (a, _) in enumerate(plan):
        found = best[o]
        for k in range(groups):
            total = jnp.full((1, tile), -1.0, jnp.float32)
            for t in range(TILES):
                turn = ((t - k) * per_tile) % tile
                moved = pltpu.roll(found, turn, 1) if turn else found
                total = jnp.where(lax.div(lane, per_tile) == t, moved[t : t + 1], total)
            block = place_ref[0] ^ k
            if joined:
                side = joined
                outs[0][pl.ds(block * side + (place_ref[1] ^ a), 1), 0, :] = total[:, :blk]
            else:
                outs[o][pl.ds(block, 1), 0, :] = total[:, :blk]


def compare(place, sets, plan, joined, sizes):
    groups, halves, half, cap, blk = sizes
    n_sets = len(sets)
    flat = [piece for one in sets for piece in one]
    rows, width = groups * blk, flat[0].shape[1]
    tile = rows // TILES
    vmem = pl.BlockSpec(memory_space=pltpu.VMEM)
    combos = sum(len(cols) for _, cols in plan) * TILES * (TILES + 1) // 2
    if joined:
        out_shape = [jax.ShapeDtypeStruct((groups * joined, 1, blk), jnp.float32)]
    else:
        out_shape = [jax.ShapeDtypeStruct((groups, 1, blk), jnp.float32)] * len(plan)
    return pl.pallas_call(
        functools.partial(compare_kernel, sizes, plan, n_sets, joined),
        out_shape=out_shape,
        in_specs=[pl.BlockSpec(memory_space=pltpu.SMEM)] + [vmem] * len(flat),
        out_specs=[vmem] * len(out_shape),
        scratch_shapes=[
            pltpu.VMEM((n_sets * rows, 128), jnp.float32),
            pltpu.VMEM((len(plan), 8, tile), jnp.float32),
            pltpu.VMEM((len(plan), 8, tile), jnp.float32),
            pltpu.VMEM((width, tile), jnp.bfloat16),
            pltpu.VMEM((len(plan), 8, tile), jnp.float32),
        ],
        compiler_params=pltpu.CompilerParams(vmem_limit_bytes=48 * 1024 * 1024),
        cost_estimate=pl.CostEstimate(
            flops=2 * combos * tile * tile * width, bytes_accessed=2 * n_sets * rows * width, transcendentals=0
        ),
    )(place, *flat)


def unpack_kernel(sizes, dest_ref, back_ref, out_ref):
    groups, halves, half, cap, blk = sizes
    side = back_ref.shape[0] // groups
    rows = dest_ref.shape[1]
    dest = dest_ref[...]
    slot = lax.broadcasted_iota(jnp.int32, (blk, rows), 0)
    field = lax.broadcasted_iota(jnp.int32, (LABEL_ROWS, blk), 0)
    total = jnp.zeros((LABEL_ROWS, rows), jnp.float32)
    for k in range(groups):
        value = back_ref[k * side]
        for more in range(1, side):
            value = jnp.maximum(value, back_ref[k * side + more])
        top = value.astype(jnp.bfloat16).astype(jnp.float32)
        rest = value - top
        mid = rest.astype(jnp.bfloat16).astype(jnp.float32)
        low = rest - mid
        stack = jnp.where(field == 0, top, jnp.where(field == 1, mid, jnp.where(field == 2, low, 0.0)))
        pick = (slot + k * blk == dest).astype(jnp.float32).astype(jnp.bfloat16)
        total = total + jnp.dot(stack.astype(jnp.bfloat16), pick, preferred_element_type=jnp.float32)
    value = (total[0:1] + total[1:2]) + total[2:3]
    out_ref[...] = jnp.where(dest >= 0, value, -1.0)


def unpack(dest, back, sizes):
    vmem = pl.BlockSpec(memory_space=pltpu.VMEM)
    return pl.pallas_call(
        functools.partial(unpack_kernel, sizes),
        out_shape=jax.ShapeDtypeStruct(dest.shape, jnp.float32),
        in_specs=[vmem] * 2,
        out_specs=vmem,
        compiler_params=pltpu.CompilerParams(vmem_limit_bytes=48 * 1024 * 1024),
    )(dest, back)


def on_device(embeddings, cluster, rank):
    rows_dev, width = embeddings.shape
    groups = lax.axis_size("grp")
    members = lax.axis_size("mem")
    devices = groups * members
    halves = 2 * members
    half = rows_dev // CLUS_GRP // 2
    blk = rows_dev // groups
    cap = blk // halves
    sizes = (groups, halves, half, cap, blk)
    side = members // groups

    def swap(value, block_step, member_step):
        mask = member_step // side * members + block_step * side + member_step % side
        if mask == 0:
            return value
        return lax.ppermute(value, ("grp", "mem"), [(i, i ^ mask) for i in range(devices)])

    offsets, pairs = cover(members)
    here = lax.axis_index("mem").astype(jnp.int32)
    place = jnp.stack([here // side, here % side])
    packed = pack(place, embeddings, cluster, rank, sizes)
    dest, sends = packed[0], packed[1:]

    own = [sends[0]]
    for k in range(1, groups):
        send = sends[k]
        if k > 2:
            send, own[k - 1] = lax.optimization_barrier((send, own[k - 1]))
        own.append(swap(send, k, 0))
    held = {0: own}
    for d in offsets[1:]:
        core_bit = d & ~side
        via = core_bit if d & side and core_bit in held else 0
        held[d] = [swap(piece, 0, d ^ via) for piece in held[via]]

    index = {d: i for i, d in enumerate(offsets)}
    starts = sorted({a for a, _ in pairs.values()})
    plan = [(index[a], [index[b] for _, (e, b) in sorted(pairs.items()) if e == a]) for a in starts]
    joined = side if all(a < side for a in starts) else 0
    found = compare(place, [held[d] for d in offsets], plan, joined, sizes)
    if joined:
        back = found[0]
    else:
        best = {}
        for a, value in zip(starts, found):
            near = a % side
            value = swap(value, 0, a - near)
            best[near] = jnp.maximum(best[near], value) if near in best else value
        none = jnp.full_like(found[0], -1.0)
        near_of = [best.get(near, none) for near in range(side)]
        rows_of = []
        for spot in range(side):
            value = near_of[spot]
            for mine in range(1, side):
                value = jnp.where(place[1] == mine, near_of[spot ^ mine], value)
            rows_of.append(value)
        back = jnp.stack(rows_of, axis=1).reshape(groups * side, 1, blk)
    back = lax.all_to_all(back, "mem", split_axis=0, concat_axis=0, tiled=True)
    return unpack(dest, back, sizes).reshape(rows_dev)


def solution(mesh):
    in_specs = (P(("grp", "mem"), None), P(("grp", "mem")), P(("grp", "mem")))
    out_specs = P(("grp", "mem"))
    return jax.shard_map(
        on_device, mesh=mesh, in_specs=in_specs, out_specs=out_specs, check_vma=False
    )
```

```python
import functools

import jax
import jax.numpy as jnp
from jax import lax
from jax.experimental import pallas as pl
from jax.experimental.pallas import tpu as pltpu
from jax.sharding import PartitionSpec as P

CLUS_GRP = 2
TILES = 4
LABEL_ROWS = 16
FAR = 1.0e9
VMEM_LIMIT = 32 * 1024 * 1024
NT = (((1,), (1,)), ((), ()))
TN = (((0,), (0,)), ((), ()))


def cover(members):
    bits = [1 << i for i in range(members.bit_length() - 1)]
    offsets = [0] + bits

    def missing(held):
        return set(range(members)) - {a ^ b for a in held for b in held}

    while missing(offsets):
        offsets.append(
            min(
                (d for d in range(members) if d not in offsets),
                key=lambda d: (len(missing(offsets + [d])), bin(d).count("1"), -d),
            )
        )
    pairs = {}
    for delta in range(members):
        pairs[delta] = min(
            (a, a ^ delta) for a in offsets if a ^ delta in offsets
        )
    return offsets, pairs


def pack_kernel(sizes, emb_hbm, cluster_hbm, rank_hbm, *refs):
    groups, halves, half, cap, blk = sizes
    dest_ref, sends = refs[0], refs[1 : 1 + TILES]
    emb_ref, cluster_ref, rank_ref, sems = refs[1 + TILES :]
    rows = emb_ref.shape[0]
    step = 256
    loads = [
        pltpu.make_async_copy(cluster_hbm, cluster_ref, sems.at[0]),
        pltpu.make_async_copy(rank_hbm, rank_ref, sems.at[1]),
    ]
    for j in range(rows // step):
        at = pl.ds(j * step, step)
        loads.append(pltpu.make_async_copy(emb_hbm.at[at], emb_ref.at[at], sems.at[2 + j]))
    for load in loads:
        load.start()
    for load in loads[:2]:
        load.wait()
    cluster = cluster_ref[...]
    rank = rank_ref[...]
    alive = cluster >= 0
    pair = lax.shift_right_logical(jnp.maximum(cluster, 0), 1)
    parity = jnp.maximum(cluster, 0) - 2 * pair
    safe_rank = jnp.maximum(rank, 0)
    which = safe_rank // half
    units = groups * halves
    unit_id = jnp.where(alive, pair * halves + which, -1)
    before_rows = lax.broadcasted_iota(jnp.int32, (step, step), 0)
    before_cols = lax.broadcasted_iota(jnp.int32, (step, step), 1)
    upper = (before_rows < before_cols).astype(jnp.float32).astype(jnp.bfloat16)
    unit_iota = lax.broadcasted_iota(jnp.int32, (units, step), 0)
    carry = jnp.zeros((units, 1), jnp.float32)
    places = []
    for j in range(rows // step):
        mine = unit_id[:, j * step : (j + 1) * step]
        hit = (unit_iota == mine).astype(jnp.float32)
        before = jnp.dot(hit.astype(jnp.bfloat16), upper, preferred_element_type=jnp.float32) + carry
        position = jnp.sum(hit * before, axis=0, keepdims=True)
        carry = carry + jnp.sum(hit, axis=1, keepdims=True)
        places.append(jnp.where(mine >= 0, mine * cap + position.astype(jnp.int32), -1))
    dest = jnp.concatenate(places, axis=1)
    dest_ref[...] = dest

    units_of = []
    for j in range(rows // step):
        loads[2 + j].wait()
        wide = emb_ref[j * step : (j + 1) * step, :].astype(jnp.float32)
        total = jnp.sum(wide * wide, axis=1, keepdims=True)
        units_of.append((wide * lax.rsqrt(total + 1e-06)).astype(jnp.bfloat16))
    unit = jnp.concatenate(units_of, axis=0)

    field = lax.broadcasted_iota(jnp.int32, (LABEL_ROWS, rows), 0)
    labels = jnp.where(
        field == 0, safe_rank - which * half, jnp.where(field == 1, parity + 1, 0)
    )
    labels = jnp.where(alive, labels, 0).astype(jnp.float32).astype(jnp.bfloat16)
    per_tile = blk // TILES
    wide_tile = groups * per_tile
    spread = (
        lax.broadcasted_iota(jnp.int32, (blk, wide_tile), 0) % per_tile
        == lax.broadcasted_iota(jnp.int32, (blk, wide_tile), 1) % per_tile
    )
    spread = spread.astype(jnp.float32).astype(jnp.bfloat16)
    label_row = lax.broadcasted_iota(jnp.int32, (LABEL_ROWS, blk), 0)
    label_col = lax.broadcasted_iota(jnp.int32, (LABEL_ROWS, blk), 1)
    own_tile = label_row == lax.div(label_col, per_tile)
    unit_col = lax.div(label_col, cap).astype(jnp.float32)
    slot = lax.broadcasted_iota(jnp.int32, (wide_tile, rows), 0)
    slot = lax.div(slot, per_tile) * blk + slot % per_tile
    width = sends[0].shape[1]
    picks = []
    for t in range(TILES):
        pick = (slot + t * per_tile == dest).astype(jnp.float32).astype(jnp.bfloat16)
        picks.append(pick)
        packed = jnp.dot(pick, unit, preferred_element_type=jnp.float32).astype(jnp.bfloat16)
        if t:
            sends[t][...] = packed
        else:
            for k in range(groups):
                at = k * (per_tile + LABEL_ROWS)
                sends[0][at : at + per_tile, :] = packed[k * per_tile : (k + 1) * per_tile]
    by_tile = [
        lax.dot_general(labels, pick, NT, preferred_element_type=jnp.float32) for pick in picks
    ]
    fold = [
        jnp.where(
            lax.broadcasted_iota(jnp.int32, (wide_tile, blk), 0)
            == lax.broadcasted_iota(jnp.int32, (wide_tile, blk), 1) % per_tile
            + lax.div(lax.broadcasted_iota(jnp.int32, (wide_tile, blk), 1), per_tile) * 0
            + k * per_tile,
            1.0,
            0.0,
        ).astype(jnp.bfloat16)
        for k in range(groups)
    ]
    for k in range(groups):
        mine = jnp.zeros((LABEL_ROWS, blk), jnp.float32)
        for t in range(TILES):
            spread_t = jnp.dot(
                by_tile[t].astype(jnp.bfloat16), fold[k], preferred_element_type=jnp.float32
            )
            mine = jnp.where(lax.div(label_col, per_tile) == t, spread_t, mine)
        plain = jnp.where(label_row == 2, unit_col, mine)
        parts = [plain] + [jnp.zeros_like(plain)] * ((wide_tile - blk) // blk)
        for f in range(2):
            line = jnp.where(own_tile, mine[f : f + 1, :], 0.0).astype(jnp.bfloat16)
            parts.append(jnp.dot(line, spread, preferred_element_type=jnp.float32))
        if width > 3 * wide_tile:
            parts.append(jnp.zeros((LABEL_ROWS, width - 3 * wide_tile), jnp.float32))
        at = k * (per_tile + LABEL_ROWS) + per_tile
        sends[0][at : at + LABEL_ROWS, :] = jnp.concatenate(parts, axis=1).astype(jnp.bfloat16)


def pack(embeddings, cluster, rank, sizes):
    groups, halves, half, cap, blk = sizes
    rows, width = embeddings.shape
    vmem = pl.BlockSpec(memory_space=pltpu.VMEM)
    hbm = pl.BlockSpec(memory_space=pltpu.HBM)
    out_shape = [jax.ShapeDtypeStruct((1, rows), jnp.int32)]
    tile = rows // TILES
    for t in range(TILES):
        extra = 0 if t else groups * LABEL_ROWS
        out_shape.append(jax.ShapeDtypeStruct((tile + extra, width), jnp.bfloat16))
    return pl.pallas_call(
        functools.partial(pack_kernel, sizes),
        out_shape=out_shape,
        in_specs=[hbm, hbm, hbm],
        out_specs=[vmem] * len(out_shape),
        scratch_shapes=[
            pltpu.VMEM((rows, width), jnp.bfloat16),
            pltpu.VMEM((1, rows), jnp.int32),
            pltpu.VMEM((1, rows), jnp.int32),
            pltpu.SemaphoreType.DMA((2 + rows // 256,)),
        ],
        compiler_params=pltpu.CompilerParams(vmem_limit_bytes=VMEM_LIMIT),
    )(embeddings, cluster.reshape(1, rows), rank.reshape(1, rows))


def compare_kernel(sizes, plan, n_sets, t, *refs):
    groups, halves, half, cap, blk = sizes
    blocks = [refs[i * (t + 1) : (i + 1) * (t + 1)] for i in range(n_sets)]
    best_ref = refs[n_sets * (t + 1)]
    key_col, turned = refs[n_sets * (t + 1) + 1 :]
    per_tile = blk // TILES
    tile = groups * per_tile
    pitch = per_tile + LABEL_ROWS
    cap_all = float(halves * half)

    lane = lax.broadcasted_iota(jnp.int32, (LABEL_ROWS, tile), 1)
    line = lax.broadcasted_iota(jnp.int32, (LABEL_ROWS, tile), 0)
    from_block = lax.div(lane, per_tile)
    which = line * (halves // TILES) + lax.div(lane - from_block * per_tile, cap)
    weight_row = lax.broadcasted_iota(jnp.int32, (LABEL_ROWS, 128), 0)
    weights = jnp.where(
        weight_row == 0,
        1.0,
        jnp.where(weight_row == 1, cap_all, jnp.where(weight_row == 2, float(half), 0.0)),
    ).astype(jnp.bfloat16)

    def label(i, k):
        return blocks[i][0][k * pitch + per_tile : (k + 1) * pitch, :]

    for i in range(n_sets):
        for k in range(groups):
            keys = lax.dot_general(
                label(i, k)[:, 0:blk], weights, TN, preferred_element_type=jnp.float32
            )
            for s in range(t + 1):
                at = (i * (t + 1) + s) * tile + k * per_tile
                key_col[at : at + per_tile, :] = keys[s * per_tile : (s + 1) * per_tile]

    def tile_of(i, s):
        if s:
            return [blocks[i][s][...]]
        return [blocks[i][0][k * pitch : k * pitch + per_tile, :] for k in range(groups)]

    for o, (a, cols) in enumerate(plan):
        rest = jnp.zeros((LABEL_ROWS, tile), jnp.float32)
        code = jnp.zeros((LABEL_ROWS, tile), jnp.float32)
        for k in range(groups):
            spread = label(a, k)[:, tile : 3 * tile].astype(jnp.float32)
            rest = jnp.where(from_block == k, spread[:, :tile], rest)
            code = jnp.where(from_block == k, spread[:, tile:], code)
        low = code * cap_all
        mine = (low + (which * half).astype(jnp.float32) + rest)[t : t + 1]
        floor = jnp.where(code > 0.5, low, FAR)[t : t + 1]
        turned[o] = jnp.concatenate(tile_of(a, t), axis=0).T
        acc = jnp.full((8, tile), -1.0, jnp.float32)
        for s in range(t + 1):
            for b in cols:
                at = (b * (t + 1) + s) * tile
                theirs = key_col[at : at + tile, :]
                theirs = jnp.concatenate([theirs] * (tile // 128), axis=1)
                sims = jnp.dot(
                    jnp.concatenate(tile_of(b, s), axis=0), turned[o], preferred_element_type=jnp.float32
                )
                keep = (theirs >= floor) & (theirs < mine)
                sims = jnp.where(keep, sims, -1.0)
                acc = jnp.maximum(acc, jnp.max(sims.reshape(tile // 8, 8, tile), axis=0))
        best_ref[o] = jnp.broadcast_to(jnp.max(acc, axis=0, keepdims=True), (8, tile))


def compare(sets, plan, t, sizes):
    groups, halves, half, cap, blk = sizes
    n_sets = len(sets)
    flat = [piece for one in sets for piece in one[: t + 1]]
    rows, width = groups * blk, flat[0].shape[1]
    tile = rows // TILES
    vmem = pl.BlockSpec(memory_space=pltpu.VMEM)
    combos = sum(len(cols) for _, cols in plan) * (t + 1)
    return pl.pallas_call(
        functools.partial(compare_kernel, sizes, plan, n_sets, t),
        out_shape=jax.ShapeDtypeStruct((len(plan), 8, tile), jnp.float32),
        in_specs=[vmem] * len(flat),
        out_specs=vmem,
        scratch_shapes=[
            pltpu.VMEM((n_sets * (t + 1) * tile, 128), jnp.float32),
            pltpu.VMEM((len(plan), width, tile), jnp.bfloat16),
        ],
        compiler_params=pltpu.CompilerParams(vmem_limit_bytes=VMEM_LIMIT),
        cost_estimate=pl.CostEstimate(
            flops=2 * combos * tile * tile * width,
            bytes_accessed=2 * n_sets * (t + 1) * tile * width,
            transcendentals=0,
        ),
    )(*flat)


def order_kernel(sizes, starts, joined, place_ref, *refs):
    groups, halves, half, cap, blk = sizes
    found, outs = refs[:TILES], refs[TILES:]
    per_tile = blk // TILES
    tile = groups * per_tile
    lane = lax.broadcasted_iota(jnp.int32, (1, tile), 1)
    for o, a in enumerate(starts):
        for k in range(groups):
            total = jnp.full((1, tile), -1.0, jnp.float32)
            for t in range(TILES):
                turn = ((t - k) * per_tile) % tile
                value = found[t][o]
                moved = pltpu.roll(value, turn, 1) if turn else value
                total = jnp.where(lax.div(lane, per_tile) == t, moved[0:1], total)
            if joined:
                outs[0][pl.ds(k * joined + (place_ref[1] ^ a), 1), 0, :] = total[:, :blk]
            else:
                outs[o][k, :, :] = total[:, :blk]


def order(place, found, starts, joined, sizes):
    groups, halves, half, cap, blk = sizes
    vmem = pl.BlockSpec(memory_space=pltpu.VMEM)
    if joined:
        out_shape = [jax.ShapeDtypeStruct((groups * joined, 1, blk), jnp.float32)]
    else:
        out_shape = [jax.ShapeDtypeStruct((groups, 1, blk), jnp.float32)] * len(starts)
    return pl.pallas_call(
        functools.partial(order_kernel, sizes, starts, joined),
        out_shape=out_shape,
        in_specs=[pl.BlockSpec(memory_space=pltpu.SMEM)] + [vmem] * TILES,
        out_specs=[vmem] * len(out_shape),
    )(place, *found)


def unpack_kernel(sizes, dest_ref, back_ref, out_ref):
    groups, halves, half, cap, blk = sizes
    side = back_ref.shape[0] // groups
    rows = dest_ref.shape[1]
    dest = dest_ref[...]
    slot = lax.broadcasted_iota(jnp.int32, (blk, rows), 0)
    field = lax.broadcasted_iota(jnp.int32, (LABEL_ROWS, blk), 0)
    total = jnp.zeros((LABEL_ROWS, rows), jnp.float32)
    for k in range(groups):
        value = back_ref[k * side]
        for more in range(1, side):
            value = jnp.maximum(value, back_ref[k * side + more])
        top = value.astype(jnp.bfloat16).astype(jnp.float32)
        rest = value - top
        mid = rest.astype(jnp.bfloat16).astype(jnp.float32)
        low = rest - mid
        stack = jnp.where(field == 0, top, jnp.where(field == 1, mid, jnp.where(field == 2, low, 0.0)))
        pick = (slot + k * blk == dest).astype(jnp.float32).astype(jnp.bfloat16)
        total = total + jnp.dot(stack.astype(jnp.bfloat16), pick, preferred_element_type=jnp.float32)
    value = (total[0:1] + total[1:2]) + total[2:3]
    out_ref[...] = jnp.where(dest >= 0, value, -1.0)


def unpack(dest, back, sizes):
    vmem = pl.BlockSpec(memory_space=pltpu.VMEM)
    return pl.pallas_call(
        functools.partial(unpack_kernel, sizes),
        out_shape=jax.ShapeDtypeStruct(dest.shape, jnp.float32),
        in_specs=[vmem] * 2,
        out_specs=vmem,
        compiler_params=pltpu.CompilerParams(vmem_limit_bytes=VMEM_LIMIT),
    )(dest, back)


def on_device(embeddings, cluster, rank):
    rows_dev, width = embeddings.shape
    groups = lax.axis_size("grp")
    members = lax.axis_size("mem")
    devices = groups * members
    halves = 2 * members
    half = rows_dev // CLUS_GRP // 2
    blk = rows_dev // groups
    cap = blk // halves
    sizes = (groups, halves, half, cap, blk)
    side = members // groups

    def swap(value, block_step, member_step):
        mask = member_step // side * members + block_step * side + member_step % side
        if mask == 0:
            return value
        return lax.ppermute(value, ("grp", "mem"), [(i, i ^ mask) for i in range(devices)])

    offsets, pairs = cover(members)
    here = lax.axis_index("mem").astype(jnp.int32)
    place = jnp.stack([here // side, here % side])
    packed = pack(embeddings, cluster, rank, sizes)
    dest, sends = packed[0], packed[1:]

    columns = [[b * side + spot for b in range(groups)] for spot in range(side)]
    held = {d: [] for d in offsets}
    for t in range(TILES):
        send = sends[t]
        if t:
            send, held[0][t - 1] = lax.optimization_barrier((send, held[0][t - 1]))
        held[0].append(
            lax.all_to_all(
                send, "mem", split_axis=0, concat_axis=0, tiled=True, axis_index_groups=columns
            )
        )
    for t in range(TILES):
        for d in offsets[1:]:
            core_bit = side
            via = d ^ core_bit if d & core_bit and d ^ core_bit in held else 0
            held[d].append(swap(held[via][t], 0, d ^ via))

    index = {d: i for i, d in enumerate(offsets)}
    starts = sorted({a for a, _ in pairs.values()})
    plan = [(index[a], [index[b] for _, (e, b) in sorted(pairs.items()) if e == a]) for a in starts]
    joined = side if all(a < side for a in starts) else 0
    found = [compare([held[d] for d in offsets], plan, t, sizes) for t in range(TILES)]
    found = order(place, found, starts, joined, sizes)
    if joined:
        back = found[0]
    else:
        best = {}
        for a, value in zip(starts, found):
            near = a % side
            value = swap(value, 0, a - near)
            best[near] = jnp.maximum(best[near], value) if near in best else value
        none = jnp.full_like(found[0], -1.0)
        near_of = [best.get(near, none) for near in range(side)]
        rows_of = []
        for spot in range(side):
            value = near_of[spot]
            for mine in range(1, side):
                value = jnp.where(place[1] == mine, near_of[spot ^ mine], value)
            rows_of.append(value)
        back = jnp.stack(rows_of, axis=1).reshape(groups * side, 1, blk)
    back = lax.all_to_all(back, "mem", split_axis=0, concat_axis=0, tiled=True)
    return unpack(dest, back, sizes).reshape(rows_dev)


def solution(mesh):
    in_specs = (P(("grp", "mem"), None), P(("grp", "mem")), P(("grp", "mem")))
    out_specs = P(("grp", "mem"))
    return jax.shard_map(
        on_device, mesh=mesh, in_specs=in_specs, out_specs=out_specs, check_vma=False
    )
```

```python
import functools

import jax
import jax.numpy as jnp
from jax import lax
from jax.experimental import pallas as pl
from jax.experimental.pallas import tpu as pltpu
from jax.sharding import PartitionSpec as P

CLUS_GRP = 2
TILES = 4
LABEL_ROWS = 16
FAR = 1.0e9
PACK_VMEM = 60 * 1024 * 1024
COMPARE_VMEM = 24 * 1024 * 1024
NT = (((1,), (1,)), ((), ()))
TN = (((0,), (0,)), ((), ()))


def cover(members):
    bits = [1 << i for i in range(members.bit_length() - 1)]
    offsets = [0] + bits

    def missing(held):
        return set(range(members)) - {a ^ b for a in held for b in held}

    while missing(offsets):
        offsets.append(
            min(
                (d for d in range(members) if d not in offsets),
                key=lambda d: (len(missing(offsets + [d])), bin(d).count("1"), -d),
            )
        )
    pairs = {}
    for delta in range(members):
        pairs[delta] = min(
            (a, a ^ delta) for a in offsets if a ^ delta in offsets
        )
    return offsets, pairs


def pack_kernel(sizes, place_ref, emb_hbm, cluster_hbm, rank_hbm, *refs):
    groups, halves, half, cap, blk = sizes
    dest_ref, sends = refs[0], refs[1 : 1 + groups]
    emb_ref, cluster_ref, rank_ref, sems = refs[1 + groups :]
    rows = emb_ref.shape[0]
    step = 256
    loads = [
        pltpu.make_async_copy(cluster_hbm, cluster_ref, sems.at[0]),
        pltpu.make_async_copy(rank_hbm, rank_ref, sems.at[1]),
    ]
    for j in range(rows // step):
        at = pl.ds(j * step, step)
        loads.append(pltpu.make_async_copy(emb_hbm.at[at], emb_ref.at[at], sems.at[2 + j]))
    for load in loads:
        load.start()
    for load in loads[:2]:
        load.wait()
    cluster = cluster_ref[...]
    rank = rank_ref[...]
    alive = cluster >= 0
    pair = lax.shift_right_logical(jnp.maximum(cluster, 0), 1)
    parity = jnp.maximum(cluster, 0) - 2 * pair
    safe_rank = jnp.maximum(rank, 0)
    which = safe_rank // half
    units = groups * halves
    unit_id = jnp.where(alive, pair * halves + which, -1)
    before_rows = lax.broadcasted_iota(jnp.int32, (step, step), 0)
    before_cols = lax.broadcasted_iota(jnp.int32, (step, step), 1)
    upper = (before_rows < before_cols).astype(jnp.float32).astype(jnp.bfloat16)
    unit_iota = lax.broadcasted_iota(jnp.int32, (units, step), 0)
    carry = jnp.zeros((units, 1), jnp.float32)
    places = []
    for j in range(rows // step):
        mine = unit_id[:, j * step : (j + 1) * step]
        hit = (unit_iota == mine).astype(jnp.float32)
        before = jnp.dot(hit.astype(jnp.bfloat16), upper, preferred_element_type=jnp.float32) + carry
        position = jnp.sum(hit * before, axis=0, keepdims=True)
        carry = carry + jnp.sum(hit, axis=1, keepdims=True)
        places.append(jnp.where(mine >= 0, mine * cap + position.astype(jnp.int32), -1))
    dest = jnp.concatenate(places, axis=1)
    dest_ref[...] = dest
    dest = jnp.where(dest >= 0, dest ^ (place_ref[0] * blk), -1)

    units_of = []
    for j in range(rows // step):
        loads[2 + j].wait()
        wide = emb_ref[j * step : (j + 1) * step, :].astype(jnp.float32)
        total = jnp.sum(wide * wide, axis=1, keepdims=True)
        units_of.append((wide * lax.rsqrt(total + 1e-06)).astype(jnp.bfloat16))
    unit = jnp.concatenate(units_of, axis=0)

    field = lax.broadcasted_iota(jnp.int32, (LABEL_ROWS, rows), 0)
    labels = jnp.where(
        field == 0, safe_rank - which * half, jnp.where(field == 1, parity + 1, 0)
    )
    labels = jnp.where(alive, labels, 0).astype(jnp.float32).astype(jnp.bfloat16)
    per_tile = blk // TILES
    wide_tile = groups * per_tile
    spread = (
        lax.broadcasted_iota(jnp.int32, (blk, wide_tile), 0) % per_tile
        == lax.broadcasted_iota(jnp.int32, (blk, wide_tile), 1) % per_tile
    )
    spread = spread.astype(jnp.float32).astype(jnp.bfloat16)
    label_row = lax.broadcasted_iota(jnp.int32, (LABEL_ROWS, blk), 0)
    label_col = lax.broadcasted_iota(jnp.int32, (LABEL_ROWS, blk), 1)
    own_tile = label_row == lax.div(label_col, per_tile)
    unit_col = lax.div(label_col, cap).astype(jnp.float32)
    slot = lax.broadcasted_iota(jnp.int32, (blk, rows), 0)
    width = sends[0].shape[1]
    for k in range(groups):
        pick = (slot + k * blk == dest).astype(jnp.float32).astype(jnp.bfloat16)
        sends[k][0:blk, :] = jnp.dot(pick, unit, preferred_element_type=jnp.float32).astype(
            jnp.bfloat16
        )
        mine = lax.dot_general(labels, pick, NT, preferred_element_type=jnp.float32)
        plain = jnp.where(label_row == 2, unit_col, mine)
        parts = [plain] + [jnp.zeros_like(plain)] * ((wide_tile - blk) // blk)
        for f in range(2):
            line = jnp.where(own_tile, mine[f : f + 1, :], 0.0).astype(jnp.bfloat16)
            parts.append(jnp.dot(line, spread, preferred_element_type=jnp.float32))
        if width > 3 * wide_tile:
            parts.append(jnp.zeros((LABEL_ROWS, width - 3 * wide_tile), jnp.float32))
        sends[k][blk : blk + LABEL_ROWS, :] = jnp.concatenate(parts, axis=1).astype(jnp.bfloat16)


def pack(place, embeddings, cluster, rank, sizes):
    groups, halves, half, cap, blk = sizes
    rows, width = embeddings.shape
    vmem = pl.BlockSpec(memory_space=pltpu.VMEM)
    hbm = pl.BlockSpec(memory_space=pltpu.HBM)
    out_shape = [jax.ShapeDtypeStruct((1, rows), jnp.int32)]
    out_shape += [jax.ShapeDtypeStruct((blk + LABEL_ROWS, width), jnp.bfloat16)] * groups
    return pl.pallas_call(
        functools.partial(pack_kernel, sizes),
        out_shape=out_shape,
        in_specs=[pl.BlockSpec(memory_space=pltpu.SMEM), hbm, hbm, hbm],
        out_specs=[vmem] * len(out_shape),
        scratch_shapes=[
            pltpu.VMEM((rows, width), jnp.bfloat16),
            pltpu.VMEM((1, rows), jnp.int32),
            pltpu.VMEM((1, rows), jnp.int32),
            pltpu.SemaphoreType.DMA((2 + rows // 256,)),
        ],
        compiler_params=pltpu.CompilerParams(vmem_limit_bytes=PACK_VMEM),
    )(place, embeddings, cluster.reshape(1, rows), rank.reshape(1, rows))


def compare_kernel(sizes, jobs, names, joined, has_prev, place_ref, *refs):
    groups, halves, half, cap, blk = sizes
    block = dict(zip(names, refs))
    refs = refs[len(names) :]
    prev = None
    if has_prev:
        prev, refs = refs[0], refs[1:]
    outs, (key_col, key_row, low_row, turned, best) = refs[:-5], refs[-5:]
    rows = groups * blk
    per_tile = blk // TILES
    tile = rows // TILES
    cap_all = float(halves * half)

    lane = lax.broadcasted_iota(jnp.int32, (LABEL_ROWS, tile), 1)
    line = lax.broadcasted_iota(jnp.int32, (LABEL_ROWS, tile), 0)
    from_block = lax.div(lane, per_tile)
    which = line * (halves // TILES) + lax.div(lane - from_block * per_tile, cap)
    weight_row = lax.broadcasted_iota(jnp.int32, (LABEL_ROWS, 128), 0)
    weights = jnp.where(
        weight_row == 0,
        1.0,
        jnp.where(weight_row == 1, cap_all, jnp.where(weight_row == 2, float(half), 0.0)),
    ).astype(jnp.bfloat16)
    needed = sorted({piece for _, pieces in jobs for piece in pieces})
    key_at = {piece: n * blk for n, piece in enumerate(needed)}
    for piece in needed:
        key_col[pl.ds(key_at[piece], blk), :] = lax.dot_general(
            block[piece][blk : blk + LABEL_ROWS, 0:blk], weights, TN, preferred_element_type=jnp.float32
        )
    for o, (a, _) in enumerate(jobs):
        rest = jnp.zeros((LABEL_ROWS, tile), jnp.float32)
        code = jnp.zeros((LABEL_ROWS, tile), jnp.float32)
        for k in range(groups):
            label = block[a, k][blk : blk + LABEL_ROWS, tile : 3 * tile].astype(jnp.float32)
            rest = jnp.where(from_block == k, label[:, :tile], rest)
            code = jnp.where(from_block == k, label[:, tile:], code)
        low = code * cap_all
        key = low + (which * half).astype(jnp.float32) + rest
        low = jnp.where(code > 0.5, low, FAR)
        key_row[o] = key[0:8]
        low_row[o] = low[0:8]

    def part_of(ref, base, t):
        return ref[pl.ds(pl.multiple_of(base + t * per_tile, per_tile), per_tile), :]

    best[...] = prev[...] if has_prev else jnp.full(best.shape, -1.0, jnp.float32)
    for o, (a, pieces) in enumerate(jobs):

        def one_tile(t, _, a=a, pieces=pieces, o=o):
            turned[...] = jnp.concatenate(
                [part_of(block[a, k], 0, t) for k in range(groups)], axis=0
            ).T
            mine = key_row[o, pl.ds(t, 1), :]
            floor = low_row[o, pl.ds(t, 1), :]

            def one_col(s, acc):
                theirs = [part_of(key_col, key_at[piece], s) for piece in pieces]
                theirs = jnp.concatenate(theirs, axis=0)
                theirs = jnp.concatenate([theirs] * (tile // 128), axis=1)
                sims = jnp.dot(
                    jnp.concatenate([part_of(block[piece], 0, s) for piece in pieces], axis=0),
                    turned[...],
                    preferred_element_type=jnp.float32,
                )
                keep = (theirs >= floor) & (theirs < mine)
                sims = jnp.where(keep, sims, -1.0)
                top = jnp.max(sims.reshape(len(pieces) * per_tile // 8, 8, tile), axis=0)
                return jnp.maximum(acc, top)

            acc = lax.fori_loop(0, t + 1, one_col, jnp.full((8, tile), -1.0, jnp.float32))
            best[a, pl.ds(t, 1), :] = jnp.maximum(
                best[a, pl.ds(t, 1), :], jnp.max(acc, axis=0, keepdims=True)
            )
            return 0

        lax.fori_loop(0, TILES, one_tile, 0)

    if not has_prev:
        outs[0][...] = best[...]
        return
    lane = lax.broadcasted_iota(jnp.int32, (1, tile), 1)
    for o, (a, _) in enumerate(jobs):
        found = best[a]
        for k in range(groups):
            total = jnp.full((1, tile), -1.0, jnp.float32)
            for t in range(TILES):
                turn = ((t - k) * per_tile) % tile
                moved = pltpu.roll(found, turn, 1) if turn else found
                total = jnp.where(lax.div(lane, per_tile) == t, moved[t : t + 1], total)
            at = place_ref[0] ^ k
            if joined:
                outs[0][pl.ds(at * joined + (place_ref[1] ^ a), 1), 0, :] = total[:, :blk]
            else:
                outs[o][pl.ds(at, 1), 0, :] = total[:, :blk]


def compare(place, blocks, jobs, prev, joined, n_sets, sizes):
    groups, halves, half, cap, blk = sizes
    names = {piece for _, pieces in jobs for piece in pieces}
    names |= {(a, k) for a, _ in jobs for k in range(groups)}
    names = sorted(names)
    width = blocks[0, 0].shape[1]
    tile = groups * blk // TILES
    vmem = pl.BlockSpec(memory_space=pltpu.VMEM)
    steps = TILES * (TILES + 1) // 2
    work = sum(len(pieces) for _, pieces in jobs) * steps * (blk // TILES) * tile * width
    if prev is None:
        out_shape = [jax.ShapeDtypeStruct((n_sets, 8, tile), jnp.float32)]
    elif joined:
        out_shape = [jax.ShapeDtypeStruct((groups * joined, 1, blk), jnp.float32)]
    else:
        out_shape = [jax.ShapeDtypeStruct((groups, 1, blk), jnp.float32)] * len(jobs)
    operands = [place] + [blocks[piece] for piece in names] + ([] if prev is None else [prev])
    needed = {piece for _, pieces in jobs for piece in pieces}
    return pl.pallas_call(
        functools.partial(compare_kernel, sizes, jobs, names, joined, prev is not None),
        out_shape=out_shape,
        in_specs=[pl.BlockSpec(memory_space=pltpu.SMEM)] + [vmem] * (len(operands) - 1),
        out_specs=[vmem] * len(out_shape),
        scratch_shapes=[
            pltpu.VMEM((len(needed) * blk, 128), jnp.float32),
            pltpu.VMEM((len(jobs), 8, tile), jnp.float32),
            pltpu.VMEM((len(jobs), 8, tile), jnp.float32),
            pltpu.VMEM((width, tile), jnp.bfloat16),
            pltpu.VMEM((n_sets, 8, tile), jnp.float32),
        ],
        compiler_params=pltpu.CompilerParams(vmem_limit_bytes=COMPARE_VMEM),
        cost_estimate=pl.CostEstimate(
            flops=2 * work, bytes_accessed=2 * len(names) * blk * width, transcendentals=0
        ),
    )(*operands)


def unpack_kernel(sizes, dest_ref, back_ref, out_ref):
    groups, halves, half, cap, blk = sizes
    side = back_ref.shape[0] // groups
    rows = dest_ref.shape[1]
    dest = dest_ref[...]
    slot = lax.broadcasted_iota(jnp.int32, (blk, rows), 0)
    field = lax.broadcasted_iota(jnp.int32, (LABEL_ROWS, blk), 0)
    total = jnp.zeros((LABEL_ROWS, rows), jnp.float32)
    for k in range(groups):
        value = back_ref[k * side]
        for more in range(1, side):
            value = jnp.maximum(value, back_ref[k * side + more])
        top = value.astype(jnp.bfloat16).astype(jnp.float32)
        rest = value - top
        mid = rest.astype(jnp.bfloat16).astype(jnp.float32)
        low = rest - mid
        stack = jnp.where(field == 0, top, jnp.where(field == 1, mid, jnp.where(field == 2, low, 0.0)))
        pick = (slot + k * blk == dest).astype(jnp.float32).astype(jnp.bfloat16)
        total = total + jnp.dot(stack.astype(jnp.bfloat16), pick, preferred_element_type=jnp.float32)
    value = (total[0:1] + total[1:2]) + total[2:3]
    out_ref[...] = jnp.where(dest >= 0, value, -1.0)


def unpack(dest, back, sizes):
    vmem = pl.BlockSpec(memory_space=pltpu.VMEM)
    return pl.pallas_call(
        functools.partial(unpack_kernel, sizes),
        out_shape=jax.ShapeDtypeStruct(dest.shape, jnp.float32),
        in_specs=[vmem] * 2,
        out_specs=vmem,
        compiler_params=pltpu.CompilerParams(vmem_limit_bytes=COMPARE_VMEM),
    )(dest, back)


def on_device(embeddings, cluster, rank):
    rows_dev, width = embeddings.shape
    groups = lax.axis_size("grp")
    members = lax.axis_size("mem")
    devices = groups * members
    halves = 2 * members
    half = rows_dev // CLUS_GRP // 2
    blk = rows_dev // groups
    cap = blk // halves
    sizes = (groups, halves, half, cap, blk)
    side = members // groups

    def swap(value, block_step, member_step):
        mask = member_step // side * members + block_step * side + member_step % side
        if mask == 0:
            return value
        return lax.ppermute(value, ("grp", "mem"), [(i, i ^ mask) for i in range(devices)])

    offsets, pairs = cover(members)
    here = lax.axis_index("mem").astype(jnp.int32)
    place = jnp.stack([here // side, here % side])
    packed = pack(place, embeddings, cluster, rank, sizes)
    dest, sends = packed[0], packed[1:]

    own = [sends[0]]
    first_hop = swap(own[0], 0, members // 2)
    for k in range(1, groups):
        send = sends[k]
        if k == 3:
            send, first_hop = lax.optimization_barrier((send, first_hop))
        elif k > 3:
            send, own[k - 2] = lax.optimization_barrier((send, own[k - 2]))
        own.append(swap(send, k, 0))
    last = groups - 1
    hop = {}
    for d in offsets[1:]:
        via = d ^ side if d & side and d ^ side in offsets else 0
        hop[d] = via
    near = [d for d in offsets[1:] if hop[d] == 0]
    far = [d for d in offsets[1:] if hop[d] != 0]
    held = {0: own}
    for d in near:
        held[d] = [
            first_hop if d == members // 2 and k == 0 else swap(own[k], 0, d) for k in range(groups)
        ]
    for d in far:
        held[d] = [swap(piece, 0, d ^ hop[d]) for piece in held[hop[d]][:last]]

    index = {d: i for i, d in enumerate(offsets)}
    starts = sorted({a for a, _ in pairs.values()})
    early, late = [], []
    for a in starts:
        cols = [index[b] for _, (e, b) in sorted(pairs.items()) if e == a]
        pieces = [(b, k) for b in cols for k in range(groups)]
        if a == 0:
            soon = [(b, k) for b, k in pieces if b == 0 or k < last]
            early.append((0, soon))
            pieces = [piece for piece in pieces if piece not in soon]
        late.append((index[a], pieces))
    joined = side if all(a < side for a in starts) else 0
    blocks = {(index[d], k): piece for d in offsets for k, piece in enumerate(held[d])}
    prev = compare(place, blocks, early, None, 0, len(offsets), sizes)[0]
    for d in far:
        piece, prev = lax.optimization_barrier((held[hop[d]][last], prev))
        blocks[index[d], last] = swap(piece, 0, d ^ hop[d])
    found = compare(place, blocks, late, prev, joined, len(offsets), sizes)
    if joined:
        back = found[0]
    else:
        best = {}
        for a, value in zip(starts, found):
            near = a % side
            value = swap(value, 0, a - near)
            best[near] = jnp.maximum(best[near], value) if near in best else value
        none = jnp.full_like(found[0], -1.0)
        near_of = [best.get(near, none) for near in range(side)]
        rows_of = []
        for spot in range(side):
            value = near_of[spot]
            for mine in range(1, side):
                value = jnp.where(place[1] == mine, near_of[spot ^ mine], value)
            rows_of.append(value)
        back = jnp.stack(rows_of, axis=1).reshape(groups * side, 1, blk)
    back = lax.all_to_all(back, "mem", split_axis=0, concat_axis=0, tiled=True)
    return unpack(dest, back, sizes).reshape(rows_dev)


def solution(mesh):
    in_specs = (P(("grp", "mem"), None), P(("grp", "mem")), P(("grp", "mem")))
    out_specs = P(("grp", "mem"))
    return jax.shard_map(
        on_device, mesh=mesh, in_specs=in_specs, out_specs=out_specs, check_vma=False
    )
```

```python
import functools

import jax
import jax.numpy as jnp
from jax import lax
from jax.experimental import pallas as pl
from jax.experimental.pallas import tpu as pltpu
from jax.sharding import PartitionSpec as P

CLUS_GRP = 2
TILES = 4
LABEL_ROWS = 16
FAR = 1.0e9
PACK_VMEM = 60 * 1024 * 1024
COMPARE_VMEM = 24 * 1024 * 1024
NT = (((1,), (1,)), ((), ()))
TN = (((0,), (0,)), ((), ()))


def cover(members):
    bits = [1 << i for i in range(members.bit_length() - 1)]
    offsets = [0] + bits

    def missing(held):
        return set(range(members)) - {a ^ b for a in held for b in held}

    while missing(offsets):
        offsets.append(
            min(
                (d for d in range(members) if d not in offsets),
                key=lambda d: (len(missing(offsets + [d])), bin(d).count("1"), -d),
            )
        )
    pairs = {}
    for delta in range(members):
        pairs[delta] = min(
            (a, a ^ delta) for a in offsets if a ^ delta in offsets
        )
    return offsets, pairs


def pack_kernel(sizes, emb_hbm, cluster_hbm, rank_hbm, *refs):
    groups, halves, half, cap, blk = sizes
    dest_ref, sends = refs[0], refs[1 : 1 + groups]
    emb_ref, cluster_ref, rank_ref, sems = refs[1 + groups :]
    rows = emb_ref.shape[0]
    step = 256
    loads = [
        pltpu.make_async_copy(cluster_hbm, cluster_ref, sems.at[0]),
        pltpu.make_async_copy(rank_hbm, rank_ref, sems.at[1]),
    ]
    for j in range(rows // step):
        at = pl.ds(j * step, step)
        loads.append(pltpu.make_async_copy(emb_hbm.at[at], emb_ref.at[at], sems.at[2 + j]))
    for load in loads:
        load.start()
    for load in loads[:2]:
        load.wait()
    cluster = cluster_ref[...]
    rank = rank_ref[...]
    alive = cluster >= 0
    pair = lax.shift_right_logical(jnp.maximum(cluster, 0), 1)
    parity = jnp.maximum(cluster, 0) - 2 * pair
    safe_rank = jnp.maximum(rank, 0)
    which = safe_rank // half
    units = groups * halves
    unit_id = jnp.where(alive, pair * halves + which, -1)
    before_rows = lax.broadcasted_iota(jnp.int32, (step, step), 0)
    before_cols = lax.broadcasted_iota(jnp.int32, (step, step), 1)
    upper = (before_rows < before_cols).astype(jnp.float32).astype(jnp.bfloat16)
    unit_iota = lax.broadcasted_iota(jnp.int32, (units, step), 0)
    carry = jnp.zeros((units, 1), jnp.float32)
    places = []
    for j in range(rows // step):
        mine = unit_id[:, j * step : (j + 1) * step]
        hit = (unit_iota == mine).astype(jnp.float32)
        before = jnp.dot(hit.astype(jnp.bfloat16), upper, preferred_element_type=jnp.float32) + carry
        position = jnp.sum(hit * before, axis=0, keepdims=True)
        carry = carry + jnp.sum(hit, axis=1, keepdims=True)
        places.append(jnp.where(mine >= 0, mine * cap + position.astype(jnp.int32), -1))
    dest = jnp.concatenate(places, axis=1)
    dest_ref[...] = dest
    dest = jnp.where(dest >= 0, dest ^ (lax.axis_index("mem") // (halves // 2 // groups) * blk), -1)

    units_of = []
    for j in range(rows // step):
        loads[2 + j].wait()
        wide = emb_ref[j * step : (j + 1) * step, :].astype(jnp.float32)
        total = jnp.sum(wide * wide, axis=1, keepdims=True)
        units_of.append((wide * lax.rsqrt(total + 1e-06)).astype(jnp.bfloat16))
    unit = jnp.concatenate(units_of, axis=0)

    field = lax.broadcasted_iota(jnp.int32, (LABEL_ROWS, rows), 0)
    labels = jnp.where(
        field == 0, safe_rank - which * half, jnp.where(field == 1, parity + 1, 0)
    )
    labels = jnp.where(alive, labels, 0).astype(jnp.float32).astype(jnp.bfloat16)
    per_tile = blk // TILES
    wide_tile = groups * per_tile
    spread = (
        lax.broadcasted_iota(jnp.int32, (blk, wide_tile), 0) % per_tile
        == lax.broadcasted_iota(jnp.int32, (blk, wide_tile), 1) % per_tile
    )
    spread = spread.astype(jnp.float32).astype(jnp.bfloat16)
    label_row = lax.broadcasted_iota(jnp.int32, (LABEL_ROWS, blk), 0)
    label_col = lax.broadcasted_iota(jnp.int32, (LABEL_ROWS, blk), 1)
    own_tile = label_row == lax.div(label_col, per_tile)
    unit_col = lax.div(label_col, cap).astype(jnp.float32)
    slot = lax.broadcasted_iota(jnp.int32, (blk, rows), 0)
    width = sends[0].shape[1]
    for k in range(groups):
        pick = (slot + k * blk == dest).astype(jnp.float32).astype(jnp.bfloat16)
        sends[k][0:blk, :] = jnp.dot(pick, unit, preferred_element_type=jnp.float32).astype(
            jnp.bfloat16
        )
        mine = lax.dot_general(labels, pick, NT, preferred_element_type=jnp.float32)
        plain = jnp.where(label_row == 2, unit_col, mine)
        parts = [plain] + [jnp.zeros_like(plain)] * ((wide_tile - blk) // blk)
        for f in range(2):
            line = jnp.where(own_tile, mine[f : f + 1, :], 0.0).astype(jnp.bfloat16)
            parts.append(jnp.dot(line, spread, preferred_element_type=jnp.float32))
        if width > 3 * wide_tile:
            parts.append(jnp.zeros((LABEL_ROWS, width - 3 * wide_tile), jnp.float32))
        sends[k][blk : blk + LABEL_ROWS, :] = jnp.concatenate(parts, axis=1).astype(jnp.bfloat16)


def pack(embeddings, cluster, rank, sizes):
    groups, halves, half, cap, blk = sizes
    rows, width = embeddings.shape
    vmem = pl.BlockSpec(memory_space=pltpu.VMEM)
    hbm = pl.BlockSpec(memory_space=pltpu.HBM)
    out_shape = [jax.ShapeDtypeStruct((1, rows), jnp.int32)]
    out_shape += [jax.ShapeDtypeStruct((blk + LABEL_ROWS, width), jnp.bfloat16)] * groups
    return pl.pallas_call(
        functools.partial(pack_kernel, sizes),
        out_shape=out_shape,
        in_specs=[hbm, hbm, hbm],
        out_specs=[vmem] * len(out_shape),
        scratch_shapes=[
            pltpu.VMEM((rows, width), jnp.bfloat16),
            pltpu.VMEM((1, rows), jnp.int32),
            pltpu.VMEM((1, rows), jnp.int32),
            pltpu.SemaphoreType.DMA((2 + rows // 256,)),
        ],
        compiler_params=pltpu.CompilerParams(vmem_limit_bytes=PACK_VMEM),
    )(embeddings, cluster.reshape(1, rows), rank.reshape(1, rows))


def compare_kernel(sizes, jobs, names, spots, joined, has_prev, *refs):
    groups, halves, half, cap, blk = sizes
    array = dict(zip(names, refs))
    refs = refs[len(names) :]
    block = {piece: (array[name], at * (blk + LABEL_ROWS)) for piece, (name, at) in spots.items()}
    prev = None
    if has_prev:
        prev, refs = refs[0], refs[1:]
    outs, (key_col, key_row, low_row, turned, best) = refs[:-5], refs[-5:]
    rows = groups * blk
    per_tile = blk // TILES
    tile = rows // TILES
    cap_all = float(halves * half)

    lane = lax.broadcasted_iota(jnp.int32, (LABEL_ROWS, tile), 1)
    line = lax.broadcasted_iota(jnp.int32, (LABEL_ROWS, tile), 0)
    from_block = lax.div(lane, per_tile)
    which = line * (halves // TILES) + lax.div(lane - from_block * per_tile, cap)
    weight_row = lax.broadcasted_iota(jnp.int32, (LABEL_ROWS, 128), 0)
    weights = jnp.where(
        weight_row == 0,
        1.0,
        jnp.where(weight_row == 1, cap_all, jnp.where(weight_row == 2, float(half), 0.0)),
    ).astype(jnp.bfloat16)
    needed = sorted({piece for _, pieces in jobs for piece in pieces})
    key_at = {piece: n * blk for n, piece in enumerate(needed)}

    def label_of(piece):
        ref, base = block[piece]
        return ref[base + blk : base + blk + LABEL_ROWS, :]

    for piece in needed:
        key_col[pl.ds(key_at[piece], blk), :] = lax.dot_general(
            label_of(piece)[:, 0:blk], weights, TN, preferred_element_type=jnp.float32
        )
    for o, (a, _) in enumerate(jobs):
        rest = jnp.zeros((LABEL_ROWS, tile), jnp.float32)
        code = jnp.zeros((LABEL_ROWS, tile), jnp.float32)
        for k in range(groups):
            label = label_of((a, k))[:, tile : 3 * tile].astype(jnp.float32)
            rest = jnp.where(from_block == k, label[:, :tile], rest)
            code = jnp.where(from_block == k, label[:, tile:], code)
        low = code * cap_all
        key = low + (which * half).astype(jnp.float32) + rest
        low = jnp.where(code > 0.5, low, FAR)
        key_row[o] = key[0:8]
        low_row[o] = low[0:8]

    def part_of(ref, base, t):
        return ref[pl.ds(pl.multiple_of(base + t * per_tile, per_tile), per_tile), :]

    best[...] = prev[...] if has_prev else jnp.full(best.shape, -1.0, jnp.float32)
    for o, (a, pieces) in enumerate(jobs):

        def one_tile(t, _, a=a, pieces=pieces, o=o):
            turned[...] = jnp.concatenate(
                [part_of(*block[a, k], t) for k in range(groups)], axis=0
            ).T
            mine = key_row[o, pl.ds(t, 1), :]
            floor = low_row[o, pl.ds(t, 1), :]

            def one_col(s, acc):
                theirs = [part_of(key_col, key_at[piece], s) for piece in pieces]
                theirs = jnp.concatenate(theirs, axis=0)
                theirs = jnp.concatenate([theirs] * (tile // 128), axis=1)
                sims = jnp.dot(
                    jnp.concatenate([part_of(*block[piece], s) for piece in pieces], axis=0),
                    turned[...],
                    preferred_element_type=jnp.float32,
                )
                keep = (theirs >= floor) & (theirs < mine)
                sims = jnp.where(keep, sims, -1.0)
                top = jnp.max(sims.reshape(len(pieces) * per_tile // 8, 8, tile), axis=0)
                return jnp.maximum(acc, top)

            acc = lax.fori_loop(0, t + 1, one_col, jnp.full((8, tile), -1.0, jnp.float32))
            best[a, pl.ds(t, 1), :] = jnp.maximum(
                best[a, pl.ds(t, 1), :], jnp.max(acc, axis=0, keepdims=True)
            )
            return 0

        lax.fori_loop(0, TILES, one_tile, 0)

    if not has_prev:
        outs[0][...] = best[...]
        return
    lane = lax.broadcasted_iota(jnp.int32, (1, tile), 1)
    side = halves // 2 // groups
    here = lax.axis_index("mem")
    for o, (a, _) in enumerate(jobs):
        found = best[a]
        for k in range(groups):
            total = jnp.full((1, tile), -1.0, jnp.float32)
            for t in range(TILES):
                turn = ((t - k) * per_tile) % tile
                moved = pltpu.roll(found, turn, 1) if turn else found
                total = jnp.where(lax.div(lane, per_tile) == t, moved[t : t + 1], total)
            at = (here // side) ^ k
            if joined:
                outs[0][pl.ds(at * joined + ((here % side) ^ a), 1), 0, :] = total[:, :blk]
            else:
                outs[o][pl.ds(at, 1), 0, :] = total[:, :blk]


def compare(blocks, jobs, prev, joined, n_sets, sizes):
    groups, halves, half, cap, blk = sizes
    used = {piece for _, pieces in jobs for piece in pieces}
    used |= {(a, k) for a, _ in jobs for k in range(groups)}
    spots = {}
    arrays = {}
    for piece in sorted(used):
        value, at = blocks[piece]
        name = next((n for n, v in arrays.items() if v is value), None)
        if name is None:
            name = len(arrays)
            arrays[name] = value
        spots[piece] = (name, at)
    names = list(arrays)
    width = arrays[0].shape[1]
    tile = groups * blk // TILES
    vmem = pl.BlockSpec(memory_space=pltpu.VMEM)
    steps = TILES * (TILES + 1) // 2
    work = sum(len(pieces) for _, pieces in jobs) * steps * (blk // TILES) * tile * width
    if prev is None:
        out_shape = [jax.ShapeDtypeStruct((n_sets, 8, tile), jnp.float32)]
    elif joined:
        out_shape = [jax.ShapeDtypeStruct((groups * joined, 1, blk), jnp.float32)]
    else:
        out_shape = [jax.ShapeDtypeStruct((groups, 1, blk), jnp.float32)] * len(jobs)
    operands = list(arrays.values()) + ([] if prev is None else [prev])
    needed = {piece for _, pieces in jobs for piece in pieces}
    return pl.pallas_call(
        functools.partial(compare_kernel, sizes, jobs, names, spots, joined, prev is not None),
        out_shape=out_shape,
        in_specs=[vmem] * len(operands),
        out_specs=[vmem] * len(out_shape),
        scratch_shapes=[
            pltpu.VMEM((len(needed) * blk, 128), jnp.float32),
            pltpu.VMEM((len(jobs), 8, tile), jnp.float32),
            pltpu.VMEM((len(jobs), 8, tile), jnp.float32),
            pltpu.VMEM((width, tile), jnp.bfloat16),
            pltpu.VMEM((n_sets, 8, tile), jnp.float32),
        ],
        compiler_params=pltpu.CompilerParams(vmem_limit_bytes=COMPARE_VMEM),
        cost_estimate=pl.CostEstimate(
            flops=2 * work, bytes_accessed=2 * len(used) * blk * width, transcendentals=0
        ),
    )(*operands)


def join_kernel(first_ref, second_ref, out_ref):
    rows = first_ref.shape[0]
    out_ref[:rows, :] = first_ref[...]
    out_ref[rows:, :] = second_ref[...]


def join(first, second):
    rows, width = first.shape
    vmem = pl.BlockSpec(memory_space=pltpu.VMEM)
    return pl.pallas_call(
        join_kernel,
        out_shape=jax.ShapeDtypeStruct((2 * rows, width), first.dtype),
        in_specs=[vmem, vmem],
        out_specs=vmem,
        compiler_params=pltpu.CompilerParams(vmem_limit_bytes=COMPARE_VMEM),
    )(first, second)


def unpack_kernel(sizes, dest_ref, back_ref, out_ref):
    groups, halves, half, cap, blk = sizes
    side = back_ref.shape[0] // groups
    rows = dest_ref.shape[1]
    dest = dest_ref[...]
    slot = lax.broadcasted_iota(jnp.int32, (blk, rows), 0)
    field = lax.broadcasted_iota(jnp.int32, (LABEL_ROWS, blk), 0)
    total = jnp.zeros((LABEL_ROWS, rows), jnp.float32)
    for k in range(groups):
        value = back_ref[k * side]
        for more in range(1, side):
            value = jnp.maximum(value, back_ref[k * side + more])
        top = value.astype(jnp.bfloat16).astype(jnp.float32)
        rest = value - top
        mid = rest.astype(jnp.bfloat16).astype(jnp.float32)
        low = rest - mid
        stack = jnp.where(field == 0, top, jnp.where(field == 1, mid, jnp.where(field == 2, low, 0.0)))
        pick = (slot + k * blk == dest).astype(jnp.float32).astype(jnp.bfloat16)
        total = total + jnp.dot(stack.astype(jnp.bfloat16), pick, preferred_element_type=jnp.float32)
    value = (total[0:1] + total[1:2]) + total[2:3]
    out_ref[...] = jnp.where(dest >= 0, value, -1.0)


def unpack(dest, back, sizes):
    vmem = pl.BlockSpec(memory_space=pltpu.VMEM)
    return pl.pallas_call(
        functools.partial(unpack_kernel, sizes),
        out_shape=jax.ShapeDtypeStruct(dest.shape, jnp.float32),
        in_specs=[vmem] * 2,
        out_specs=vmem,
        compiler_params=pltpu.CompilerParams(vmem_limit_bytes=COMPARE_VMEM),
    )(dest, back)


def on_device(embeddings, cluster, rank):
    rows_dev, width = embeddings.shape
    groups = lax.axis_size("grp")
    members = lax.axis_size("mem")
    devices = groups * members
    halves = 2 * members
    half = rows_dev // CLUS_GRP // 2
    blk = rows_dev // groups
    cap = blk // halves
    sizes = (groups, halves, half, cap, blk)
    side = members // groups

    def swap(value, block_step, member_step):
        mask = member_step // side * members + block_step * side + member_step % side
        if mask == 0:
            return value
        return lax.ppermute(value, ("grp", "mem"), [(i, i ^ mask) for i in range(devices)])

    offsets, pairs = cover(members)
    packed = pack(embeddings, cluster, rank, sizes)
    dest, sends = packed[0], packed[1:]

    last = groups - 1
    far = [d for d in offsets if d & side and d != side and d ^ side in offsets]
    near = [d for d in offsets[1:] if d not in far]
    lead = far[0] ^ side if far else near[0]
    held = {0: [sends[0]]}
    for d in near:
        held[d] = [swap(sends[0], 0, d)]
    for d in far:
        held[d] = [swap(held[d ^ side][0], 0, side)]
    after = held[lead][0]
    for k in range(1, groups, 2):
        if k > 1:
            send, after = lax.optimization_barrier((sends[k], after))
        else:
            send = sends[k]
        mine = swap(send, k, 0)
        if k < last:
            also = swap(sends[k + 1], k + 1, 0)
            if k == 1:
                mine, also, *firsts = lax.optimization_barrier(
                    (mine, also, *(held[d][0] for d in near))
                )
                for d, first in zip(near, firsts):
                    held[d] = [first]
            mine = join(mine, also)
            after = mine
        held[0].append(mine)
        for d in near:
            held[d].append(swap(mine, 0, d))
    for spot in range(1, len(held[0]) - 1):
        for d in far:
            piece, held[0][spot + 1] = lax.optimization_barrier(
                (held[d ^ side][spot], held[0][spot + 1])
            )
            held[d].append(swap(piece, 0, side))

    index = {d: i for i, d in enumerate(offsets)}
    starts = sorted({a for a, _ in pairs.values()})
    early, late = [], []
    for a in starts:
        cols = [index[b] for _, (e, b) in sorted(pairs.items()) if e == a]
        pieces = [(b, k) for b in cols for k in range(groups)]
        if a == 0:
            soon = [(b, k) for b, k in pieces if b == 0 or k < last]
            early.append((0, soon))
            pieces = [piece for piece in pieces if piece not in soon]
        late.append((index[a], pieces))
    joined = side if all(a < side for a in starts) else 0
    blocks = {}
    for d in offsets:
        for k in range(groups):
            spot = (k + 1) // 2
            if spot < len(held[d]):
                blocks[index[d], k] = (held[d][spot], 1 - k % 2 if 0 < k < last else 0)
    prev = compare(blocks, early, None, 0, len(offsets), sizes)[0]
    for d in far:
        piece, prev = lax.optimization_barrier((held[d ^ side][-1], prev))
        blocks[index[d], last] = (swap(piece, 0, side), 0)
    found = compare(blocks, late, prev, joined, len(offsets), sizes)
    if joined:
        back = found[0]
    else:
        best = {}
        for a, value in zip(starts, found):
            near = a % side
            value = swap(value, 0, a - near)
            best[near] = jnp.maximum(best[near], value) if near in best else value
        none = jnp.full_like(found[0], -1.0)
        near_of = [best.get(near, none) for near in range(side)]
        rows_of = []
        for spot in range(side):
            value = near_of[spot]
            for mine in range(1, side):
                value = jnp.where(lax.axis_index("mem") % side == mine, near_of[spot ^ mine], value)
            rows_of.append(value)
        back = jnp.stack(rows_of, axis=1).reshape(groups * side, 1, blk)
    back = lax.all_to_all(back, "mem", split_axis=0, concat_axis=0, tiled=True)
    return unpack(dest, back, sizes).reshape(rows_dev)


def solution(mesh):
    in_specs = (P(("grp", "mem"), None), P(("grp", "mem")), P(("grp", "mem")))
    out_specs = P(("grp", "mem"))
    return jax.shard_map(
        on_device, mesh=mesh, in_specs=in_specs, out_specs=out_specs, check_vma=False
    )
```

```python
import functools

import jax
import jax.numpy as jnp
from jax import lax
from jax.experimental import pallas as pl
from jax.experimental.pallas import tpu as pltpu
from jax.sharding import PartitionSpec as P

CLUS_GRP = 2
TILES = 4
LABEL_ROWS = 16
FAR = 1.0e9
PACK_VMEM = 60 * 1024 * 1024
COMPARE_VMEM = 24 * 1024 * 1024
NT = (((1,), (1,)), ((), ()))
TN = (((0,), (0,)), ((), ()))


def cover(members):
    bits = [1 << i for i in range(members.bit_length() - 1)]
    offsets = [0] + bits

    def missing(held):
        return set(range(members)) - {a ^ b for a in held for b in held}

    while missing(offsets):
        offsets.append(
            min(
                (d for d in range(members) if d not in offsets),
                key=lambda d: (len(missing(offsets + [d])), bin(d).count("1"), -d),
            )
        )
    pairs = {}
    for delta in range(members):
        pairs[delta] = min(
            (a, a ^ delta) for a in offsets if a ^ delta in offsets
        )
    return offsets, pairs


def pack_kernel(sizes, ks, emb_hbm, cluster_hbm, rank_hbm, *refs):
    groups, halves, half, cap, blk = sizes
    dest_ref, outs = refs[0], refs[1 : 1 + len(ks)]
    emb_ref, cluster_ref, rank_ref, stage, sems, out_sems = refs[1 + len(ks) :]
    rows = emb_ref.shape[0]
    step = 256
    loads = [
        pltpu.make_async_copy(cluster_hbm, cluster_ref, sems.at[0]),
        pltpu.make_async_copy(rank_hbm, rank_ref, sems.at[1]),
    ]
    for j in range(rows // step):
        at = pl.ds(j * step, step)
        loads.append(pltpu.make_async_copy(emb_hbm.at[at], emb_ref.at[at], sems.at[2 + j]))
    for load in loads:
        load.start()
    for load in loads[:2]:
        load.wait()
    cluster = cluster_ref[...]
    rank = rank_ref[...]
    alive = cluster >= 0
    pair = lax.shift_right_logical(jnp.maximum(cluster, 0), 1)
    parity = jnp.maximum(cluster, 0) - 2 * pair
    safe_rank = jnp.maximum(rank, 0)
    which = safe_rank // half
    units = groups * halves
    unit_id = jnp.where(alive, pair * halves + which, -1)
    before_rows = lax.broadcasted_iota(jnp.int32, (step, step), 0)
    before_cols = lax.broadcasted_iota(jnp.int32, (step, step), 1)
    upper = (before_rows < before_cols).astype(jnp.float32).astype(jnp.bfloat16)
    unit_iota = lax.broadcasted_iota(jnp.int32, (units, step), 0)
    carry = jnp.zeros((units, 1), jnp.float32)
    places = []
    for j in range(rows // step):
        mine = unit_id[:, j * step : (j + 1) * step]
        hit = (unit_iota == mine).astype(jnp.float32)
        before = jnp.dot(hit.astype(jnp.bfloat16), upper, preferred_element_type=jnp.float32) + carry
        position = jnp.sum(hit * before, axis=0, keepdims=True)
        carry = carry + jnp.sum(hit, axis=1, keepdims=True)
        places.append(jnp.where(mine >= 0, mine * cap + position.astype(jnp.int32), -1))
    dest = jnp.concatenate(places, axis=1)
    dest_ref[...] = dest
    dest = jnp.where(dest >= 0, dest ^ (lax.axis_index("mem") // (halves // 2 // groups) * blk), -1)

    units_of = []
    for j in range(rows // step):
        loads[2 + j].wait()
        wide = emb_ref[j * step : (j + 1) * step, :].astype(jnp.float32)
        total = jnp.sum(wide * wide, axis=1, keepdims=True)
        units_of.append((wide * lax.rsqrt(total + 1e-06)).astype(jnp.bfloat16))
    unit = jnp.concatenate(units_of, axis=0)

    field = lax.broadcasted_iota(jnp.int32, (LABEL_ROWS, rows), 0)
    labels = jnp.where(
        field == 0, safe_rank - which * half, jnp.where(field == 1, parity + 1, 0)
    )
    labels = jnp.where(alive, labels, 0).astype(jnp.float32).astype(jnp.bfloat16)
    per_tile = blk // TILES
    wide_tile = groups * per_tile
    spread = (
        lax.broadcasted_iota(jnp.int32, (blk, wide_tile), 0) % per_tile
        == lax.broadcasted_iota(jnp.int32, (blk, wide_tile), 1) % per_tile
    )
    spread = spread.astype(jnp.float32).astype(jnp.bfloat16)
    label_row = lax.broadcasted_iota(jnp.int32, (LABEL_ROWS, blk), 0)
    label_col = lax.broadcasted_iota(jnp.int32, (LABEL_ROWS, blk), 1)
    own_tile = label_row == lax.div(label_col, per_tile)
    unit_col = lax.div(label_col, cap).astype(jnp.float32)
    slot = lax.broadcasted_iota(jnp.int32, (blk, rows), 0)
    width = emb_ref.shape[1]
    leaving = []
    for n, k in enumerate(ks):
        pick = (slot + k * blk == dest).astype(jnp.float32).astype(jnp.bfloat16)
        stage[n, 0:blk, :] = jnp.dot(pick, unit, preferred_element_type=jnp.float32).astype(
            jnp.bfloat16
        )
        mine = lax.dot_general(labels, pick, NT, preferred_element_type=jnp.float32)
        plain = jnp.where(label_row == 2, unit_col, mine)
        parts = [plain] + [jnp.zeros_like(plain)] * ((wide_tile - blk) // blk)
        for f in range(2):
            line = jnp.where(own_tile, mine[f : f + 1, :], 0.0).astype(jnp.bfloat16)
            parts.append(jnp.dot(line, spread, preferred_element_type=jnp.float32))
        if width > 3 * wide_tile:
            parts.append(jnp.zeros((LABEL_ROWS, width - 3 * wide_tile), jnp.float32))
        stage[n, blk : blk + LABEL_ROWS, :] = jnp.concatenate(parts, axis=1).astype(jnp.bfloat16)
        leaving.append(pltpu.make_async_copy(stage.at[n], outs[n], out_sems.at[n]))
        leaving[-1].start()
    for copy in leaving:
        copy.wait()


def pack(embeddings, cluster, rank, ks, sizes):
    groups, halves, half, cap, blk = sizes
    rows, width = embeddings.shape
    hbm = pl.BlockSpec(memory_space=pltpu.HBM)
    out_shape = [jax.ShapeDtypeStruct((1, rows), jnp.int32)]
    out_shape += [jax.ShapeDtypeStruct((blk + LABEL_ROWS, width), jnp.bfloat16)] * len(ks)
    return pl.pallas_call(
        functools.partial(pack_kernel, sizes, ks),
        out_shape=out_shape,
        in_specs=[hbm, hbm, hbm],
        out_specs=[pl.BlockSpec(memory_space=pltpu.VMEM)] + [hbm] * len(ks),
        scratch_shapes=[
            pltpu.VMEM((rows, width), jnp.bfloat16),
            pltpu.VMEM((1, rows), jnp.int32),
            pltpu.VMEM((1, rows), jnp.int32),
            pltpu.VMEM((len(ks), blk + LABEL_ROWS, width), jnp.bfloat16),
            pltpu.SemaphoreType.DMA((2 + rows // 256,)),
            pltpu.SemaphoreType.DMA((len(ks),)),
        ],
        compiler_params=pltpu.CompilerParams(vmem_limit_bytes=PACK_VMEM),
        cost_estimate=pl.CostEstimate(
            flops=2 * len(ks) * blk * rows * width, bytes_accessed=4 * rows * width, transcendentals=0
        ),
    )(embeddings, cluster.reshape(1, rows), rank.reshape(1, rows))


def compare_kernel(sizes, jobs, names, spots, joined, has_prev, *refs):
    groups, halves, half, cap, blk = sizes
    array = dict(zip(names, refs))
    refs = refs[len(names) :]
    block = {piece: (array[name], at * (blk + LABEL_ROWS)) for piece, (name, at) in spots.items()}
    prev = None
    if has_prev:
        prev, refs = refs[0], refs[1:]
    outs, (key_col, key_row, low_row, turned, best) = refs[:-5], refs[-5:]
    rows = groups * blk
    per_tile = blk // TILES
    tile = rows // TILES
    cap_all = float(halves * half)

    lane = lax.broadcasted_iota(jnp.int32, (LABEL_ROWS, tile), 1)
    line = lax.broadcasted_iota(jnp.int32, (LABEL_ROWS, tile), 0)
    from_block = lax.div(lane, per_tile)
    which = line * (halves // TILES) + lax.div(lane - from_block * per_tile, cap)
    weight_row = lax.broadcasted_iota(jnp.int32, (LABEL_ROWS, 128), 0)
    weights = jnp.where(
        weight_row == 0,
        1.0,
        jnp.where(weight_row == 1, cap_all, jnp.where(weight_row == 2, float(half), 0.0)),
    ).astype(jnp.bfloat16)
    needed = sorted({piece for _, pieces in jobs for piece in pieces})
    key_at = {piece: n * blk for n, piece in enumerate(needed)}

    def label_of(piece):
        ref, base = block[piece]
        return ref[base + blk : base + blk + LABEL_ROWS, :]

    for piece in needed:
        key_col[pl.ds(key_at[piece], blk), :] = lax.dot_general(
            label_of(piece)[:, 0:blk], weights, TN, preferred_element_type=jnp.float32
        )
    for o, (a, _) in enumerate(jobs):
        rest = jnp.zeros((LABEL_ROWS, tile), jnp.float32)
        code = jnp.zeros((LABEL_ROWS, tile), jnp.float32)
        for k in range(groups):
            label = label_of((a, k))[:, tile : 3 * tile].astype(jnp.float32)
            rest = jnp.where(from_block == k, label[:, :tile], rest)
            code = jnp.where(from_block == k, label[:, tile:], code)
        low = code * cap_all
        key = low + (which * half).astype(jnp.float32) + rest
        low = jnp.where(code > 0.5, low, FAR)
        key_row[o] = key[0:8]
        low_row[o] = low[0:8]

    def rows_of(ref, base, first, last):
        return ref[base + first * per_tile : base + last * per_tile, :]

    best[...] = prev[...] if has_prev else jnp.full(best.shape, -1.0, jnp.float32)
    for o, (a, pieces) in enumerate(jobs):
        for t in range(TILES):
            turned[o, t] = jnp.concatenate(
                [rows_of(*block[a, k], t, t + 1) for k in range(groups)], axis=0
            ).T
            mine = key_row[o, t : t + 1, :]
            floor = low_row[o, t : t + 1, :]
            acc = jnp.full((8, tile), -1.0, jnp.float32)
            for at in range(0, len(pieces), groups):
                some = pieces[at : at + groups]
                theirs = [rows_of(key_col, key_at[piece], 0, t + 1) for piece in some]
                theirs = jnp.concatenate(theirs, axis=0)
                theirs = jnp.concatenate([theirs] * (tile // 128), axis=1)
                sims = jnp.dot(
                    jnp.concatenate([rows_of(*block[piece], 0, t + 1) for piece in some], axis=0),
                    turned[o, t],
                    preferred_element_type=jnp.float32,
                )
                keep = (theirs >= floor) & (theirs < mine)
                sims = jnp.where(keep, sims, -1.0)
                top = jnp.max(sims.reshape(sims.shape[0] // 8, 8, tile), axis=0)
                acc = jnp.maximum(acc, top)
            best[a, t : t + 1, :] = jnp.maximum(
                best[a, t : t + 1, :], jnp.max(acc, axis=0, keepdims=True)
            )

    if not has_prev:
        outs[0][...] = best[...]
        return
    lane = lax.broadcasted_iota(jnp.int32, (1, tile), 1)
    side = halves // 2 // groups
    here = lax.axis_index("mem")
    for o, (a, _) in enumerate(jobs):
        found = best[a]
        for k in range(groups):
            total = jnp.full((1, tile), -1.0, jnp.float32)
            for t in range(TILES):
                turn = ((t - k) * per_tile) % tile
                moved = pltpu.roll(found, turn, 1) if turn else found
                total = jnp.where(lax.div(lane, per_tile) == t, moved[t : t + 1], total)
            at = (here // side) ^ k
            if joined:
                outs[0][pl.ds(at * joined + ((here % side) ^ a), 1), 0, :] = total[:, :blk]
            else:
                outs[o][pl.ds(at, 1), 0, :] = total[:, :blk]


def compare(blocks, jobs, prev, joined, n_sets, sizes):
    groups, halves, half, cap, blk = sizes
    used = {piece for _, pieces in jobs for piece in pieces}
    used |= {(a, k) for a, _ in jobs for k in range(groups)}
    spots = {}
    arrays = {}
    for piece in sorted(used):
        value, at = blocks[piece]
        name = next((n for n, v in arrays.items() if v is value), None)
        if name is None:
            name = len(arrays)
            arrays[name] = value
        spots[piece] = (name, at)
    names = list(arrays)
    width = arrays[0].shape[1]
    tile = groups * blk // TILES
    vmem = pl.BlockSpec(memory_space=pltpu.VMEM)
    steps = TILES * (TILES + 1) // 2
    work = sum(len(pieces) for _, pieces in jobs) * steps * (blk // TILES) * tile * width
    if prev is None:
        out_shape = [jax.ShapeDtypeStruct((n_sets, 8, tile), jnp.float32)]
    elif joined:
        out_shape = [jax.ShapeDtypeStruct((groups * joined, 1, blk), jnp.float32)]
    else:
        out_shape = [jax.ShapeDtypeStruct((groups, 1, blk), jnp.float32)] * len(jobs)
    operands = list(arrays.values()) + ([] if prev is None else [prev])
    needed = {piece for _, pieces in jobs for piece in pieces}
    return pl.pallas_call(
        functools.partial(compare_kernel, sizes, jobs, names, spots, joined, prev is not None),
        out_shape=out_shape,
        in_specs=[vmem] * len(operands),
        out_specs=[vmem] * len(out_shape),
        scratch_shapes=[
            pltpu.VMEM((len(needed) * blk, 128), jnp.float32),
            pltpu.VMEM((len(jobs), 8, tile), jnp.float32),
            pltpu.VMEM((len(jobs), 8, tile), jnp.float32),
            pltpu.VMEM((len(jobs), TILES, width, tile), jnp.bfloat16),
            pltpu.VMEM((n_sets, 8, tile), jnp.float32),
        ],
        compiler_params=pltpu.CompilerParams(vmem_limit_bytes=COMPARE_VMEM),
        cost_estimate=pl.CostEstimate(
            flops=2 * work, bytes_accessed=2 * len(used) * blk * width, transcendentals=0
        ),
    )(*operands)


def join_kernel(first_ref, second_ref, out_ref):
    rows = first_ref.shape[0]
    out_ref[:rows, :] = first_ref[...]
    out_ref[rows:, :] = second_ref[...]


def join(first, second):
    rows, width = first.shape
    vmem = pl.BlockSpec(memory_space=pltpu.VMEM)
    return pl.pallas_call(
        join_kernel,
        out_shape=jax.ShapeDtypeStruct((2 * rows, width), first.dtype),
        in_specs=[vmem, vmem],
        out_specs=vmem,
        compiler_params=pltpu.CompilerParams(vmem_limit_bytes=COMPARE_VMEM),
    )(first, second)


def unpack_kernel(sizes, dest_ref, back_ref, out_ref):
    groups, halves, half, cap, blk = sizes
    side = back_ref.shape[0] // groups
    rows = dest_ref.shape[1]
    dest = dest_ref[...]
    slot = lax.broadcasted_iota(jnp.int32, (blk, rows), 0)
    field = lax.broadcasted_iota(jnp.int32, (LABEL_ROWS, blk), 0)
    total = jnp.zeros((LABEL_ROWS, rows), jnp.float32)
    for k in range(groups):
        value = back_ref[k * side]
        for more in range(1, side):
            value = jnp.maximum(value, back_ref[k * side + more])
        top = value.astype(jnp.bfloat16).astype(jnp.float32)
        rest = value - top
        mid = rest.astype(jnp.bfloat16).astype(jnp.float32)
        low = rest - mid
        stack = jnp.where(field == 0, top, jnp.where(field == 1, mid, jnp.where(field == 2, low, 0.0)))
        pick = (slot + k * blk == dest).astype(jnp.float32).astype(jnp.bfloat16)
        total = total + jnp.dot(stack.astype(jnp.bfloat16), pick, preferred_element_type=jnp.float32)
    value = (total[0:1] + total[1:2]) + total[2:3]
    out_ref[...] = jnp.where(dest >= 0, value, -1.0)


def unpack(dest, back, sizes):
    vmem = pl.BlockSpec(memory_space=pltpu.VMEM)
    return pl.pallas_call(
        functools.partial(unpack_kernel, sizes),
        out_shape=jax.ShapeDtypeStruct(dest.shape, jnp.float32),
        in_specs=[vmem] * 2,
        out_specs=vmem,
        compiler_params=pltpu.CompilerParams(vmem_limit_bytes=COMPARE_VMEM),
    )(dest, back)


def on_device(embeddings, cluster, rank):
    rows_dev, width = embeddings.shape
    groups = lax.axis_size("grp")
    members = lax.axis_size("mem")
    devices = groups * members
    halves = 2 * members
    half = rows_dev // CLUS_GRP // 2
    blk = rows_dev // groups
    cap = blk // halves
    sizes = (groups, halves, half, cap, blk)
    side = members // groups

    def swap(value, block_step, member_step):
        mask = member_step // side * members + block_step * side + member_step % side
        if mask == 0:
            return value
        return lax.ppermute(value, ("grp", "mem"), [(i, i ^ mask) for i in range(devices)])

    offsets, pairs = cover(members)
    sends = [None] * groups
    first = tuple(range(1, min(3, groups)))
    dest, *packed = pack(embeddings, cluster, rank, first, sizes)
    for k, value in zip(first, packed):
        sends[k] = value
    rest = tuple(k for k in range(groups) if k not in first)
    cluster, dest = lax.optimization_barrier((cluster, dest))
    _, *packed = pack(embeddings, cluster, rank, rest, sizes)
    for k, value in zip(rest, packed):
        sends[k] = value

    last = groups - 1
    far = [d for d in offsets if d & side and d != side and d ^ side in offsets]
    near = [d for d in offsets[1:] if d not in far]
    lead = far[0] ^ side if far else near[0]
    held = {0: [sends[0]]}
    for d in near:
        held[d] = [swap(sends[0], 0, d)]
    for d in far:
        held[d] = [swap(held[d ^ side][0], 0, side)]
    after = held[lead][0]
    for k in range(1, groups, 2):
        if k > 1:
            send, after = lax.optimization_barrier((sends[k], after))
        else:
            send = sends[k]
        mine = swap(send, k, 0)
        if k < last:
            also = swap(sends[k + 1], k + 1, 0)
            if k == 1:
                mine, also, *firsts = lax.optimization_barrier(
                    (mine, also, *(held[d][0] for d in near))
                )
                for d, first in zip(near, firsts):
                    held[d] = [first]
            mine = join(mine, also)
            after = mine
        held[0].append(mine)
        for d in near:
            held[d].append(swap(mine, 0, d))
    for spot in range(1, len(held[0]) - 1):
        values = lax.optimization_barrier(
            (held[0][spot + 1], *(held[d][spot] for d in near))
        )
        held[0][spot + 1] = values[0]
        for d, value in zip(near, values[1:]):
            held[d][spot] = value
        for d in far:
            held[d].append(swap(held[d ^ side][spot], 0, side))

    index = {d: i for i, d in enumerate(offsets)}
    starts = sorted({a for a, _ in pairs.values()})
    early, late = [], []
    for a in starts:
        cols = [index[b] for _, (e, b) in sorted(pairs.items()) if e == a]
        pieces = [(b, k) for b in cols for k in range(groups)]
        if a == 0:
            soon = [(b, k) for b, k in pieces if b == 0 or k < last]
            early.append((0, soon))
            pieces = [piece for piece in pieces if piece not in soon]
        late.append((index[a], pieces))
    joined = side if all(a < side for a in starts) else 0
    blocks = {}
    for d in offsets:
        for k in range(groups):
            spot = (k + 1) // 2
            if spot < len(held[d]):
                blocks[index[d], k] = (held[d][spot], 1 - k % 2 if 0 < k < last else 0)
    prev = compare(blocks, early, None, 0, len(offsets), sizes)[0]
    for d in far:
        piece, prev = lax.optimization_barrier((held[d ^ side][-1], prev))
        blocks[index[d], last] = (swap(piece, 0, side), 0)
    found = compare(blocks, late, prev, joined, len(offsets), sizes)
    if joined:
        back = found[0]
    else:
        best = {}
        for a, value in zip(starts, found):
            near = a % side
            value = swap(value, 0, a - near)
            best[near] = jnp.maximum(best[near], value) if near in best else value
        none = jnp.full_like(found[0], -1.0)
        near_of = [best.get(near, none) for near in range(side)]
        rows_of = []
        for spot in range(side):
            value = near_of[spot]
            for mine in range(1, side):
                value = jnp.where(lax.axis_index("mem") % side == mine, near_of[spot ^ mine], value)
            rows_of.append(value)
        back = jnp.stack(rows_of, axis=1).reshape(groups * side, 1, blk)
    back = lax.all_to_all(back, "mem", split_axis=0, concat_axis=0, tiled=True)
    return unpack(dest, back, sizes).reshape(rows_dev)


def solution(mesh):
    in_specs = (P(("grp", "mem"), None), P(("grp", "mem")), P(("grp", "mem")))
    out_specs = P(("grp", "mem"))
    return jax.shard_map(
        on_device, mesh=mesh, in_specs=in_specs, out_specs=out_specs, check_vma=False
    )
```

```python
import functools

import jax
import jax.numpy as jnp
from jax import lax
from jax.experimental import pallas as pl
from jax.experimental.pallas import tpu as pltpu
from jax.sharding import PartitionSpec as P

CLUS_GRP = 2
TILES = 4
LABEL_ROWS = 16
FAR = 1.0e9
JOIN_FLOPS = 10_000_000_000
PACK_VMEM = 60 * 1024 * 1024
COMPARE_VMEM = 24 * 1024 * 1024
NT = (((1,), (1,)), ((), ()))
TN = (((0,), (0,)), ((), ()))


def cover(members):
    bits = [1 << i for i in range(members.bit_length() - 1)]
    offsets = [0] + bits

    def missing(held):
        return set(range(members)) - {a ^ b for a in held for b in held}

    while missing(offsets):
        offsets.append(
            min(
                (d for d in range(members) if d not in offsets),
                key=lambda d: (len(missing(offsets + [d])), bin(d).count("1"), -d),
            )
        )
    pairs = {}
    for delta in range(members):
        pairs[delta] = min(
            (a, a ^ delta) for a in offsets if a ^ delta in offsets
        )
    return offsets, pairs


def pack_kernel(sizes, ks, emb_hbm, cluster_hbm, rank_hbm, *refs):
    groups, halves, half, cap, blk = sizes
    dest_ref, outs = refs[0], refs[1 : 1 + len(ks)]
    emb_ref, cluster_ref, rank_ref, stage, sems, out_sems = refs[1 + len(ks) :]
    rows = emb_ref.shape[0]
    step = 256
    loads = [
        pltpu.make_async_copy(cluster_hbm, cluster_ref, sems.at[0]),
        pltpu.make_async_copy(rank_hbm, rank_ref, sems.at[1]),
    ]
    for j in range(rows // step):
        at = pl.ds(j * step, step)
        loads.append(pltpu.make_async_copy(emb_hbm.at[at], emb_ref.at[at], sems.at[2 + j]))
    for load in loads:
        load.start()
    for load in loads[:2]:
        load.wait()
    cluster = cluster_ref[...]
    rank = rank_ref[...]
    alive = cluster >= 0
    pair = lax.shift_right_logical(jnp.maximum(cluster, 0), 1)
    parity = jnp.maximum(cluster, 0) - 2 * pair
    safe_rank = jnp.maximum(rank, 0)
    which = safe_rank // half
    units = groups * halves
    unit_id = jnp.where(alive, pair * halves + which, -1)
    before_rows = lax.broadcasted_iota(jnp.int32, (step, step), 0)
    before_cols = lax.broadcasted_iota(jnp.int32, (step, step), 1)
    upper = (before_rows < before_cols).astype(jnp.float32).astype(jnp.bfloat16)
    unit_iota = lax.broadcasted_iota(jnp.int32, (units, step), 0)
    carry = jnp.zeros((units, 1), jnp.float32)
    places = []
    for j in range(rows // step):
        mine = unit_id[:, j * step : (j + 1) * step]
        hit = (unit_iota == mine).astype(jnp.float32)
        before = jnp.dot(hit.astype(jnp.bfloat16), upper, preferred_element_type=jnp.float32) + carry
        position = jnp.sum(hit * before, axis=0, keepdims=True)
        carry = carry + jnp.sum(hit, axis=1, keepdims=True)
        places.append(jnp.where(mine >= 0, mine * cap + position.astype(jnp.int32), -1))
    dest = jnp.concatenate(places, axis=1)
    dest_ref[...] = dest
    dest = jnp.where(dest >= 0, dest ^ (lax.axis_index("mem") // (halves // 2 // groups) * blk), -1)

    units_of = []
    for j in range(rows // step):
        loads[2 + j].wait()
        wide = emb_ref[j * step : (j + 1) * step, :].astype(jnp.float32)
        total = jnp.sum(wide * wide, axis=1, keepdims=True)
        units_of.append((wide * lax.rsqrt(total + 1e-06)).astype(jnp.bfloat16))
    unit = jnp.concatenate(units_of, axis=0)

    field = lax.broadcasted_iota(jnp.int32, (LABEL_ROWS, rows), 0)
    labels = jnp.where(
        field == 0, safe_rank - which * half, jnp.where(field == 1, parity + 1, 0)
    )
    labels = jnp.where(alive, labels, 0).astype(jnp.float32).astype(jnp.bfloat16)
    per_tile = blk // TILES
    wide_tile = groups * per_tile
    spread = (
        lax.broadcasted_iota(jnp.int32, (blk, wide_tile), 0) % per_tile
        == lax.broadcasted_iota(jnp.int32, (blk, wide_tile), 1) % per_tile
    )
    spread = spread.astype(jnp.float32).astype(jnp.bfloat16)
    label_row = lax.broadcasted_iota(jnp.int32, (LABEL_ROWS, blk), 0)
    label_col = lax.broadcasted_iota(jnp.int32, (LABEL_ROWS, blk), 1)
    own_tile = label_row == lax.div(label_col, per_tile)
    unit_col = lax.div(label_col, cap).astype(jnp.float32)
    slot = lax.broadcasted_iota(jnp.int32, (blk, rows), 0)
    width = emb_ref.shape[1]
    leaving = []
    for n, k in enumerate(ks):
        pick = (slot + k * blk == dest).astype(jnp.float32).astype(jnp.bfloat16)
        stage[n, 0:blk, :] = jnp.dot(pick, unit, preferred_element_type=jnp.float32).astype(
            jnp.bfloat16
        )
        mine = lax.dot_general(labels, pick, NT, preferred_element_type=jnp.float32)
        plain = jnp.where(label_row == 2, unit_col, mine)
        parts = [plain] + [jnp.zeros_like(plain)] * ((wide_tile - blk) // blk)
        for f in range(2):
            line = jnp.where(own_tile, mine[f : f + 1, :], 0.0).astype(jnp.bfloat16)
            parts.append(jnp.dot(line, spread, preferred_element_type=jnp.float32))
        if width > 3 * wide_tile:
            parts.append(jnp.zeros((LABEL_ROWS, width - 3 * wide_tile), jnp.float32))
        stage[n, blk : blk + LABEL_ROWS, :] = jnp.concatenate(parts, axis=1).astype(jnp.bfloat16)
        leaving.append(pltpu.make_async_copy(stage.at[n], outs[n], out_sems.at[n]))
        leaving[-1].start()
    for copy in leaving:
        copy.wait()


def pack(embeddings, cluster, rank, ks, sizes):
    groups, halves, half, cap, blk = sizes
    rows, width = embeddings.shape
    hbm = pl.BlockSpec(memory_space=pltpu.HBM)
    out_shape = [jax.ShapeDtypeStruct((1, rows), jnp.int32)]
    out_shape += [jax.ShapeDtypeStruct((blk + LABEL_ROWS, width), jnp.bfloat16)] * len(ks)
    return pl.pallas_call(
        functools.partial(pack_kernel, sizes, ks),
        out_shape=out_shape,
        in_specs=[hbm, hbm, hbm],
        out_specs=[pl.BlockSpec(memory_space=pltpu.VMEM)] + [hbm] * len(ks),
        scratch_shapes=[
            pltpu.VMEM((rows, width), jnp.bfloat16),
            pltpu.VMEM((1, rows), jnp.int32),
            pltpu.VMEM((1, rows), jnp.int32),
            pltpu.VMEM((len(ks), blk + LABEL_ROWS, width), jnp.bfloat16),
            pltpu.SemaphoreType.DMA((2 + rows // 256,)),
            pltpu.SemaphoreType.DMA((len(ks),)),
        ],
        compiler_params=pltpu.CompilerParams(vmem_limit_bytes=PACK_VMEM),
        cost_estimate=pl.CostEstimate(
            flops=2 * len(ks) * blk * rows * width, bytes_accessed=4 * rows * width, transcendentals=0
        ),
    )(embeddings, cluster.reshape(1, rows), rank.reshape(1, rows))


def compare_kernel(sizes, jobs, names, spots, joined, has_prev, *refs):
    groups, halves, half, cap, blk = sizes
    array = dict(zip(names, refs))
    refs = refs[len(names) :]
    block = {piece: (array[name], at * (blk + LABEL_ROWS)) for piece, (name, at) in spots.items()}
    prev = None
    if has_prev:
        prev, refs = refs[0], refs[1:]
    outs, (key_col, key_row, low_row, turned, best) = refs[:-5], refs[-5:]
    rows = groups * blk
    per_tile = blk // TILES
    tile = rows // TILES
    cap_all = float(halves * half)

    lane = lax.broadcasted_iota(jnp.int32, (LABEL_ROWS, tile), 1)
    line = lax.broadcasted_iota(jnp.int32, (LABEL_ROWS, tile), 0)
    from_block = lax.div(lane, per_tile)
    which = line * (halves // TILES) + lax.div(lane - from_block * per_tile, cap)
    weight_row = lax.broadcasted_iota(jnp.int32, (LABEL_ROWS, 128), 0)
    weights = jnp.where(
        weight_row == 0,
        1.0,
        jnp.where(weight_row == 1, cap_all, jnp.where(weight_row == 2, float(half), 0.0)),
    ).astype(jnp.bfloat16)
    needed = sorted({piece for _, pieces in jobs for piece in pieces})
    key_at = {piece: n * blk for n, piece in enumerate(needed)}

    def label_of(piece):
        ref, base = block[piece]
        return ref[base + blk : base + blk + LABEL_ROWS, :]

    for piece in needed:
        key_col[pl.ds(key_at[piece], blk), :] = lax.dot_general(
            label_of(piece)[:, 0:blk], weights, TN, preferred_element_type=jnp.float32
        )
    for o, (a, _) in enumerate(jobs):
        rest = jnp.zeros((LABEL_ROWS, tile), jnp.float32)
        code = jnp.zeros((LABEL_ROWS, tile), jnp.float32)
        for k in range(groups):
            label = label_of((a, k))[:, tile : 3 * tile].astype(jnp.float32)
            rest = jnp.where(from_block == k, label[:, :tile], rest)
            code = jnp.where(from_block == k, label[:, tile:], code)
        low = code * cap_all
        key = low + (which * half).astype(jnp.float32) + rest
        low = jnp.where(code > 0.5, low, FAR)
        key_row[o] = key[0:8]
        low_row[o] = low[0:8]

    def rows_of(ref, base, first, last):
        return ref[base + first * per_tile : base + last * per_tile, :]

    best[...] = prev[...] if has_prev else jnp.full(best.shape, -1.0, jnp.float32)
    for o, (a, pieces) in enumerate(jobs):
        for t in range(TILES):
            turned[o, t] = jnp.concatenate(
                [rows_of(*block[a, k], t, t + 1) for k in range(groups)], axis=0
            ).T
            mine = key_row[o, t : t + 1, :]
            floor = low_row[o, t : t + 1, :]
            acc = jnp.full((8, tile), -1.0, jnp.float32)
            for at in range(0, len(pieces), groups):
                some = pieces[at : at + groups]
                theirs = [rows_of(key_col, key_at[piece], 0, t + 1) for piece in some]
                theirs = jnp.concatenate(theirs, axis=0)
                theirs = jnp.concatenate([theirs] * (tile // 128), axis=1)
                sims = jnp.dot(
                    jnp.concatenate([rows_of(*block[piece], 0, t + 1) for piece in some], axis=0),
                    turned[o, t],
                    preferred_element_type=jnp.float32,
                )
                keep = (theirs >= floor) & (theirs < mine)
                sims = jnp.where(keep, sims, -1.0)
                top = jnp.max(sims.reshape(sims.shape[0] // 8, 8, tile), axis=0)
                acc = jnp.maximum(acc, top)
            best[a, t : t + 1, :] = jnp.maximum(
                best[a, t : t + 1, :], jnp.max(acc, axis=0, keepdims=True)
            )

    if not has_prev:
        outs[0][...] = best[...]
        return
    lane = lax.broadcasted_iota(jnp.int32, (1, tile), 1)
    side = halves // 2 // groups
    here = lax.axis_index("mem")
    for o, (a, _) in enumerate(jobs):
        found = best[a]
        for k in range(groups):
            total = jnp.full((1, tile), -1.0, jnp.float32)
            for t in range(TILES):
                turn = ((t - k) * per_tile) % tile
                moved = pltpu.roll(found, turn, 1) if turn else found
                total = jnp.where(lax.div(lane, per_tile) == t, moved[t : t + 1], total)
            at = (here // side) ^ k
            if joined:
                outs[0][pl.ds(at * joined + ((here % side) ^ a), 1), 0, :] = total[:, :blk]
            else:
                outs[o][pl.ds(at, 1), 0, :] = total[:, :blk]


def compare(blocks, jobs, prev, joined, n_sets, sizes):
    groups, halves, half, cap, blk = sizes
    used = {piece for _, pieces in jobs for piece in pieces}
    used |= {(a, k) for a, _ in jobs for k in range(groups)}
    spots = {}
    arrays = {}
    for piece in sorted(used):
        value, at = blocks[piece]
        name = next((n for n, v in arrays.items() if v is value), None)
        if name is None:
            name = len(arrays)
            arrays[name] = value
        spots[piece] = (name, at)
    names = list(arrays)
    width = arrays[0].shape[1]
    tile = groups * blk // TILES
    vmem = pl.BlockSpec(memory_space=pltpu.VMEM)
    steps = TILES * (TILES + 1) // 2
    work = sum(len(pieces) for _, pieces in jobs) * steps * (blk // TILES) * tile * width
    if prev is None:
        out_shape = [jax.ShapeDtypeStruct((n_sets, 8, tile), jnp.float32)]
    elif joined:
        out_shape = [jax.ShapeDtypeStruct((groups * joined, 1, blk), jnp.float32)]
    else:
        out_shape = [jax.ShapeDtypeStruct((groups, 1, blk), jnp.float32)] * len(jobs)
    operands = list(arrays.values()) + ([] if prev is None else [prev])
    needed = {piece for _, pieces in jobs for piece in pieces}
    return pl.pallas_call(
        functools.partial(compare_kernel, sizes, jobs, names, spots, joined, prev is not None),
        out_shape=out_shape,
        in_specs=[vmem] * len(operands),
        out_specs=[vmem] * len(out_shape),
        scratch_shapes=[
            pltpu.VMEM((len(needed) * blk, 128), jnp.float32),
            pltpu.VMEM((len(jobs), 8, tile), jnp.float32),
            pltpu.VMEM((len(jobs), 8, tile), jnp.float32),
            pltpu.VMEM((len(jobs), TILES, width, tile), jnp.bfloat16),
            pltpu.VMEM((n_sets, 8, tile), jnp.float32),
        ],
        compiler_params=pltpu.CompilerParams(vmem_limit_bytes=COMPARE_VMEM),
        cost_estimate=pl.CostEstimate(
            flops=2 * work, bytes_accessed=2 * len(used) * blk * width, transcendentals=0
        ),
    )(*operands)


def join_kernel(*refs):
    out_ref, at = refs[-1], 0
    for ref in refs[:-1]:
        out_ref[at : at + ref.shape[0], :] = ref[...]
        at += ref.shape[0]


def join(pieces):
    if len(pieces) == 1:
        return pieces[0]
    rows = sum(piece.shape[0] for piece in pieces)
    vmem = pl.BlockSpec(memory_space=pltpu.VMEM)
    return pl.pallas_call(
        join_kernel,
        out_shape=jax.ShapeDtypeStruct((rows, pieces[0].shape[1]), pieces[0].dtype),
        in_specs=[vmem] * len(pieces),
        out_specs=vmem,
        compiler_params=pltpu.CompilerParams(vmem_limit_bytes=COMPARE_VMEM),
        cost_estimate=pl.CostEstimate(flops=JOIN_FLOPS, bytes_accessed=0, transcendentals=0),
    )(*pieces)


def unpack_kernel(sizes, dest_ref, back_ref, out_ref):
    groups, halves, half, cap, blk = sizes
    side = back_ref.shape[0] // groups
    rows = dest_ref.shape[1]
    dest = dest_ref[...]
    slot = lax.broadcasted_iota(jnp.int32, (blk, rows), 0)
    field = lax.broadcasted_iota(jnp.int32, (LABEL_ROWS, blk), 0)
    total = jnp.zeros((LABEL_ROWS, rows), jnp.float32)
    for k in range(groups):
        value = back_ref[k * side]
        for more in range(1, side):
            value = jnp.maximum(value, back_ref[k * side + more])
        top = value.astype(jnp.bfloat16).astype(jnp.float32)
        rest = value - top
        mid = rest.astype(jnp.bfloat16).astype(jnp.float32)
        low = rest - mid
        stack = jnp.where(field == 0, top, jnp.where(field == 1, mid, jnp.where(field == 2, low, 0.0)))
        pick = (slot + k * blk == dest).astype(jnp.float32).astype(jnp.bfloat16)
        total = total + jnp.dot(stack.astype(jnp.bfloat16), pick, preferred_element_type=jnp.float32)
    value = (total[0:1] + total[1:2]) + total[2:3]
    out_ref[...] = jnp.where(dest >= 0, value, -1.0)


def unpack(dest, back, sizes):
    vmem = pl.BlockSpec(memory_space=pltpu.VMEM)
    return pl.pallas_call(
        functools.partial(unpack_kernel, sizes),
        out_shape=jax.ShapeDtypeStruct(dest.shape, jnp.float32),
        in_specs=[vmem] * 2,
        out_specs=vmem,
        compiler_params=pltpu.CompilerParams(vmem_limit_bytes=COMPARE_VMEM),
    )(dest, back)


def on_device(embeddings, cluster, rank):
    rows_dev, width = embeddings.shape
    groups = lax.axis_size("grp")
    members = lax.axis_size("mem")
    devices = groups * members
    halves = 2 * members
    half = rows_dev // CLUS_GRP // 2
    blk = rows_dev // groups
    cap = blk // halves
    sizes = (groups, halves, half, cap, blk)
    side = members // groups

    def swap(value, block_step, member_step):
        mask = member_step // side * members + block_step * side + member_step % side
        if mask == 0:
            return value
        return lax.ppermute(value, ("grp", "mem"), [(i, i ^ mask) for i in range(devices)])

    offsets, pairs = cover(members)
    sends = [None] * groups
    first = (1,)
    dest, *packed = pack(embeddings, cluster, rank, first, sizes)
    for k, value in zip(first, packed):
        sends[k] = value
    rest = (2, 0, *range(3, groups))
    cluster, dest = lax.optimization_barrier((cluster, dest))
    _, *packed = pack(embeddings, cluster, rank, rest, sizes)
    for k, value in zip(rest, packed):
        sends[k] = value

    last = groups - 1
    across = {0: side}
    across.update({d: d ^ side for d in offsets if d & side == 0 and d and d ^ side in offsets})
    near = [d for d in offsets[1:] if d not in across.values()]

    held = {d: [] for d in [0, *near]}
    for k in range(groups):
        send = sends[k]
        if k > 2:
            send, held[0][k - 2] = lax.optimization_barrier((send, held[0][k - 2]))
        held[0].append(swap(send, k, 0))
    for k in range(groups):
        for d in near:
            piece = held[0][k]
            if k == 1:
                piece, held[d][0] = lax.optimization_barrier((piece, held[d][0]))
            elif k == 2:
                piece, *values = lax.optimization_barrier((piece, *(held[e][1] for e in near)))
                for e, value in zip(near, values):
                    held[e][1] = value
            held[d].append(swap(piece, 0, d))
    index = {d: i for i, d in enumerate(offsets)}
    blocks = {(index[d], k): (piece, 0) for d in held for k, piece in enumerate(held[d])}

    def cross(wanted, after):
        pieces = [held[d][k] for d, k in wanted]
        pieces[0], *after = lax.optimization_barrier((pieces[0], *after))
        moved = swap(join(pieces), 0, side)
        for at, (d, k) in enumerate(wanted):
            blocks[index[across[d]], k] = (moved, at)
        return after

    for d in across:
        cross([(d, k) for k in range(last - 1)], [])
    starts = sorted({a for a, _ in pairs.values()})
    early, late = [], []
    for a in starts:
        cols = [index[b] for _, (e, b) in sorted(pairs.items()) if e == a]
        pieces = [(b, k) for b in cols for k in range(groups)]
        if a == 0:
            ready = {(0, last)} | {(index[d], k) for d in held for k in range(last)}
            ready |= {(index[d], k) for d in across.values() for k in range(last - 1)}
            early.append((0, [piece for piece in pieces if piece in ready]))
            pieces = [piece for piece in pieces if piece not in ready]
        late.append((index[a], pieces))
    joined = side if all(a < side for a in starts) else 0
    prev = compare(blocks, early, None, 0, len(offsets), sizes)[0]
    for d, k in [(0, last - 1), (0, last)] + [
        (d, k) for k in (last - 1, last) for d in across if d
    ]:
        (prev,) = cross([(d, k)], [prev])
    found = compare(blocks, late, prev, joined, len(offsets), sizes)
    if joined:
        back = found[0]
    else:
        best = {}
        for a, value in zip(starts, found):
            near = a % side
            value = swap(value, 0, a - near)
            best[near] = jnp.maximum(best[near], value) if near in best else value
        none = jnp.full_like(found[0], -1.0)
        near_of = [best.get(near, none) for near in range(side)]
        rows_of = []
        for spot in range(side):
            value = near_of[spot]
            for mine in range(1, side):
                value = jnp.where(lax.axis_index("mem") % side == mine, near_of[spot ^ mine], value)
            rows_of.append(value)
        back = jnp.stack(rows_of, axis=1).reshape(groups * side, 1, blk)
    back = lax.all_to_all(back, "mem", split_axis=0, concat_axis=0, tiled=True)
    return unpack(dest, back, sizes).reshape(rows_dev)


def solution(mesh):
    in_specs = (P(("grp", "mem"), None), P(("grp", "mem")), P(("grp", "mem")))
    out_specs = P(("grp", "mem"))
    return jax.shard_map(
        on_device, mesh=mesh, in_specs=in_specs, out_specs=out_specs, check_vma=False
    )
```

```python
import functools

import jax
import jax.numpy as jnp
from jax import lax
from jax.experimental import pallas as pl
from jax.experimental.pallas import tpu as pltpu
from jax.sharding import PartitionSpec as P

CLUS_GRP = 2
TILES = 4
LABEL_ROWS = 16
FAR = 1.0e9
PACK_VMEM = 60 * 1024 * 1024
COMPARE_VMEM = 24 * 1024 * 1024
NT = (((1,), (1,)), ((), ()))
TN = (((0,), (0,)), ((), ()))


def cover(members):
    bits = [1 << i for i in range(members.bit_length() - 1)]
    offsets = [0] + bits

    def missing(held):
        return set(range(members)) - {a ^ b for a in held for b in held}

    while missing(offsets):
        offsets.append(
            min(
                (d for d in range(members) if d not in offsets),
                key=lambda d: (len(missing(offsets + [d])), bin(d).count("1"), -d),
            )
        )
    pairs = {}
    for delta in range(members):
        pairs[delta] = min(
            (a, a ^ delta) for a in offsets if a ^ delta in offsets
        )
    return offsets, pairs


def pack_kernel(sizes, ks, labelled, emb_hbm, cluster_hbm, rank_hbm, *refs):
    groups, halves, half, cap, blk = sizes
    outs, refs = refs[: len(ks)], refs[len(ks) :]
    if labelled:
        dest_ref, key_ref, *refs = refs
    emb_ref, cluster_ref, rank_ref, stage, sems, out_sems = refs
    rows = emb_ref.shape[0]
    step = 256
    loads = [
        pltpu.make_async_copy(cluster_hbm, cluster_ref, sems.at[0]),
        pltpu.make_async_copy(rank_hbm, rank_ref, sems.at[1]),
    ]
    for j in range(rows // step):
        at = pl.ds(j * step, step)
        loads.append(pltpu.make_async_copy(emb_hbm.at[at], emb_ref.at[at], sems.at[2 + j]))
    for load in loads:
        load.start()
    for load in loads[:2]:
        load.wait()
    cluster = cluster_ref[...]
    rank = rank_ref[...]
    alive = cluster >= 0
    pair = lax.shift_right_logical(jnp.maximum(cluster, 0), 1)
    parity = jnp.maximum(cluster, 0) - 2 * pair
    safe_rank = jnp.maximum(rank, 0)
    which = safe_rank // half
    units = groups * halves
    unit_id = jnp.where(alive, pair * halves + which, -1)
    before_rows = lax.broadcasted_iota(jnp.int32, (step, step), 0)
    before_cols = lax.broadcasted_iota(jnp.int32, (step, step), 1)
    upper = (before_rows < before_cols).astype(jnp.float32).astype(jnp.bfloat16)
    unit_iota = lax.broadcasted_iota(jnp.int32, (units, step), 0)
    carry = jnp.zeros((units, 1), jnp.float32)
    places = []
    for j in range(rows // step):
        mine = unit_id[:, j * step : (j + 1) * step]
        hit = (unit_iota == mine).astype(jnp.float32)
        before = jnp.dot(hit.astype(jnp.bfloat16), upper, preferred_element_type=jnp.float32) + carry
        position = jnp.sum(hit * before, axis=0, keepdims=True)
        carry = carry + jnp.sum(hit, axis=1, keepdims=True)
        places.append(jnp.where(mine >= 0, mine * cap + position.astype(jnp.int32), -1))
    dest = jnp.concatenate(places, axis=1)
    if labelled:
        dest_ref[...] = dest
    members = halves // 2
    side = members // groups
    here = lax.axis_index("mem") // side
    dest = jnp.where(dest >= 0, dest ^ (here * blk), -1)

    units_of = []
    for j in range(rows // step):
        loads[2 + j].wait()
        wide = emb_ref[j * step : (j + 1) * step, :].astype(jnp.float32)
        total = jnp.sum(wide * wide, axis=1, keepdims=True)
        units_of.append((wide * lax.rsqrt(total + 1e-06)).astype(jnp.bfloat16))
    unit = jnp.concatenate(units_of, axis=0)

    field = lax.broadcasted_iota(jnp.int32, (LABEL_ROWS, rows), 0)
    labels = jnp.where(
        field == 0, safe_rank - which * half, jnp.where(field == 1, parity + 1, 0)
    )
    labels = jnp.where(alive, labels, 0).astype(jnp.float32).astype(jnp.bfloat16)
    unit_of = lax.div(lax.broadcasted_iota(jnp.int32, (1, blk), 1), cap).astype(jnp.float32)
    slot = lax.broadcasted_iota(jnp.int32, (blk, rows), 0)
    leaving = []
    for k in (*ks, *(k for k in range(groups) if labelled and k not in ks)):
        pick = (slot + k * blk == dest).astype(jnp.float32).astype(jnp.bfloat16)
        if labelled:
            mine = lax.dot_general(labels, pick, NT, preferred_element_type=jnp.float32)
            key = mine[0:1] + float(half) * unit_of + float(halves * half) * mine[1:2]
            for p in range(groups):
                for y in range(side):
                    key_ref[pl.ds(p * members + (here ^ k) * side + y, 1), :] = key
        if k in ks:
            n = ks.index(k)
            stage[n] = jnp.dot(pick, unit, preferred_element_type=jnp.float32).astype(jnp.bfloat16)
            leaving.append(pltpu.make_async_copy(stage.at[n], outs[n], out_sems.at[n]))
            leaving[-1].start()
    for copy in leaving:
        copy.wait()


def pack(embeddings, cluster, rank, ks, labelled, sizes):
    groups, halves, half, cap, blk = sizes
    rows, width = embeddings.shape
    hbm = pl.BlockSpec(memory_space=pltpu.HBM)
    vmem = pl.BlockSpec(memory_space=pltpu.VMEM)
    out_shape = [jax.ShapeDtypeStruct((blk, width), jnp.bfloat16)] * len(ks)
    out_specs = [hbm] * len(ks)
    if labelled:
        out_shape.append(jax.ShapeDtypeStruct((1, rows), jnp.int32))
        out_shape.append(jax.ShapeDtypeStruct((groups * halves // 2, blk), jnp.float32))
        out_specs += [vmem, vmem]
    return pl.pallas_call(
        functools.partial(pack_kernel, sizes, ks, labelled),
        out_shape=out_shape,
        in_specs=[hbm, hbm, hbm],
        out_specs=out_specs,
        scratch_shapes=[
            pltpu.VMEM((rows, width), jnp.bfloat16),
            pltpu.VMEM((1, rows), jnp.int32),
            pltpu.VMEM((1, rows), jnp.int32),
            pltpu.VMEM((len(ks), blk, width), jnp.bfloat16),
            pltpu.SemaphoreType.DMA((2 + rows // 256,)),
            pltpu.SemaphoreType.DMA((len(ks),)),
        ],
        compiler_params=pltpu.CompilerParams(vmem_limit_bytes=PACK_VMEM),
        cost_estimate=pl.CostEstimate(
            flops=2 * len(ks) * blk * rows * width, bytes_accessed=4 * rows * width, transcendentals=0
        ),
    )(embeddings, cluster.reshape(1, rows), rank.reshape(1, rows))


def compare_kernel(sizes, jobs, names, spots, offsets, joined, has_prev, label_ref, *refs):
    groups, halves, half, cap, blk = sizes
    array = dict(zip(names, refs))
    refs = refs[len(names) :]
    block = {piece: (array[name], at * blk) for piece, (name, at) in spots.items()}
    prev = None
    if has_prev:
        prev, refs = refs[0], refs[1:]
    outs, (key_col, key_row, low_row, turned, best) = refs[:-5], refs[-5:]
    rows = groups * blk
    per_tile = blk // TILES
    tile = rows // TILES
    cap_all = float(halves * half)

    members = halves // 2
    side = members // groups
    across, along = lax.axis_index("grp"), lax.axis_index("mem")

    def keys_of(piece):
        i, k = piece
        row = (across ^ (offsets[i] // side)) * members
        row += ((along // side) ^ k) * side + ((along % side) ^ (offsets[i] % side))
        return label_ref[pl.ds(row, 1), :]

    weight_row = lax.broadcasted_iota(jnp.int32, (LABEL_ROWS, 128), 0)
    weights = jnp.where(weight_row == 0, 1.0, jnp.where(weight_row == 1, float(half), 0.0))
    weights = weights.astype(jnp.bfloat16)
    field = lax.broadcasted_iota(jnp.int32, (LABEL_ROWS, blk), 0)
    needed = sorted({piece for _, pieces in jobs for piece in pieces})
    key_at = {piece: n * blk for n, piece in enumerate(needed)}
    for piece in needed:
        key = keys_of(piece)
        high = jnp.floor(key * (1.0 / half))
        split = jnp.where(field == 0, key - high * half, jnp.where(field == 1, high, 0.0))
        key_col[pl.ds(key_at[piece], blk), :] = lax.dot_general(
            split.astype(jnp.bfloat16), weights, TN, preferred_element_type=jnp.float32
        )
    lane = lax.div(lax.broadcasted_iota(jnp.int32, (1, tile), 1), per_tile)
    for o, (a, _) in enumerate(jobs):
        keys = [keys_of((a, k)) for k in range(groups)]
        keys = [jnp.concatenate([key] * (tile // blk), axis=1) for key in keys]
        for t in range(TILES):
            line = jnp.zeros((1, tile), jnp.float32)
            for k in range(groups):
                turn = ((k - t) * per_tile) % tile
                moved = pltpu.roll(keys[k], turn, 1) if turn else keys[k]
                line = jnp.where(lane == k, moved, line)
            low = jnp.floor(line * (1.0 / cap_all)) * cap_all
            key_row[o, t : t + 1, :] = line
            low_row[o, t : t + 1, :] = jnp.where(low > 0.5, low, FAR)

    def rows_of(ref, base, first, last):
        return ref[base + first * per_tile : base + last * per_tile, :]

    best[...] = prev[...] if has_prev else jnp.full(best.shape, -1.0, jnp.float32)
    for o, (a, pieces) in enumerate(jobs):
        for t in range(TILES):
            turned[o, t] = jnp.concatenate(
                [rows_of(*block[a, k], t, t + 1) for k in range(groups)], axis=0
            ).T
            mine = key_row[o, t : t + 1, :]
            floor = low_row[o, t : t + 1, :]
            acc = jnp.full((8, tile), -1.0, jnp.float32)
            for at in range(0, len(pieces), groups):
                some = pieces[at : at + groups]
                theirs = [rows_of(key_col, key_at[piece], 0, t + 1) for piece in some]
                theirs = jnp.concatenate(theirs, axis=0)
                theirs = jnp.concatenate([theirs] * (tile // 128), axis=1)
                sims = jnp.dot(
                    jnp.concatenate([rows_of(*block[piece], 0, t + 1) for piece in some], axis=0),
                    turned[o, t],
                    preferred_element_type=jnp.float32,
                )
                keep = (theirs >= floor) & (theirs < mine)
                sims = jnp.where(keep, sims, -1.0)
                top = jnp.max(sims.reshape(sims.shape[0] // 8, 8, tile), axis=0)
                acc = jnp.maximum(acc, top)
            best[a, t : t + 1, :] = jnp.maximum(
                best[a, t : t + 1, :], jnp.max(acc, axis=0, keepdims=True)
            )

    if not has_prev:
        outs[0][...] = best[...]
        return
    for o, (a, _) in enumerate(jobs):
        found = best[a]
        for k in range(groups):
            total = jnp.full((1, tile), -1.0, jnp.float32)
            for t in range(TILES):
                turn = ((t - k) * per_tile) % tile
                moved = pltpu.roll(found, turn, 1) if turn else found
                total = jnp.where(lane == t, moved[t : t + 1], total)
            at = (along // side) ^ k
            if joined:
                outs[0][pl.ds(at * joined + ((along % side) ^ a), 1), 0, :] = total[:, :blk]
            else:
                outs[o][pl.ds(at, 1), 0, :] = total[:, :blk]


def compare(labels, blocks, jobs, prev, joined, offsets, sizes):
    groups, halves, half, cap, blk = sizes
    n_sets = len(offsets)
    used = {piece for _, pieces in jobs for piece in pieces}
    used |= {(a, k) for a, _ in jobs for k in range(groups)}
    spots = {}
    arrays = {}
    for piece in sorted(used):
        value, at = blocks[piece]
        name = next((n for n, v in arrays.items() if v is value), None)
        if name is None:
            name = len(arrays)
            arrays[name] = value
        spots[piece] = (name, at)
    names = list(arrays)
    width = arrays[0].shape[1]
    tile = groups * blk // TILES
    vmem = pl.BlockSpec(memory_space=pltpu.VMEM)
    steps = TILES * (TILES + 1) // 2
    work = sum(len(pieces) for _, pieces in jobs) * steps * (blk // TILES) * tile * width
    if prev is None:
        out_shape = [jax.ShapeDtypeStruct((n_sets, 8, tile), jnp.float32)]
    elif joined:
        out_shape = [jax.ShapeDtypeStruct((groups * joined, 1, blk), jnp.float32)]
    else:
        out_shape = [jax.ShapeDtypeStruct((groups, 1, blk), jnp.float32)] * len(jobs)
    operands = [labels] + list(arrays.values()) + ([] if prev is None else [prev])
    needed = {piece for _, pieces in jobs for piece in pieces}
    return pl.pallas_call(
        functools.partial(
            compare_kernel, sizes, jobs, names, spots, offsets, joined, prev is not None
        ),
        out_shape=out_shape,
        in_specs=[vmem] * len(operands),
        out_specs=[vmem] * len(out_shape),
        scratch_shapes=[
            pltpu.VMEM((len(needed) * blk, 128), jnp.float32),
            pltpu.VMEM((len(jobs), 8, tile), jnp.float32),
            pltpu.VMEM((len(jobs), 8, tile), jnp.float32),
            pltpu.VMEM((len(jobs), TILES, width, tile), jnp.bfloat16),
            pltpu.VMEM((n_sets, 8, tile), jnp.float32),
        ],
        compiler_params=pltpu.CompilerParams(vmem_limit_bytes=COMPARE_VMEM),
        cost_estimate=pl.CostEstimate(
            flops=2 * work, bytes_accessed=2 * len(used) * blk * width, transcendentals=0
        ),
    )(*operands)


def join_kernel(first_ref, second_ref, out_ref):
    rows = first_ref.shape[0]
    out_ref[:rows, :] = first_ref[...]
    out_ref[rows:, :] = second_ref[...]


def join(first, second):
    rows, width = first.shape
    vmem = pl.BlockSpec(memory_space=pltpu.VMEM)
    return pl.pallas_call(
        join_kernel,
        out_shape=jax.ShapeDtypeStruct((2 * rows, width), first.dtype),
        in_specs=[vmem, vmem],
        out_specs=vmem,
        compiler_params=pltpu.CompilerParams(vmem_limit_bytes=COMPARE_VMEM),
    )(first, second)


def unpack_kernel(sizes, dest_ref, back_ref, out_ref):
    groups, halves, half, cap, blk = sizes
    side = back_ref.shape[0] // groups
    rows = dest_ref.shape[1]
    dest = dest_ref[...]
    slot = lax.broadcasted_iota(jnp.int32, (blk, rows), 0)
    field = lax.broadcasted_iota(jnp.int32, (LABEL_ROWS, blk), 0)
    total = jnp.zeros((LABEL_ROWS, rows), jnp.float32)
    for k in range(groups):
        value = back_ref[k * side]
        for more in range(1, side):
            value = jnp.maximum(value, back_ref[k * side + more])
        top = value.astype(jnp.bfloat16).astype(jnp.float32)
        rest = value - top
        mid = rest.astype(jnp.bfloat16).astype(jnp.float32)
        low = rest - mid
        stack = jnp.where(field == 0, top, jnp.where(field == 1, mid, jnp.where(field == 2, low, 0.0)))
        pick = (slot + k * blk == dest).astype(jnp.float32).astype(jnp.bfloat16)
        total = total + jnp.dot(stack.astype(jnp.bfloat16), pick, preferred_element_type=jnp.float32)
    value = (total[0:1] + total[1:2]) + total[2:3]
    out_ref[...] = jnp.where(dest >= 0, value, -1.0)


def unpack(dest, back, sizes):
    vmem = pl.BlockSpec(memory_space=pltpu.VMEM)
    return pl.pallas_call(
        functools.partial(unpack_kernel, sizes),
        out_shape=jax.ShapeDtypeStruct(dest.shape, jnp.float32),
        in_specs=[vmem] * 2,
        out_specs=vmem,
        compiler_params=pltpu.CompilerParams(vmem_limit_bytes=COMPARE_VMEM),
    )(dest, back)


def on_device(embeddings, cluster, rank):
    rows_dev, width = embeddings.shape
    groups = lax.axis_size("grp")
    members = lax.axis_size("mem")
    devices = groups * members
    halves = 2 * members
    half = rows_dev // CLUS_GRP // 2
    blk = rows_dev // groups
    cap = blk // halves
    sizes = (groups, halves, half, cap, blk)
    side = members // groups

    def swap(value, block_step, member_step):
        mask = member_step // side * members + block_step * side + member_step % side
        if mask == 0:
            return value
        return lax.ppermute(value, ("grp", "mem"), [(i, i ^ mask) for i in range(devices)])

    offsets, pairs = cover(members)
    sends = [None] * groups
    first = tuple(range(1, min(3, groups)))
    for k, value in zip(first, pack(embeddings, cluster, rank, first, False, sizes)):
        sends[k] = value
    rest = tuple(k for k in range(groups) if k not in first)
    cluster, sends[1] = lax.optimization_barrier((cluster, sends[1]))
    *packed, dest, labels = pack(embeddings, cluster, rank, rest, True, sizes)
    for k, value in zip(rest, packed):
        sends[k] = value
    labels = lax.all_to_all(labels, ("grp", "mem"), split_axis=0, concat_axis=0, tiled=True)

    last = groups - 1
    far = [d for d in offsets if d & side and d != side and d ^ side in offsets]
    near = [d for d in offsets[1:] if d not in far]
    lead = far[0] ^ side if far else near[0]
    held = {0: [sends[0]]}
    for d in near:
        held[d] = [swap(sends[0], 0, d)]
    for d in far:
        held[d] = [swap(held[d ^ side][0], 0, side)]
    after = held[lead][0]
    for k in range(1, groups, 2):
        if k > 1:
            send, after = lax.optimization_barrier((sends[k], after))
        else:
            send = sends[k]
        mine = swap(send, k, 0)
        if k < last:
            also = swap(sends[k + 1], k + 1, 0)
            if k == 1:
                mine, also, labels, *firsts = lax.optimization_barrier(
                    (mine, also, labels, *(held[d][0] for d in near))
                )
                for d, value in zip(near, firsts):
                    held[d] = [value]
            mine = join(mine, also)
            after = mine
        held[0].append(mine)
        for d in near:
            held[d].append(swap(mine, 0, d))
    for spot in range(1, len(held[0]) - 1):
        values = lax.optimization_barrier(
            (held[0][spot + 1], *(held[d][spot] for d in near))
        )
        held[0][spot + 1] = values[0]
        for d, value in zip(near, values[1:]):
            held[d][spot] = value
        for d in far:
            held[d].append(swap(held[d ^ side][spot], 0, side))

    index = {d: i for i, d in enumerate(offsets)}
    blocks = {}

    def note():
        for d in offsets:
            for spot, value in enumerate(held[d]):
                ks = [0] if spot == 0 else [k for k in (2 * spot - 1, 2 * spot) if k < groups]
                for at, k in enumerate(ks):
                    blocks[index[d], k] = (value, at)

    note()
    starts = sorted({a for a, _ in pairs.values()})
    early, late = [], []
    for a in starts:
        cols = [index[b] for _, (e, b) in sorted(pairs.items()) if e == a]
        pieces = [(b, k) for b in cols for k in range(groups)]
        if a == 0:
            soon = [(b, k) for b, k in pieces if b == 0 or k < last]
            early.append((0, soon))
            pieces = [piece for piece in pieces if piece not in soon]
        late.append((index[a], pieces))
    joined = side if all(a < side for a in starts) else 0
    prev = compare(labels, blocks, early, None, 0, offsets, sizes)[0]
    for d in far:
        piece, prev = lax.optimization_barrier((held[d ^ side][-1], prev))
        held[d].append(swap(piece, 0, side))
    note()
    found = compare(labels, blocks, late, prev, joined, offsets, sizes)
    if joined:
        back = found[0]
    else:
        best = {}
        for a, value in zip(starts, found):
            near = a % side
            value = swap(value, 0, a - near)
            best[near] = jnp.maximum(best[near], value) if near in best else value
        none = jnp.full_like(found[0], -1.0)
        near_of = [best.get(near, none) for near in range(side)]
        rows_of = []
        for spot in range(side):
            value = near_of[spot]
            for mine in range(1, side):
                value = jnp.where(lax.axis_index("mem") % side == mine, near_of[spot ^ mine], value)
            rows_of.append(value)
        back = jnp.stack(rows_of, axis=1).reshape(groups * side, 1, blk)
    back = lax.all_to_all(back, "mem", split_axis=0, concat_axis=0, tiled=True)
    return unpack(dest, back, sizes).reshape(rows_dev)


def solution(mesh):
    in_specs = (P(("grp", "mem"), None), P(("grp", "mem")), P(("grp", "mem")))
    out_specs = P(("grp", "mem"))
    return jax.shard_map(
        on_device, mesh=mesh, in_specs=in_specs, out_specs=out_specs, check_vma=False
    )
```

```python
import functools

import jax
import jax.numpy as jnp
from jax import lax
from jax.experimental import pallas as pl
from jax.experimental.pallas import tpu as pltpu
from jax.sharding import PartitionSpec as P

CLUS_GRP = 2
TILES = 4
LABEL_ROWS = 16
FAR = 1.0e9
PACK_VMEM = 60 * 1024 * 1024
COMPARE_VMEM = 24 * 1024 * 1024
NT = (((1,), (1,)), ((), ()))
TN = (((0,), (0,)), ((), ()))


def cover(members):
    bits = [1 << i for i in range(members.bit_length() - 1)]
    offsets = [0] + bits

    def missing(held):
        return set(range(members)) - {a ^ b for a in held for b in held}

    while missing(offsets):
        offsets.append(
            min(
                (d for d in range(members) if d not in offsets),
                key=lambda d: (len(missing(offsets + [d])), bin(d).count("1"), -d),
            )
        )
    pairs = {}
    for delta in range(members):
        pairs[delta] = min(
            (a, a ^ delta) for a in offsets if a ^ delta in offsets
        )
    return offsets, pairs


def pack_kernel(sizes, ks, labelled, emb_hbm, cluster_hbm, rank_hbm, *refs):
    groups, halves, half, cap, blk = sizes
    outs, refs = refs[: len(ks)], refs[len(ks) :]
    if labelled:
        dest_ref, key_ref, *refs = refs
    emb_ref, cluster_ref, rank_ref, stage, sems, out_sems = refs
    rows = emb_ref.shape[0]
    step = 256
    loads = [
        pltpu.make_async_copy(cluster_hbm, cluster_ref, sems.at[0]),
        pltpu.make_async_copy(rank_hbm, rank_ref, sems.at[1]),
    ]
    for j in range(rows // step):
        at = pl.ds(j * step, step)
        loads.append(pltpu.make_async_copy(emb_hbm.at[at], emb_ref.at[at], sems.at[2 + j]))
    for load in loads:
        load.start()
    for load in loads[:2]:
        load.wait()
    cluster = cluster_ref[...]
    rank = rank_ref[...]
    alive = cluster >= 0
    pair = lax.shift_right_logical(jnp.maximum(cluster, 0), 1)
    parity = jnp.maximum(cluster, 0) - 2 * pair
    safe_rank = jnp.maximum(rank, 0)
    which = safe_rank // half
    units = groups * halves
    unit_id = jnp.where(alive, pair * halves + which, -1)
    before_rows = lax.broadcasted_iota(jnp.int32, (step, step), 0)
    before_cols = lax.broadcasted_iota(jnp.int32, (step, step), 1)
    upper = (before_rows < before_cols).astype(jnp.float32).astype(jnp.bfloat16)
    unit_iota = lax.broadcasted_iota(jnp.int32, (units, step), 0)
    carry = jnp.zeros((units, 1), jnp.float32)
    places = []
    for j in range(rows // step):
        mine = unit_id[:, j * step : (j + 1) * step]
        hit = (unit_iota == mine).astype(jnp.float32)
        before = jnp.dot(hit.astype(jnp.bfloat16), upper, preferred_element_type=jnp.float32) + carry
        position = jnp.sum(hit * before, axis=0, keepdims=True)
        carry = carry + jnp.sum(hit, axis=1, keepdims=True)
        places.append(jnp.where(mine >= 0, mine * cap + position.astype(jnp.int32), -1))
    dest = jnp.concatenate(places, axis=1)
    if labelled:
        dest_ref[...] = dest
    members = halves // 2
    side = members // groups
    here = lax.axis_index("mem") // side
    dest = jnp.where(dest >= 0, dest ^ (here * blk), -1)

    units_of = []
    for j in range(rows // step):
        loads[2 + j].wait()
        wide = emb_ref[j * step : (j + 1) * step, :].astype(jnp.float32)
        total = jnp.sum(wide * wide, axis=1, keepdims=True)
        units_of.append((wide * lax.rsqrt(total + 1e-06)).astype(jnp.bfloat16))
    unit = jnp.concatenate(units_of, axis=0)

    field = lax.broadcasted_iota(jnp.int32, (LABEL_ROWS, rows), 0)
    labels = jnp.where(
        field == 0, safe_rank - which * half, jnp.where(field == 1, parity + 1, 0)
    )
    labels = jnp.where(alive, labels, 0).astype(jnp.float32).astype(jnp.bfloat16)
    unit_of = lax.div(lax.broadcasted_iota(jnp.int32, (1, blk), 1), cap).astype(jnp.float32)
    slot = lax.broadcasted_iota(jnp.int32, (blk, rows), 0)
    leaving = []
    for k in (*ks, *(k for k in range(groups) if labelled and k not in ks)):
        pick = (slot + k * blk == dest).astype(jnp.float32).astype(jnp.bfloat16)
        if labelled:
            mine = lax.dot_general(labels, pick, NT, preferred_element_type=jnp.float32)
            key = mine[0:1] + float(half) * unit_of + float(halves * half) * mine[1:2]
            for p in range(groups):
                for y in range(side):
                    key_ref[pl.ds(p * members + (here ^ k) * side + y, 1), 0, :] = key
        if k in ks:
            n = ks.index(k)
            stage[n] = jnp.dot(pick, unit, preferred_element_type=jnp.float32).astype(jnp.bfloat16)
            leaving.append(pltpu.make_async_copy(stage.at[n], outs[n], out_sems.at[n]))
            leaving[-1].start()
    for copy in leaving:
        copy.wait()


def pack(embeddings, cluster, rank, ks, labelled, sizes):
    groups, halves, half, cap, blk = sizes
    rows, width = embeddings.shape
    hbm = pl.BlockSpec(memory_space=pltpu.HBM)
    vmem = pl.BlockSpec(memory_space=pltpu.VMEM)
    out_shape = [jax.ShapeDtypeStruct((blk, width), jnp.bfloat16)] * len(ks)
    out_specs = [hbm] * len(ks)
    if labelled:
        out_shape.append(jax.ShapeDtypeStruct((1, rows), jnp.int32))
        out_shape.append(jax.ShapeDtypeStruct((groups * halves // 2, 1, blk), jnp.float32))
        out_specs += [vmem, vmem]
    return pl.pallas_call(
        functools.partial(pack_kernel, sizes, ks, labelled),
        out_shape=out_shape,
        in_specs=[hbm, hbm, hbm],
        out_specs=out_specs,
        scratch_shapes=[
            pltpu.VMEM((rows, width), jnp.bfloat16),
            pltpu.VMEM((1, rows), jnp.int32),
            pltpu.VMEM((1, rows), jnp.int32),
            pltpu.VMEM((len(ks), blk, width), jnp.bfloat16),
            pltpu.SemaphoreType.DMA((2 + rows // 256,)),
            pltpu.SemaphoreType.DMA((len(ks),)),
        ],
        compiler_params=pltpu.CompilerParams(vmem_limit_bytes=PACK_VMEM),
        cost_estimate=pl.CostEstimate(
            flops=2 * len(ks) * blk * rows * width, bytes_accessed=4 * rows * width, transcendentals=0
        ),
    )(embeddings, cluster.reshape(1, rows), rank.reshape(1, rows))


def compare_kernel(sizes, jobs, names, spots, offsets, joined, has_prev, label_ref, *refs):
    groups, halves, half, cap, blk = sizes
    array = dict(zip(names, refs))
    refs = refs[len(names) :]
    block = {piece: (array[name], at * blk) for piece, (name, at) in spots.items()}
    prev = None
    if has_prev:
        prev, refs = refs[0], refs[1:]
    outs, (key_col, key_row, low_row, turned, best) = refs[:-5], refs[-5:]
    rows = groups * blk
    per_tile = blk // TILES
    tile = rows // TILES
    cap_all = float(halves * half)

    members = halves // 2
    side = members // groups
    across, along = lax.axis_index("grp"), lax.axis_index("mem")

    def keys_of(piece):
        i, k = piece
        row = (across ^ (offsets[i] // side)) * members
        row += ((along // side) ^ k) * side + ((along % side) ^ (offsets[i] % side))
        return label_ref[pl.ds(row, 1), 0, :]

    weight_row = lax.broadcasted_iota(jnp.int32, (LABEL_ROWS, 128), 0)
    weights = jnp.where(weight_row == 0, 1.0, jnp.where(weight_row == 1, float(half), 0.0))
    weights = weights.astype(jnp.bfloat16)
    field = lax.broadcasted_iota(jnp.int32, (LABEL_ROWS, blk), 0)
    needed = sorted({piece for _, pieces in jobs for piece in pieces})
    key_at = {piece: n * blk for n, piece in enumerate(needed)}
    for piece in needed:
        key = keys_of(piece)
        high = jnp.floor(key * (1.0 / half))
        split = jnp.where(field == 0, key - high * half, jnp.where(field == 1, high, 0.0))
        key_col[pl.ds(key_at[piece], blk), :] = lax.dot_general(
            split.astype(jnp.bfloat16), weights, TN, preferred_element_type=jnp.float32
        )
    lane = lax.div(lax.broadcasted_iota(jnp.int32, (1, tile), 1), per_tile)
    for o, (a, _) in enumerate(jobs):
        keys = [keys_of((a, k)) for k in range(groups)]
        keys = [jnp.concatenate([key] * (tile // blk), axis=1) for key in keys]
        for t in range(TILES):
            line = jnp.zeros((1, tile), jnp.float32)
            for k in range(groups):
                turn = ((k - t) * per_tile) % tile
                moved = pltpu.roll(keys[k], turn, 1) if turn else keys[k]
                line = jnp.where(lane == k, moved, line)
            low = jnp.floor(line * (1.0 / cap_all)) * cap_all
            key_row[o, t : t + 1, :] = line
            low_row[o, t : t + 1, :] = jnp.where(low > 0.5, low, FAR)

    def rows_of(ref, base, first, last):
        return ref[base + first * per_tile : base + last * per_tile, :]

    best[...] = prev[...] if has_prev else jnp.full(best.shape, -1.0, jnp.float32)
    for o, (a, pieces) in enumerate(jobs):
        for t in range(TILES):
            turned[o, t] = jnp.concatenate(
                [rows_of(*block[a, k], t, t + 1) for k in range(groups)], axis=0
            ).T
            mine = key_row[o, t : t + 1, :]
            floor = low_row[o, t : t + 1, :]
            acc = jnp.full((8, tile), -1.0, jnp.float32)
            for at in range(0, len(pieces), groups):
                some = pieces[at : at + groups]
                theirs = [rows_of(key_col, key_at[piece], 0, t + 1) for piece in some]
                theirs = jnp.concatenate(theirs, axis=0)
                theirs = jnp.concatenate([theirs] * (tile // 128), axis=1)
                sims = jnp.dot(
                    jnp.concatenate([rows_of(*block[piece], 0, t + 1) for piece in some], axis=0),
                    turned[o, t],
                    preferred_element_type=jnp.float32,
                )
                keep = (theirs >= floor) & (theirs < mine)
                sims = jnp.where(keep, sims, -1.0)
                top = jnp.max(sims.reshape(sims.shape[0] // 8, 8, tile), axis=0)
                acc = jnp.maximum(acc, top)
            best[a, t : t + 1, :] = jnp.maximum(
                best[a, t : t + 1, :], jnp.max(acc, axis=0, keepdims=True)
            )

    if not has_prev:
        outs[0][...] = best[...]
        return
    for o, (a, _) in enumerate(jobs):
        found = best[a]
        for k in range(groups):
            total = jnp.full((1, tile), -1.0, jnp.float32)
            for t in range(TILES):
                turn = ((t - k) * per_tile) % tile
                moved = pltpu.roll(found, turn, 1) if turn else found
                total = jnp.where(lane == t, moved[t : t + 1], total)
            at = (along // side) ^ k
            if joined:
                outs[0][pl.ds(at * joined + ((along % side) ^ a), 1), 0, :] = total[:, :blk]
            else:
                outs[o][pl.ds(at, 1), 0, :] = total[:, :blk]


def compare(labels, blocks, jobs, prev, joined, offsets, sizes):
    groups, halves, half, cap, blk = sizes
    n_sets = len(offsets)
    used = {piece for _, pieces in jobs for piece in pieces}
    used |= {(a, k) for a, _ in jobs for k in range(groups)}
    spots = {}
    arrays = {}
    for piece in sorted(used):
        value, at = blocks[piece]
        name = next((n for n, v in arrays.items() if v is value), None)
        if name is None:
            name = len(arrays)
            arrays[name] = value
        spots[piece] = (name, at)
    names = list(arrays)
    width = arrays[0].shape[1]
    tile = groups * blk // TILES
    vmem = pl.BlockSpec(memory_space=pltpu.VMEM)
    steps = TILES * (TILES + 1) // 2
    work = sum(len(pieces) for _, pieces in jobs) * steps * (blk // TILES) * tile * width
    if prev is None:
        out_shape = [jax.ShapeDtypeStruct((n_sets, 8, tile), jnp.float32)]
    elif joined:
        out_shape = [jax.ShapeDtypeStruct((groups * joined, 1, blk), jnp.float32)]
    else:
        out_shape = [jax.ShapeDtypeStruct((groups, 1, blk), jnp.float32)] * len(jobs)
    operands = [labels] + list(arrays.values()) + ([] if prev is None else [prev])
    needed = {piece for _, pieces in jobs for piece in pieces}
    return pl.pallas_call(
        functools.partial(
            compare_kernel, sizes, jobs, names, spots, offsets, joined, prev is not None
        ),
        out_shape=out_shape,
        in_specs=[vmem] * len(operands),
        out_specs=[vmem] * len(out_shape),
        scratch_shapes=[
            pltpu.VMEM((len(needed) * blk, 128), jnp.float32),
            pltpu.VMEM((len(jobs), 8, tile), jnp.float32),
            pltpu.VMEM((len(jobs), 8, tile), jnp.float32),
            pltpu.VMEM((len(jobs), TILES, width, tile), jnp.bfloat16),
            pltpu.VMEM((n_sets, 8, tile), jnp.float32),
        ],
        compiler_params=pltpu.CompilerParams(vmem_limit_bytes=COMPARE_VMEM),
        cost_estimate=pl.CostEstimate(
            flops=2 * work, bytes_accessed=2 * len(used) * blk * width, transcendentals=0
        ),
    )(*operands)


def join_kernel(first_ref, second_ref, out_ref):
    rows = first_ref.shape[0]
    out_ref[:rows, :] = first_ref[...]
    out_ref[rows:, :] = second_ref[...]


def join(first, second):
    rows, width = first.shape
    vmem = pl.BlockSpec(memory_space=pltpu.VMEM)
    return pl.pallas_call(
        join_kernel,
        out_shape=jax.ShapeDtypeStruct((2 * rows, width), first.dtype),
        in_specs=[vmem, vmem],
        out_specs=vmem,
        compiler_params=pltpu.CompilerParams(vmem_limit_bytes=COMPARE_VMEM),
    )(first, second)


def unpack_kernel(sizes, dest_ref, back_ref, out_ref):
    groups, halves, half, cap, blk = sizes
    side = back_ref.shape[0] // groups
    rows = dest_ref.shape[1]
    dest = dest_ref[...]
    slot = lax.broadcasted_iota(jnp.int32, (blk, rows), 0)
    field = lax.broadcasted_iota(jnp.int32, (LABEL_ROWS, blk), 0)
    total = jnp.zeros((LABEL_ROWS, rows), jnp.float32)
    for k in range(groups):
        value = back_ref[k * side]
        for more in range(1, side):
            value = jnp.maximum(value, back_ref[k * side + more])
        top = value.astype(jnp.bfloat16).astype(jnp.float32)
        rest = value - top
        mid = rest.astype(jnp.bfloat16).astype(jnp.float32)
        low = rest - mid
        stack = jnp.where(field == 0, top, jnp.where(field == 1, mid, jnp.where(field == 2, low, 0.0)))
        pick = (slot + k * blk == dest).astype(jnp.float32).astype(jnp.bfloat16)
        total = total + jnp.dot(stack.astype(jnp.bfloat16), pick, preferred_element_type=jnp.float32)
    value = (total[0:1] + total[1:2]) + total[2:3]
    out_ref[...] = jnp.where(dest >= 0, value, -1.0)


def unpack(dest, back, sizes):
    vmem = pl.BlockSpec(memory_space=pltpu.VMEM)
    return pl.pallas_call(
        functools.partial(unpack_kernel, sizes),
        out_shape=jax.ShapeDtypeStruct(dest.shape, jnp.float32),
        in_specs=[vmem] * 2,
        out_specs=vmem,
        compiler_params=pltpu.CompilerParams(vmem_limit_bytes=COMPARE_VMEM),
    )(dest, back)


def on_device(embeddings, cluster, rank):
    rows_dev, width = embeddings.shape
    groups = lax.axis_size("grp")
    members = lax.axis_size("mem")
    devices = groups * members
    halves = 2 * members
    half = rows_dev // CLUS_GRP // 2
    blk = rows_dev // groups
    cap = blk // halves
    sizes = (groups, halves, half, cap, blk)
    side = members // groups

    def swap(value, block_step, member_step):
        mask = member_step // side * members + block_step * side + member_step % side
        if mask == 0:
            return value
        return lax.ppermute(value, ("grp", "mem"), [(i, i ^ mask) for i in range(devices)])

    offsets, pairs = cover(members)
    sends = [None] * groups
    first = tuple(range(1, min(3, groups)))
    for k, value in zip(first, pack(embeddings, cluster, rank, first, False, sizes)):
        sends[k] = value
    rest = tuple(k for k in range(groups) if k not in first)
    cluster, sends[1] = lax.optimization_barrier((cluster, sends[1]))
    *packed, dest, labels = pack(embeddings, cluster, rank, rest, True, sizes)
    for k, value in zip(rest, packed):
        sends[k] = value

    last = groups - 1
    far = [d for d in offsets if d & side and d != side and d ^ side in offsets]
    near = [d for d in offsets[1:] if d not in far]
    lead = far[0] ^ side if far else near[0]
    held = {0: [sends[0]]}
    for d in near:
        held[d] = [swap(sends[0], 0, d)]
    for d in far:
        held[d] = [swap(held[d ^ side][0], 0, side)]
    after = held[lead][0]
    for k in range(1, groups, 2):
        if k > 1:
            send, after = lax.optimization_barrier((sends[k], after))
        else:
            send = sends[k]
        mine = swap(send, k, 0)
        if k < last:
            also = swap(sends[k + 1], k + 1, 0)
            if k == 1:
                mine, also, *firsts = lax.optimization_barrier(
                    (mine, also, *(held[d][0] for d in near))
                )
                for d, value in zip(near, firsts):
                    held[d] = [value]
            mine = join(mine, also)
            if k == 1:
                mine, labels = lax.optimization_barrier((mine, labels))
                labels = lax.all_to_all(
                    labels, ("grp", "mem"), split_axis=0, concat_axis=0, tiled=True
                )
            after = mine
        held[0].append(mine)
        for d in near:
            held[d].append(swap(mine, 0, d))
    for spot in range(1, len(held[0]) - 1):
        held[0][spot + 1], labels, *values = lax.optimization_barrier(
            (held[0][spot + 1], labels, *(held[d][spot] for d in near))
        )
        for d, value in zip(near, values):
            held[d][spot] = value
        for d in far:
            held[d].append(swap(held[d ^ side][spot], 0, side))

    index = {d: i for i, d in enumerate(offsets)}
    blocks = {}

    def note():
        for d in offsets:
            for spot, value in enumerate(held[d]):
                ks = [0] if spot == 0 else [k for k in (2 * spot - 1, 2 * spot) if k < groups]
                for at, k in enumerate(ks):
                    blocks[index[d], k] = (value, at)

    note()
    starts = sorted({a for a, _ in pairs.values()})
    early, late = [], []
    for a in starts:
        cols = [index[b] for _, (e, b) in sorted(pairs.items()) if e == a]
        pieces = [(b, k) for b in cols for k in range(groups)]
        if a == 0:
            soon = [(b, k) for b, k in pieces if b == 0 or k < last]
            early.append((0, soon))
            pieces = [piece for piece in pieces if piece not in soon]
        late.append((index[a], pieces))
    joined = side if all(a < side for a in starts) else 0
    prev = compare(labels, blocks, early, None, 0, offsets, sizes)[0]
    for d in far:
        piece, prev = lax.optimization_barrier((held[d ^ side][-1], prev))
        held[d].append(swap(piece, 0, side))
    note()
    found = compare(labels, blocks, late, prev, joined, offsets, sizes)
    if joined:
        back = found[0]
    else:
        best = {}
        for a, value in zip(starts, found):
            near = a % side
            value = swap(value, 0, a - near)
            best[near] = jnp.maximum(best[near], value) if near in best else value
        none = jnp.full_like(found[0], -1.0)
        near_of = [best.get(near, none) for near in range(side)]
        rows_of = []
        for spot in range(side):
            value = near_of[spot]
            for mine in range(1, side):
                value = jnp.where(lax.axis_index("mem") % side == mine, near_of[spot ^ mine], value)
            rows_of.append(value)
        back = jnp.stack(rows_of, axis=1).reshape(groups * side, 1, blk)
    back = lax.all_to_all(back, "mem", split_axis=0, concat_axis=0, tiled=True)
    return unpack(dest, back, sizes).reshape(rows_dev)


def solution(mesh):
    in_specs = (P(("grp", "mem"), None), P(("grp", "mem")), P(("grp", "mem")))
    out_specs = P(("grp", "mem"))
    return jax.shard_map(
        on_device, mesh=mesh, in_specs=in_specs, out_specs=out_specs, check_vma=False
    )
```

```python
import functools

import jax
import jax.numpy as jnp
from jax import lax
from jax.experimental import pallas as pl
from jax.experimental.pallas import tpu as pltpu
from jax.sharding import PartitionSpec as P

CLUS_GRP = 2
TILES = 4
LABEL_ROWS = 16
FAR = 1.0e9
PACK_VMEM = 60 * 1024 * 1024
COMPARE_VMEM = 24 * 1024 * 1024
NT = (((1,), (1,)), ((), ()))
TN = (((0,), (0,)), ((), ()))


def cover(members):
    bits = [1 << i for i in range(members.bit_length() - 1)]
    offsets = [0] + bits

    def missing(held):
        return set(range(members)) - {a ^ b for a in held for b in held}

    while missing(offsets):
        offsets.append(
            min(
                (d for d in range(members) if d not in offsets),
                key=lambda d: (len(missing(offsets + [d])), bin(d).count("1"), -d),
            )
        )
    pairs = {}
    for delta in range(members):
        pairs[delta] = min(
            (a, a ^ delta) for a in offsets if a ^ delta in offsets
        )
    return offsets, pairs


def pack_kernel(sizes, ks, labelled, emb_hbm, cluster_hbm, rank_hbm, *refs):
    groups, halves, half, cap, blk = sizes
    outs, refs = refs[: len(ks)], refs[len(ks) :]
    if labelled:
        dest_ref, key_ref, *refs = refs
    emb_ref, cluster_ref, rank_ref, stage, sems, out_sems = refs
    rows = emb_ref.shape[0]
    step = 256
    loads = [
        pltpu.make_async_copy(cluster_hbm, cluster_ref, sems.at[0]),
        pltpu.make_async_copy(rank_hbm, rank_ref, sems.at[1]),
    ]
    for j in range(rows // step):
        at = pl.ds(j * step, step)
        loads.append(pltpu.make_async_copy(emb_hbm.at[at], emb_ref.at[at], sems.at[2 + j]))
    for load in loads:
        load.start()
    for load in loads[:2]:
        load.wait()
    cluster = cluster_ref[...]
    rank = rank_ref[...]
    alive = cluster >= 0
    pair = lax.shift_right_logical(jnp.maximum(cluster, 0), 1)
    parity = jnp.maximum(cluster, 0) - 2 * pair
    safe_rank = jnp.maximum(rank, 0)
    which = safe_rank // half
    units = groups * halves
    unit_id = jnp.where(alive, pair * halves + which, -1)
    before_rows = lax.broadcasted_iota(jnp.int32, (step, step), 0)
    before_cols = lax.broadcasted_iota(jnp.int32, (step, step), 1)
    upper = (before_rows < before_cols).astype(jnp.float32).astype(jnp.bfloat16)
    unit_iota = lax.broadcasted_iota(jnp.int32, (units, step), 0)
    carry = jnp.zeros((units, 1), jnp.float32)
    places = []
    for j in range(rows // step):
        mine = unit_id[:, j * step : (j + 1) * step]
        hit = (unit_iota == mine).astype(jnp.float32)
        before = jnp.dot(hit.astype(jnp.bfloat16), upper, preferred_element_type=jnp.float32) + carry
        position = jnp.sum(hit * before, axis=0, keepdims=True)
        carry = carry + jnp.sum(hit, axis=1, keepdims=True)
        places.append(jnp.where(mine >= 0, mine * cap + position.astype(jnp.int32), -1))
    dest = jnp.concatenate(places, axis=1)
    if labelled:
        dest_ref[...] = dest
    members = halves // 2
    side = members // groups
    here = lax.axis_index("mem") // side
    dest = jnp.where(dest >= 0, dest ^ (here * blk), -1)

    units_of = []
    for j in range(rows // step):
        loads[2 + j].wait()
        wide = emb_ref[j * step : (j + 1) * step, :].astype(jnp.float32)
        total = jnp.sum(wide * wide, axis=1, keepdims=True)
        units_of.append((wide * lax.rsqrt(total + 1e-06)).astype(jnp.bfloat16))
    unit = jnp.concatenate(units_of, axis=0)

    field = lax.broadcasted_iota(jnp.int32, (LABEL_ROWS, rows), 0)
    labels = jnp.where(
        field == 0, safe_rank - which * half, jnp.where(field == 1, parity + 1, 0)
    )
    labels = jnp.where(alive, labels, 0).astype(jnp.float32).astype(jnp.bfloat16)
    unit_of = lax.div(lax.broadcasted_iota(jnp.int32, (1, blk), 1), cap).astype(jnp.float32)
    slot = lax.broadcasted_iota(jnp.int32, (blk, rows), 0)
    leaving = []
    for k in (*ks, *(k for k in range(groups) if labelled and k not in ks)):
        pick = (slot + k * blk == dest).astype(jnp.float32).astype(jnp.bfloat16)
        if labelled:
            mine = lax.dot_general(labels, pick, NT, preferred_element_type=jnp.float32)
            key = mine[0:1] + float(half) * unit_of + float(halves * half) * mine[1:2]
            for p in range(groups):
                for y in range(side):
                    key_ref[pl.ds(p * members + (here ^ k) * side + y, 1), 0, :] = key
        if k in ks:
            n = ks.index(k)
            stage[n] = jnp.dot(pick, unit, preferred_element_type=jnp.float32).astype(jnp.bfloat16)
            leaving.append(pltpu.make_async_copy(stage.at[n], outs[n], out_sems.at[n]))
            leaving[-1].start()
    for copy in leaving:
        copy.wait()


def pack(embeddings, cluster, rank, ks, labelled, sizes):
    groups, halves, half, cap, blk = sizes
    rows, width = embeddings.shape
    hbm = pl.BlockSpec(memory_space=pltpu.HBM)
    vmem = pl.BlockSpec(memory_space=pltpu.VMEM)
    out_shape = [jax.ShapeDtypeStruct((blk, width), jnp.bfloat16)] * len(ks)
    out_specs = [hbm] * len(ks)
    if labelled:
        out_shape.append(jax.ShapeDtypeStruct((1, rows), jnp.int32))
        out_shape.append(jax.ShapeDtypeStruct((groups * halves // 2, 1, blk), jnp.float32))
        out_specs += [vmem, vmem]
    return pl.pallas_call(
        functools.partial(pack_kernel, sizes, ks, labelled),
        out_shape=out_shape,
        in_specs=[hbm, hbm, hbm],
        out_specs=out_specs,
        scratch_shapes=[
            pltpu.VMEM((rows, width), jnp.bfloat16),
            pltpu.VMEM((1, rows), jnp.int32),
            pltpu.VMEM((1, rows), jnp.int32),
            pltpu.VMEM((len(ks), blk, width), jnp.bfloat16),
            pltpu.SemaphoreType.DMA((2 + rows // 256,)),
            pltpu.SemaphoreType.DMA((len(ks),)),
        ],
        compiler_params=pltpu.CompilerParams(vmem_limit_bytes=PACK_VMEM),
        cost_estimate=pl.CostEstimate(
            flops=2 * len(ks) * blk * rows * width, bytes_accessed=4 * rows * width, transcendentals=0
        ),
    )(embeddings, cluster.reshape(1, rows), rank.reshape(1, rows))


def compare_kernel(sizes, jobs, names, spots, offsets, starts, joined, has_prev, label_ref, *refs):
    groups, halves, half, cap, blk = sizes
    array = dict(zip(names, refs))
    refs = refs[len(names) :]
    block = {piece: (array[name], at * blk) for piece, (name, at) in spots.items()}
    prev = None
    if has_prev:
        prev, refs = refs[0], refs[1:]
    outs, (key_col, turned, best) = refs[:-3], refs[-3:]
    rows = groups * blk
    per_tile = blk // TILES
    tile = rows // TILES
    cap_all = float(halves * half)

    members = halves // 2
    side = members // groups
    across, along = lax.axis_index("grp"), lax.axis_index("mem")

    def keys_of(piece):
        i, k = piece
        row = (across ^ (offsets[i] // side)) * members
        row += ((along // side) ^ k) * side + ((along % side) ^ (offsets[i] % side))
        return label_ref[pl.ds(row, 1), 0, :]

    weight_row = lax.broadcasted_iota(jnp.int32, (LABEL_ROWS, 128), 0)
    weights = jnp.where(weight_row == 0, 1.0, jnp.where(weight_row == 1, float(half), 0.0))
    weights = weights.astype(jnp.bfloat16)
    field = lax.broadcasted_iota(jnp.int32, (LABEL_ROWS, blk), 0)
    needed = sorted({piece for *_, pieces in jobs for piece in pieces})
    key_at = {piece: n * blk for n, piece in enumerate(needed)}
    for piece in needed:
        key = keys_of(piece)
        high = jnp.floor(key * (1.0 / half))
        split = jnp.where(field == 0, key - high * half, jnp.where(field == 1, high, 0.0))
        key_col[pl.ds(key_at[piece], blk), :] = lax.dot_general(
            split.astype(jnp.bfloat16), weights, TN, preferred_element_type=jnp.float32
        )
    lane = lax.div(lax.broadcasted_iota(jnp.int32, (1, tile), 1), per_tile)

    def floor_of(key):
        low = jnp.floor(key * (1.0 / cap_all)) * cap_all
        return jnp.where(low > 0.5, low, FAR)

    def lines_of(a, ks):
        keys = [keys_of((a, k)) if k in ks else jnp.zeros((1, blk), jnp.float32) for k in range(groups)]
        keys = [jnp.concatenate([key] * (tile // blk), axis=1) for key in keys]
        lines = []
        for t in range(TILES):
            line = jnp.zeros((1, tile), jnp.float32)
            for k in range(groups):
                turn = ((k - t) * per_tile) % tile
                moved = pltpu.roll(keys[k], turn, 1) if turn else keys[k]
                line = jnp.where(lane == k, moved, line)
            lines.append(line)
        return lines

    def rows_of(ref, base, first, last):
        return ref[base + first * per_tile : base + last * per_tile, :]

    best[...] = prev[...] if has_prev else jnp.full(best.shape, -1.0, jnp.float32)

    def search(a, row, queries, mine, pieces, last, spot):
        width = mine.shape[1]
        turned[spot, :, 0:width] = jnp.concatenate(queries, axis=0).T
        floor = floor_of(mine)
        acc = jnp.full((8, width), -1.0, jnp.float32)
        for at in range(0, len(pieces), groups):
            some = pieces[at : at + groups]
            theirs = [rows_of(key_col, key_at[piece], 0, last) for piece in some]
            theirs = jnp.concatenate(theirs, axis=0)
            theirs = jnp.concatenate([theirs] * (width // 128), axis=1)
            sims = jnp.dot(
                jnp.concatenate([rows_of(*block[piece], 0, last) for piece in some], axis=0),
                turned[spot, :, 0:width],
                preferred_element_type=jnp.float32,
            )
            keep = (theirs >= floor) & (theirs < mine)
            sims = jnp.where(keep, sims, -1.0)
            top = jnp.max(sims.reshape(sims.shape[0] // 8, 8, width), axis=0)
            acc = jnp.maximum(acc, top)
        best[a, row : row + 1, 0:width] = jnp.maximum(
            best[a, row : row + 1, 0:width], jnp.max(acc, axis=0, keepdims=True)
        )

    spot = 0
    for a, whole, ks, pieces in jobs:
        if whole:
            (k,) = ks
            queries = [rows_of(*block[a, k], 0, TILES)]
            search(a, TILES, queries, keys_of((a, k)), pieces, TILES, spot)
            spot += 1
            continue
        lines = lines_of(a, ks)
        for t in range(TILES):
            queries = [rows_of(*block[a, k if k in ks else ks[0]], t, t + 1) for k in range(groups)]
            search(a, t, queries, lines[t], pieces, t + 1, spot)
            spot += 1

    if not starts:
        outs[0][...] = best[...]
        return
    for o, a in enumerate(starts):
        found = best[a]
        for k in range(groups):
            total = jnp.full((1, tile), -1.0, jnp.float32)
            for t in range(TILES):
                turn = ((t - k) * per_tile) % tile
                moved = pltpu.roll(found, turn, 1) if turn else found
                total = jnp.where(lane == t, moved[t : t + 1], total)
            if any(a == e and whole and k in ks for e, whole, ks, _ in jobs):
                total = jnp.maximum(total, found[TILES : TILES + 1])
            at = (along // side) ^ k
            if joined:
                outs[0][pl.ds(at * joined + ((along % side) ^ a), 1), 0, :] = total[:, :blk]
            else:
                outs[o][pl.ds(at, 1), 0, :] = total[:, :blk]


def compare(labels, blocks, jobs, prev, starts, joined, offsets, sizes):
    groups, halves, half, cap, blk = sizes
    n_sets = len(offsets)
    used = {piece for *_, pieces in jobs for piece in pieces}
    used |= {(a, k) for a, _, ks, _ in jobs for k in ks}
    searches = sum(1 if whole else TILES for _, whole, _, _ in jobs)
    spots = {}
    arrays = {}
    for piece in sorted(used):
        value, at = blocks[piece]
        name = next((n for n, v in arrays.items() if v is value), None)
        if name is None:
            name = len(arrays)
            arrays[name] = value
        spots[piece] = (name, at)
    names = list(arrays)
    width = arrays[0].shape[1]
    tile = groups * blk // TILES
    vmem = pl.BlockSpec(memory_space=pltpu.VMEM)
    work = blk * tile * width * sum(
        len(pieces) * (1.0 if whole else (TILES + 1) / 2 / TILES) for _, whole, _, pieces in jobs
    )
    if not starts:
        out_shape = [jax.ShapeDtypeStruct((n_sets, 8, tile), jnp.float32)]
    elif joined:
        out_shape = [jax.ShapeDtypeStruct((groups * joined, 1, blk), jnp.float32)]
    else:
        out_shape = [jax.ShapeDtypeStruct((groups, 1, blk), jnp.float32)] * len(starts)
    operands = [labels] + list(arrays.values()) + ([] if prev is None else [prev])
    needed = {piece for *_, pieces in jobs for piece in pieces}
    return pl.pallas_call(
        functools.partial(
            compare_kernel, sizes, jobs, names, spots, offsets, starts, joined, prev is not None
        ),
        out_shape=out_shape,
        in_specs=[vmem] * len(operands),
        out_specs=[vmem] * len(out_shape),
        scratch_shapes=[
            pltpu.VMEM((len(needed) * blk, 128), jnp.float32),
            pltpu.VMEM((searches, width, tile), jnp.bfloat16),
            pltpu.VMEM((n_sets, 8, tile), jnp.float32),
        ],
        compiler_params=pltpu.CompilerParams(vmem_limit_bytes=COMPARE_VMEM),
        cost_estimate=pl.CostEstimate(
            flops=int(2 * work), bytes_accessed=2 * len(used) * blk * width, transcendentals=0
        ),
    )(*operands)


def join_kernel(first_ref, second_ref, out_ref):
    rows = first_ref.shape[0]
    out_ref[:rows, :] = first_ref[...]
    out_ref[rows:, :] = second_ref[...]


def join(first, second):
    rows, width = first.shape
    vmem = pl.BlockSpec(memory_space=pltpu.VMEM)
    return pl.pallas_call(
        join_kernel,
        out_shape=jax.ShapeDtypeStruct((2 * rows, width), first.dtype),
        in_specs=[vmem, vmem],
        out_specs=vmem,
        compiler_params=pltpu.CompilerParams(vmem_limit_bytes=COMPARE_VMEM),
    )(first, second)


def unpack_kernel(sizes, dest_ref, back_ref, out_ref):
    groups, halves, half, cap, blk = sizes
    side = back_ref.shape[0] // groups
    rows = dest_ref.shape[1]
    dest = dest_ref[...]
    slot = lax.broadcasted_iota(jnp.int32, (blk, rows), 0)
    field = lax.broadcasted_iota(jnp.int32, (LABEL_ROWS, blk), 0)
    total = jnp.zeros((LABEL_ROWS, rows), jnp.float32)
    for k in range(groups):
        value = back_ref[k * side]
        for more in range(1, side):
            value = jnp.maximum(value, back_ref[k * side + more])
        top = value.astype(jnp.bfloat16).astype(jnp.float32)
        rest = value - top
        mid = rest.astype(jnp.bfloat16).astype(jnp.float32)
        low = rest - mid
        stack = jnp.where(field == 0, top, jnp.where(field == 1, mid, jnp.where(field == 2, low, 0.0)))
        pick = (slot + k * blk == dest).astype(jnp.float32).astype(jnp.bfloat16)
        total = total + jnp.dot(stack.astype(jnp.bfloat16), pick, preferred_element_type=jnp.float32)
    value = (total[0:1] + total[1:2]) + total[2:3]
    out_ref[...] = jnp.where(dest >= 0, value, -1.0)


def unpack(dest, back, sizes):
    vmem = pl.BlockSpec(memory_space=pltpu.VMEM)
    return pl.pallas_call(
        functools.partial(unpack_kernel, sizes),
        out_shape=jax.ShapeDtypeStruct(dest.shape, jnp.float32),
        in_specs=[vmem] * 2,
        out_specs=vmem,
        compiler_params=pltpu.CompilerParams(vmem_limit_bytes=COMPARE_VMEM),
    )(dest, back)


def on_device(embeddings, cluster, rank):
    rows_dev, width = embeddings.shape
    groups = lax.axis_size("grp")
    members = lax.axis_size("mem")
    devices = groups * members
    halves = 2 * members
    half = rows_dev // CLUS_GRP // 2
    blk = rows_dev // groups
    cap = blk // halves
    sizes = (groups, halves, half, cap, blk)
    side = members // groups

    def swap(value, block_step, member_step):
        mask = member_step // side * members + block_step * side + member_step % side
        if mask == 0:
            return value
        return lax.ppermute(value, ("grp", "mem"), [(i, i ^ mask) for i in range(devices)])

    offsets, pairs = cover(members)
    sends = [None] * groups
    first = tuple(range(1, min(3, groups)))
    for k, value in zip(first, pack(embeddings, cluster, rank, first, False, sizes)):
        sends[k] = value
    rest = tuple(k for k in range(groups) if k not in first)
    cluster, sends[1] = lax.optimization_barrier((cluster, sends[1]))
    *packed, dest, labels = pack(embeddings, cluster, rank, rest, True, sizes)
    for k, value in zip(rest, packed):
        sends[k] = value

    last = groups - 1
    far = [d for d in offsets if d & side and d != side and d ^ side in offsets]
    near = [d for d in offsets[1:] if d not in far]
    lead = far[0] ^ side if far else near[0]
    held = {0: [sends[0]]}
    for d in near:
        held[d] = [swap(sends[0], 0, d)]
    for d in far:
        held[d] = [swap(held[d ^ side][0], 0, side)]
    after = held[lead][0]
    for k in range(1, groups, 2):
        if k > 1:
            send, after = lax.optimization_barrier((sends[k], after))
        else:
            send = sends[k]
        mine = swap(send, k, 0)
        if k < last:
            also = swap(sends[k + 1], k + 1, 0)
            if k == 1:
                mine, also, *firsts = lax.optimization_barrier(
                    (mine, also, *(held[d][0] for d in near))
                )
                for d, value in zip(near, firsts):
                    held[d] = [value]
            mine = join(mine, also)
            if k == 1:
                mine, labels = lax.optimization_barrier((mine, labels))
                labels = lax.all_to_all(
                    labels, ("grp", "mem"), split_axis=0, concat_axis=0, tiled=True
                )
            after = mine
        held[0].append(mine)
        for d in near:
            held[d].append(swap(mine, 0, d))
    for spot in range(1, len(held[0]) - 1):
        held[0][spot + 1], labels, *values = lax.optimization_barrier(
            (held[0][spot + 1], labels, *(held[d][0] for d in far), *(held[d][spot] for d in near))
        )
        for d in far:
            held[d][0] = values.pop(0)
        for d, value in zip(near, values):
            held[d][spot] = value
    for d in far:
        for spot in range(1, len(held[0]) - 1):
            held[d].append(swap(held[d ^ side][spot], 0, side))

    index = {d: i for i, d in enumerate(offsets)}
    blocks = {}

    def note():
        for d in offsets:
            for spot, value in enumerate(held[d]):
                ks = [0] if spot == 0 else [k for k in (2 * spot - 1, 2 * spot) if k < groups]
                for at, k in enumerate(ks):
                    blocks[index[d], k] = (value, at)

    note()
    starts = sorted({a for a, _ in pairs.values()})
    every = tuple(range(groups))
    early, middle, late = [], [], []
    for a in starts:
        cols = [index[b] for _, (e, b) in sorted(pairs.items()) if e == a]
        pieces = [(b, k) for b in cols for k in every]
        soon = [(b, k) for b, k in pieces if k < last]
        if a == 0:
            slow = {(index[d], k) for d in far for k in range(1, last)} | {(index[side], last)}
            ready = [piece for piece in pieces if piece in soon or piece[0] == 0]
            early.append((0, False, every, [piece for piece in ready if piece not in slow]))
            middle.append((0, False, every, [piece for piece in pieces if piece in slow]))
            done = early[-1][-1] + middle[-1][-1]
            late.append((0, False, every, [piece for piece in pieces if piece not in done]))
        else:
            middle.append((index[a], False, every[:-1], soon))
            late.append((index[a], False, every, [piece for piece in pieces if piece not in soon]))
            late.append((index[a], True, (last,), soon))
    order = [index[a] for a in starts]
    joined = side if all(a < side for a in starts) else 0
    prev = compare(labels, blocks, early, None, (), 0, offsets, sizes)[0]
    prev = compare(labels, blocks, middle, prev, (), 0, offsets, sizes)[0]
    for d in far:
        piece, prev = lax.optimization_barrier((held[d ^ side][-1], prev))
        held[d].append(swap(piece, 0, side))
    note()
    found = compare(labels, blocks, late, prev, order, joined, offsets, sizes)
    if joined:
        back = found[0]
    else:
        best = {}
        for a, value in zip(starts, found):
            near = a % side
            value = swap(value, 0, a - near)
            best[near] = jnp.maximum(best[near], value) if near in best else value
        none = jnp.full_like(found[0], -1.0)
        near_of = [best.get(near, none) for near in range(side)]
        rows_of = []
        for spot in range(side):
            value = near_of[spot]
            for mine in range(1, side):
                value = jnp.where(lax.axis_index("mem") % side == mine, near_of[spot ^ mine], value)
            rows_of.append(value)
        back = jnp.stack(rows_of, axis=1).reshape(groups * side, 1, blk)
    back = lax.all_to_all(back, "mem", split_axis=0, concat_axis=0, tiled=True)
    return unpack(dest, back, sizes).reshape(rows_dev)


def solution(mesh):
    in_specs = (P(("grp", "mem"), None), P(("grp", "mem")), P(("grp", "mem")))
    out_specs = P(("grp", "mem"))
    return jax.shard_map(
        on_device, mesh=mesh, in_specs=in_specs, out_specs=out_specs, check_vma=False
    )
```

```python
import functools

import jax
import jax.numpy as jnp
from jax import lax
from jax.experimental import pallas as pl
from jax.experimental.pallas import tpu as pltpu
from jax.sharding import PartitionSpec as P

CLUS_GRP = 2
TILES = 4
LABEL_ROWS = 16
FAR = 1.0e9
PACK_VMEM = 60 * 1024 * 1024
COMPARE_VMEM = 24 * 1024 * 1024
NT = (((1,), (1,)), ((), ()))
TN = (((0,), (0,)), ((), ()))


def cover(members):
    bits = [1 << i for i in range(members.bit_length() - 1)]
    offsets = [0] + bits

    def missing(held):
        return set(range(members)) - {a ^ b for a in held for b in held}

    while missing(offsets):
        offsets.append(
            min(
                (d for d in range(members) if d not in offsets),
                key=lambda d: (len(missing(offsets + [d])), bin(d).count("1"), -d),
            )
        )
    pairs = {}
    for delta in range(members):
        pairs[delta] = min(
            (a, a ^ delta) for a in offsets if a ^ delta in offsets
        )
    return offsets, pairs


def pack_kernel(sizes, ks, labelled, emb_hbm, cluster_hbm, rank_hbm, *refs):
    groups, halves, half, cap, blk = sizes
    outs, refs = refs[: len(ks)], refs[len(ks) :]
    if labelled:
        dest_ref, key_ref, *refs = refs
    emb_ref, cluster_ref, rank_ref, stage, sems, out_sems = refs
    rows = emb_ref.shape[0]
    step = 256
    loads = [
        pltpu.make_async_copy(cluster_hbm, cluster_ref, sems.at[0]),
        pltpu.make_async_copy(rank_hbm, rank_ref, sems.at[1]),
    ]
    for j in range(rows // step):
        at = pl.ds(j * step, step)
        loads.append(pltpu.make_async_copy(emb_hbm.at[at], emb_ref.at[at], sems.at[2 + j]))
    for load in loads:
        load.start()
    for load in loads[:2]:
        load.wait()
    cluster = cluster_ref[...]
    rank = rank_ref[...]
    alive = cluster >= 0
    pair = lax.shift_right_logical(jnp.maximum(cluster, 0), 1)
    parity = jnp.maximum(cluster, 0) - 2 * pair
    safe_rank = jnp.maximum(rank, 0)
    which = safe_rank // half
    units = groups * halves
    unit_id = jnp.where(alive, pair * halves + which, -1)
    before_rows = lax.broadcasted_iota(jnp.int32, (step, step), 0)
    before_cols = lax.broadcasted_iota(jnp.int32, (step, step), 1)
    upper = (before_rows < before_cols).astype(jnp.float32).astype(jnp.bfloat16)
    unit_iota = lax.broadcasted_iota(jnp.int32, (units, step), 0)
    carry = jnp.zeros((units, 1), jnp.float32)
    places = []
    for j in range(rows // step):
        mine = unit_id[:, j * step : (j + 1) * step]
        hit = (unit_iota == mine).astype(jnp.float32)
        before = jnp.dot(hit.astype(jnp.bfloat16), upper, preferred_element_type=jnp.float32) + carry
        position = jnp.sum(hit * before, axis=0, keepdims=True)
        carry = carry + jnp.sum(hit, axis=1, keepdims=True)
        places.append(jnp.where(mine >= 0, mine * cap + position.astype(jnp.int32), -1))
    dest = jnp.concatenate(places, axis=1)
    if labelled:
        dest_ref[...] = dest
    members = halves // 2
    side = members // groups
    here = lax.axis_index("mem") // side
    dest = jnp.where(dest >= 0, dest ^ (here * blk), -1)

    units_of = []
    for j in range(rows // step):
        loads[2 + j].wait()
        wide = emb_ref[j * step : (j + 1) * step, :].astype(jnp.float32)
        total = jnp.sum(wide * wide, axis=1, keepdims=True)
        units_of.append((wide * lax.rsqrt(total + 1e-06)).astype(jnp.bfloat16))
    unit = jnp.concatenate(units_of, axis=0)

    field = lax.broadcasted_iota(jnp.int32, (LABEL_ROWS, rows), 0)
    labels = jnp.where(
        field == 0, safe_rank - which * half, jnp.where(field == 1, parity + 1, 0)
    )
    labels = jnp.where(alive, labels, 0).astype(jnp.float32).astype(jnp.bfloat16)
    unit_of = lax.div(lax.broadcasted_iota(jnp.int32, (1, blk), 1), cap).astype(jnp.float32)
    slot = lax.broadcasted_iota(jnp.int32, (blk, rows), 0)
    leaving = []
    for k in (*ks, *(k for k in range(groups) if labelled and k not in ks)):
        pick = (slot + k * blk == dest).astype(jnp.float32).astype(jnp.bfloat16)
        if labelled:
            mine = lax.dot_general(labels, pick, NT, preferred_element_type=jnp.float32)
            key = mine[0:1] + float(half) * unit_of + float(halves * half) * mine[1:2]
            for p in range(groups):
                for y in range(side):
                    key_ref[pl.ds(p * members + (here ^ k) * side + y, 1), 0, :] = key
        if k in ks:
            n = ks.index(k)
            stage[n] = jnp.dot(pick, unit, preferred_element_type=jnp.float32).astype(jnp.bfloat16)
            leaving.append(pltpu.make_async_copy(stage.at[n], outs[n], out_sems.at[n]))
            leaving[-1].start()
    for copy in leaving:
        copy.wait()


def pack(embeddings, cluster, rank, ks, labelled, sizes):
    groups, halves, half, cap, blk = sizes
    rows, width = embeddings.shape
    hbm = pl.BlockSpec(memory_space=pltpu.HBM)
    vmem = pl.BlockSpec(memory_space=pltpu.VMEM)
    out_shape = [jax.ShapeDtypeStruct((blk, width), jnp.bfloat16)] * len(ks)
    out_specs = [hbm] * len(ks)
    if labelled:
        out_shape.append(jax.ShapeDtypeStruct((1, rows), jnp.int32))
        out_shape.append(jax.ShapeDtypeStruct((groups * halves // 2, 1, blk), jnp.float32))
        out_specs += [vmem, vmem]
    return pl.pallas_call(
        functools.partial(pack_kernel, sizes, ks, labelled),
        out_shape=out_shape,
        in_specs=[hbm, hbm, hbm],
        out_specs=out_specs,
        scratch_shapes=[
            pltpu.VMEM((rows, width), jnp.bfloat16),
            pltpu.VMEM((1, rows), jnp.int32),
            pltpu.VMEM((1, rows), jnp.int32),
            pltpu.VMEM((len(ks), blk, width), jnp.bfloat16),
            pltpu.SemaphoreType.DMA((2 + rows // 256,)),
            pltpu.SemaphoreType.DMA((len(ks),)),
        ],
        compiler_params=pltpu.CompilerParams(vmem_limit_bytes=PACK_VMEM),
        cost_estimate=pl.CostEstimate(
            flops=2 * len(ks) * blk * rows * width, bytes_accessed=4 * rows * width, transcendentals=0
        ),
    )(embeddings, cluster.reshape(1, rows), rank.reshape(1, rows))


def compare_kernel(sizes, jobs, names, spots, offsets, starts, joined, has_prev, label_ref, *refs):
    groups, halves, half, cap, blk = sizes
    array = dict(zip(names, refs))
    refs = refs[len(names) :]
    block = {piece: (array[name], at * blk) for piece, (name, at) in spots.items()}
    prev = None
    if has_prev:
        prev, refs = refs[0], refs[1:]
    outs, (key_col, turned, best) = refs[:-3], refs[-3:]
    rows = groups * blk
    per_tile = blk // TILES
    tile = rows // TILES
    cap_all = float(halves * half)

    members = halves // 2
    side = members // groups
    across, along = lax.axis_index("grp"), lax.axis_index("mem")

    def keys_of(piece):
        i, k = piece
        row = (across ^ (offsets[i] // side)) * members
        row += ((along // side) ^ k) * side + ((along % side) ^ (offsets[i] % side))
        return label_ref[pl.ds(row, 1), 0, :]

    weight_row = lax.broadcasted_iota(jnp.int32, (LABEL_ROWS, 128), 0)
    weights = jnp.where(weight_row == 0, 1.0, jnp.where(weight_row == 1, float(half), 0.0))
    weights = weights.astype(jnp.bfloat16)
    field = lax.broadcasted_iota(jnp.int32, (LABEL_ROWS, blk), 0)
    needed = sorted({piece for *_, pieces in jobs for piece in pieces})
    key_at = {piece: n * blk for n, piece in enumerate(needed)}
    for piece in needed:
        key = keys_of(piece)
        high = jnp.floor(key * (1.0 / half))
        split = jnp.where(field == 0, key - high * half, jnp.where(field == 1, high, 0.0))
        key_col[pl.ds(key_at[piece], blk), :] = lax.dot_general(
            split.astype(jnp.bfloat16), weights, TN, preferred_element_type=jnp.float32
        )
    lane = lax.div(lax.broadcasted_iota(jnp.int32, (1, tile), 1), per_tile)

    def floor_of(key):
        low = jnp.floor(key * (1.0 / cap_all)) * cap_all
        return jnp.where(low > 0.5, low, FAR)

    def lines_of(a, ks):
        keys = [keys_of((a, k)) if k in ks else jnp.zeros((1, blk), jnp.float32) for k in range(groups)]
        keys = [jnp.concatenate([key] * (tile // blk), axis=1) for key in keys]
        lines = []
        for t in range(TILES):
            line = jnp.zeros((1, tile), jnp.float32)
            for k in range(groups):
                turn = ((k - t) * per_tile) % tile
                moved = pltpu.roll(keys[k], turn, 1) if turn else keys[k]
                line = jnp.where(lane == k, moved, line)
            lines.append(line)
        return lines

    def rows_of(ref, base, first, last):
        return ref[base + first * per_tile : base + last * per_tile, :]

    best[...] = prev[...] if has_prev else jnp.full(best.shape, -1.0, jnp.float32)

    def search(a, row, queries, mine, pieces, last, spot):
        width = mine.shape[1]
        turned[spot, :, 0:width] = jnp.concatenate(queries, axis=0).T
        floor = floor_of(mine)
        acc = jnp.full((8, width), -1.0, jnp.float32)
        for at in range(0, len(pieces), groups):
            some = pieces[at : at + groups]
            theirs = [rows_of(key_col, key_at[piece], 0, last) for piece in some]
            theirs = jnp.concatenate(theirs, axis=0)
            theirs = jnp.concatenate([theirs] * (width // 128), axis=1)
            sims = jnp.dot(
                jnp.concatenate([rows_of(*block[piece], 0, last) for piece in some], axis=0),
                turned[spot, :, 0:width],
                preferred_element_type=jnp.float32,
            )
            keep = (theirs >= floor) & (theirs < mine)
            sims = jnp.where(keep, sims, -1.0)
            top = jnp.max(sims.reshape(sims.shape[0] // 8, 8, width), axis=0)
            acc = jnp.maximum(acc, top)
        best[a, row : row + 1, 0:width] = jnp.maximum(
            best[a, row : row + 1, 0:width], jnp.max(acc, axis=0, keepdims=True)
        )

    spot = 0
    for a, whole, ks, pieces in jobs:
        if whole:
            (k,) = ks
            queries = [rows_of(*block[a, k], 0, TILES)]
            search(a, TILES, queries, keys_of((a, k)), pieces, TILES, spot)
            spot += 1
            continue
        lines = lines_of(a, ks)
        for t in range(TILES):
            queries = [rows_of(*block[a, k if k in ks else ks[0]], t, t + 1) for k in range(groups)]
            search(a, t, queries, lines[t], pieces, t + 1, spot)
            spot += 1

    if not starts:
        outs[0][...] = best[...]
        return
    for o, a in enumerate(starts):
        found = best[a]
        for k in range(groups):
            total = jnp.full((1, tile), -1.0, jnp.float32)
            for t in range(TILES):
                turn = ((t - k) * per_tile) % tile
                moved = pltpu.roll(found, turn, 1) if turn else found
                total = jnp.where(lane == t, moved[t : t + 1], total)
            if any(a == e and whole and k in ks for e, whole, ks, _ in jobs):
                total = jnp.maximum(total, found[TILES : TILES + 1])
            at = (along // side) ^ k
            if joined:
                outs[0][pl.ds(at * joined + ((along % side) ^ a), 1), 0, :] = total[:, :blk]
            else:
                outs[o][pl.ds(at, 1), 0, :] = total[:, :blk]


def compare(labels, blocks, jobs, prev, starts, joined, offsets, sizes):
    groups, halves, half, cap, blk = sizes
    n_sets = len(offsets)
    used = {piece for *_, pieces in jobs for piece in pieces}
    used |= {(a, k) for a, _, ks, _ in jobs for k in ks}
    searches = sum(1 if whole else TILES for _, whole, _, _ in jobs)
    spots = {}
    arrays = {}
    for piece in sorted(used):
        value, at = blocks[piece]
        name = next((n for n, v in arrays.items() if v is value), None)
        if name is None:
            name = len(arrays)
            arrays[name] = value
        spots[piece] = (name, at)
    names = list(arrays)
    width = arrays[0].shape[1]
    tile = groups * blk // TILES
    vmem = pl.BlockSpec(memory_space=pltpu.VMEM)
    work = blk * tile * width * sum(
        len(pieces) * (1.0 if whole else (TILES + 1) / 2 / TILES) for _, whole, _, pieces in jobs
    )
    if not starts:
        out_shape = [jax.ShapeDtypeStruct((n_sets, 8, tile), jnp.float32)]
    elif joined:
        out_shape = [jax.ShapeDtypeStruct((groups * joined, 1, blk), jnp.float32)]
    else:
        out_shape = [jax.ShapeDtypeStruct((groups, 1, blk), jnp.float32)] * len(starts)
    operands = [labels] + list(arrays.values()) + ([] if prev is None else [prev])
    needed = {piece for *_, pieces in jobs for piece in pieces}
    return pl.pallas_call(
        functools.partial(
            compare_kernel, sizes, jobs, names, spots, offsets, starts, joined, prev is not None
        ),
        out_shape=out_shape,
        in_specs=[vmem] * len(operands),
        out_specs=[vmem] * len(out_shape),
        scratch_shapes=[
            pltpu.VMEM((len(needed) * blk, 128), jnp.float32),
            pltpu.VMEM((searches, width, tile), jnp.bfloat16),
            pltpu.VMEM((n_sets, 8, tile), jnp.float32),
        ],
        compiler_params=pltpu.CompilerParams(vmem_limit_bytes=COMPARE_VMEM),
        cost_estimate=pl.CostEstimate(
            flops=int(2 * work), bytes_accessed=2 * len(used) * blk * width, transcendentals=0
        ),
    )(*operands)


def join_kernel(first_ref, second_ref, out_ref):
    rows = first_ref.shape[0]
    out_ref[:rows, :] = first_ref[...]
    out_ref[rows:, :] = second_ref[...]


def join(first, second):
    rows, width = first.shape
    vmem = pl.BlockSpec(memory_space=pltpu.VMEM)
    return pl.pallas_call(
        join_kernel,
        out_shape=jax.ShapeDtypeStruct((2 * rows, width), first.dtype),
        in_specs=[vmem, vmem],
        out_specs=vmem,
        compiler_params=pltpu.CompilerParams(vmem_limit_bytes=COMPARE_VMEM),
    )(first, second)


def unpack_kernel(sizes, dest_ref, back_ref, out_ref):
    groups, halves, half, cap, blk = sizes
    side = back_ref.shape[0] // groups
    rows = dest_ref.shape[1]
    dest = dest_ref[...]
    slot = lax.broadcasted_iota(jnp.int32, (blk, rows), 0)
    field = lax.broadcasted_iota(jnp.int32, (LABEL_ROWS, blk), 0)
    total = jnp.zeros((LABEL_ROWS, rows), jnp.float32)
    for k in range(groups):
        value = back_ref[k * side]
        for more in range(1, side):
            value = jnp.maximum(value, back_ref[k * side + more])
        top = value.astype(jnp.bfloat16).astype(jnp.float32)
        rest = value - top
        mid = rest.astype(jnp.bfloat16).astype(jnp.float32)
        low = rest - mid
        stack = jnp.where(field == 0, top, jnp.where(field == 1, mid, jnp.where(field == 2, low, 0.0)))
        pick = (slot + k * blk == dest).astype(jnp.float32).astype(jnp.bfloat16)
        total = total + jnp.dot(stack.astype(jnp.bfloat16), pick, preferred_element_type=jnp.float32)
    value = (total[0:1] + total[1:2]) + total[2:3]
    out_ref[...] = jnp.where(dest >= 0, value, -1.0)


def unpack(dest, back, sizes):
    vmem = pl.BlockSpec(memory_space=pltpu.VMEM)
    return pl.pallas_call(
        functools.partial(unpack_kernel, sizes),
        out_shape=jax.ShapeDtypeStruct(dest.shape, jnp.float32),
        in_specs=[vmem] * 2,
        out_specs=vmem,
        compiler_params=pltpu.CompilerParams(vmem_limit_bytes=COMPARE_VMEM),
    )(dest, back)


def on_device(embeddings, cluster, rank):
    rows_dev, width = embeddings.shape
    groups = lax.axis_size("grp")
    members = lax.axis_size("mem")
    devices = groups * members
    halves = 2 * members
    half = rows_dev // CLUS_GRP // 2
    blk = rows_dev // groups
    cap = blk // halves
    sizes = (groups, halves, half, cap, blk)
    side = members // groups

    def swap(value, block_step, member_step):
        mask = member_step // side * members + block_step * side + member_step % side
        if mask == 0:
            return value
        return lax.ppermute(value, ("grp", "mem"), [(i, i ^ mask) for i in range(devices)])

    offsets, pairs = cover(members)
    sends = [None] * groups
    first = tuple(range(1, min(3, groups)))
    for k, value in zip(first, pack(embeddings, cluster, rank, first, False, sizes)):
        sends[k] = value
    rest = tuple(k for k in range(groups) if k not in first)
    cluster, sends[1] = lax.optimization_barrier((cluster, sends[1]))
    *packed, dest, labels = pack(embeddings, cluster, rank, rest, True, sizes)
    for k, value in zip(rest, packed):
        sends[k] = value
    labels = lax.all_to_all(labels, ("grp", "mem"), split_axis=0, concat_axis=0, tiled=True)

    last = groups - 1
    far = [d for d in offsets if d & side and d != side and d ^ side in offsets]
    near = [d for d in offsets[1:] if d not in far]
    lead = far[0] ^ side if far else near[0]
    held = {0: [sends[0]]}
    for d in near:
        held[d] = [swap(sends[0], 0, d)]
    for d in far:
        held[d] = [swap(held[d ^ side][0], 0, side)]
    after = held[lead][0]
    for k in range(1, groups, 2):
        if k > 1:
            send, after = lax.optimization_barrier((sends[k], after))
        else:
            send = sends[k]
        mine = swap(send, k, 0)
        if k < last:
            also = swap(sends[k + 1], k + 1, 0)
            if k == 1:
                mine, also, labels, *firsts = lax.optimization_barrier(
                    (mine, also, labels, *(held[d][0] for d in near))
                )
                for d, value in zip(near, firsts):
                    held[d] = [value]
            mine = join(mine, also)
            after = mine
        held[0].append(mine)
        for d in near:
            held[d].append(swap(mine, 0, d))
    for spot in range(1, len(held[0]) - 1):
        held[0][spot + 1], *values = lax.optimization_barrier(
            (held[0][spot + 1], *(held[d][0] for d in far), *(held[d][spot] for d in near))
        )
        for d in far:
            held[d][0] = values.pop(0)
        for d, value in zip(near, values):
            held[d][spot] = value
    for d in far:
        for spot in range(1, len(held[0]) - 1):
            held[d].append(swap(held[d ^ side][spot], 0, side))

    index = {d: i for i, d in enumerate(offsets)}
    blocks = {}

    def note():
        for d in offsets:
            for spot, value in enumerate(held[d]):
                ks = [0] if spot == 0 else [k for k in (2 * spot - 1, 2 * spot) if k < groups]
                for at, k in enumerate(ks):
                    blocks[index[d], k] = (value, at)

    note()
    starts = sorted({a for a, _ in pairs.values()})
    every = tuple(range(groups))
    early, middle, late = [], [], []
    for a in starts:
        cols = [index[b] for _, (e, b) in sorted(pairs.items()) if e == a]
        pieces = [(b, k) for b in cols for k in every]
        soon = [(b, k) for b, k in pieces if k < last]
        if a == 0:
            slow = {(index[d], k) for d in far for k in range(1, last)} | {(index[side], last)}
            ready = [piece for piece in pieces if piece in soon or piece[0] == 0]
            early.append((0, False, every, [piece for piece in ready if piece not in slow]))
            middle.append((0, False, every, [piece for piece in pieces if piece in slow]))
            done = early[-1][-1] + middle[-1][-1]
            late.append((0, False, every, [piece for piece in pieces if piece not in done]))
        else:
            middle.append((index[a], False, every[:-1], soon))
            late.append((index[a], False, every, [piece for piece in pieces if piece not in soon]))
            late.append((index[a], True, (last,), soon))
    order = [index[a] for a in starts]
    joined = side if all(a < side for a in starts) else 0
    prev = compare(labels, blocks, early, None, (), 0, offsets, sizes)[0]
    prev = compare(labels, blocks, middle, prev, (), 0, offsets, sizes)[0]
    for d in far:
        piece, prev = lax.optimization_barrier((held[d ^ side][-1], prev))
        held[d].append(swap(piece, 0, side))
    note()
    found = compare(labels, blocks, late, prev, order, joined, offsets, sizes)
    if joined:
        back = found[0]
    else:
        best = {}
        for a, value in zip(starts, found):
            near = a % side
            value = swap(value, 0, a - near)
            best[near] = jnp.maximum(best[near], value) if near in best else value
        none = jnp.full_like(found[0], -1.0)
        near_of = [best.get(near, none) for near in range(side)]
        rows_of = []
        for spot in range(side):
            value = near_of[spot]
            for mine in range(1, side):
                value = jnp.where(lax.axis_index("mem") % side == mine, near_of[spot ^ mine], value)
            rows_of.append(value)
        back = jnp.stack(rows_of, axis=1).reshape(groups * side, 1, blk)
    back = lax.all_to_all(back, "mem", split_axis=0, concat_axis=0, tiled=True)
    return unpack(dest, back, sizes).reshape(rows_dev)


def solution(mesh):
    in_specs = (P(("grp", "mem"), None), P(("grp", "mem")), P(("grp", "mem")))
    out_specs = P(("grp", "mem"))
    return jax.shard_map(
        on_device, mesh=mesh, in_specs=in_specs, out_specs=out_specs, check_vma=False
    )
```

```python
import functools

import jax
import jax.numpy as jnp
from jax import lax
from jax.experimental import pallas as pl
from jax.experimental.pallas import tpu as pltpu
from jax.sharding import PartitionSpec as P

CLUS_GRP = 2
TILES = 4
LABEL_ROWS = 16
FAR = 1.0e9
WANTED = 20_000_000_000
PACK_VMEM = 60 * 1024 * 1024
COMPARE_VMEM = 24 * 1024 * 1024
NT = (((1,), (1,)), ((), ()))
TN = (((0,), (0,)), ((), ()))


def cover(members):
    bits = [1 << i for i in range(members.bit_length() - 1)]
    offsets = [0] + bits

    def missing(held):
        return set(range(members)) - {a ^ b for a in held for b in held}

    while missing(offsets):
        offsets.append(
            min(
                (d for d in range(members) if d not in offsets),
                key=lambda d: (len(missing(offsets + [d])), bin(d).count("1"), -d),
            )
        )
    pairs = {}
    for delta in range(members):
        pairs[delta] = min(
            (a, a ^ delta) for a in offsets if a ^ delta in offsets
        )
    return offsets, pairs


def pack_kernel(sizes, ks, placed, emb_hbm, cluster_hbm, rank_hbm, *refs):
    groups, halves, half, cap, blk = sizes
    outs, refs = refs[: len(ks)], refs[len(ks) :]
    if placed:
        dest_ref, *refs = refs
    emb_ref, cluster_ref, rank_ref, stage, sems, out_sems = refs
    rows = emb_ref.shape[0]
    step = 256
    loads = [
        pltpu.make_async_copy(cluster_hbm, cluster_ref, sems.at[0]),
        pltpu.make_async_copy(rank_hbm, rank_ref, sems.at[1]),
    ]
    for j in range(rows // step):
        at = pl.ds(j * step, step)
        loads.append(pltpu.make_async_copy(emb_hbm.at[at], emb_ref.at[at], sems.at[2 + j]))
    for load in loads:
        load.start()
    for load in loads[:2]:
        load.wait()
    cluster = cluster_ref[...]
    rank = rank_ref[...]
    alive = cluster >= 0
    pair = lax.shift_right_logical(jnp.maximum(cluster, 0), 1)
    parity = jnp.maximum(cluster, 0) - 2 * pair
    safe_rank = jnp.maximum(rank, 0)
    which = safe_rank // half
    units = groups * halves
    unit_id = jnp.where(alive, pair * halves + which, -1)
    before_rows = lax.broadcasted_iota(jnp.int32, (step, step), 0)
    before_cols = lax.broadcasted_iota(jnp.int32, (step, step), 1)
    upper = (before_rows < before_cols).astype(jnp.float32).astype(jnp.bfloat16)
    unit_iota = lax.broadcasted_iota(jnp.int32, (units, step), 0)
    carry = jnp.zeros((units, 1), jnp.float32)
    places = []
    for j in range(rows // step):
        mine = unit_id[:, j * step : (j + 1) * step]
        hit = (unit_iota == mine).astype(jnp.float32)
        before = jnp.dot(hit.astype(jnp.bfloat16), upper, preferred_element_type=jnp.float32) + carry
        position = jnp.sum(hit * before, axis=0, keepdims=True)
        carry = carry + jnp.sum(hit, axis=1, keepdims=True)
        places.append(jnp.where(mine >= 0, mine * cap + position.astype(jnp.int32), -1))
    dest = jnp.concatenate(places, axis=1)
    if placed:
        dest_ref[...] = dest
    members = halves // 2
    side = members // groups
    here = lax.axis_index("mem") // side
    dest = jnp.where(dest >= 0, dest ^ (here * blk), -1)

    units_of = []
    for j in range(rows // step):
        loads[2 + j].wait()
        wide = emb_ref[j * step : (j + 1) * step, :].astype(jnp.float32)
        total = jnp.sum(wide * wide, axis=1, keepdims=True)
        units_of.append((wide * lax.rsqrt(total + 1e-06)).astype(jnp.bfloat16))
    unit = jnp.concatenate(units_of, axis=0)

    field = lax.broadcasted_iota(jnp.int32, (LABEL_ROWS, rows), 0)
    labels = jnp.where(
        field == 0, safe_rank - which * half, jnp.where(field == 1, parity + 1, 0)
    )
    labels = jnp.where(alive, labels, 0).astype(jnp.float32).astype(jnp.bfloat16)
    unit_of = lax.div(lax.broadcasted_iota(jnp.int32, (1, blk), 1), cap).astype(jnp.float32)
    slot = lax.broadcasted_iota(jnp.int32, (blk, rows), 0)
    line = lax.broadcasted_iota(jnp.int32, (LABEL_ROWS, blk), 0)
    width = emb_ref.shape[1]
    leaving = []
    for n, k in enumerate(ks):
        pick = (slot + k * blk == dest).astype(jnp.float32).astype(jnp.bfloat16)
        stage[n, 0:blk, :] = jnp.dot(pick, unit, preferred_element_type=jnp.float32).astype(
            jnp.bfloat16
        )
        mine = lax.dot_general(labels, pick, NT, preferred_element_type=jnp.float32)
        high = unit_of + float(halves) * mine[1:2]
        strip = jnp.where(line == 0, mine[0:1], jnp.where(line == 1, high, 0.0))
        strip = jnp.concatenate([strip, jnp.zeros((LABEL_ROWS, width - blk), jnp.float32)], axis=1)
        stage[n, blk : blk + LABEL_ROWS, :] = strip.astype(jnp.bfloat16)
        leaving.append(pltpu.make_async_copy(stage.at[n], outs[n], out_sems.at[n]))
        leaving[-1].start()
    for copy in leaving:
        copy.wait()


def pack(embeddings, cluster, rank, ks, placed, sizes):
    groups, halves, half, cap, blk = sizes
    rows, width = embeddings.shape
    hbm = pl.BlockSpec(memory_space=pltpu.HBM)
    vmem = pl.BlockSpec(memory_space=pltpu.VMEM)
    out_shape = [jax.ShapeDtypeStruct((blk + LABEL_ROWS, width), jnp.bfloat16)] * len(ks)
    out_specs = [hbm] * len(ks)
    if placed:
        out_shape.append(jax.ShapeDtypeStruct((1, rows), jnp.int32))
        out_specs.append(vmem)
    return pl.pallas_call(
        functools.partial(pack_kernel, sizes, ks, placed),
        out_shape=out_shape,
        in_specs=[hbm, hbm, hbm],
        out_specs=out_specs,
        scratch_shapes=[
            pltpu.VMEM((rows, width), jnp.bfloat16),
            pltpu.VMEM((1, rows), jnp.int32),
            pltpu.VMEM((1, rows), jnp.int32),
            pltpu.VMEM((len(ks), blk + LABEL_ROWS, width), jnp.bfloat16),
            pltpu.SemaphoreType.DMA((2 + rows // 256,)),
            pltpu.SemaphoreType.DMA((len(ks),)),
        ],
        compiler_params=pltpu.CompilerParams(vmem_limit_bytes=PACK_VMEM),
        cost_estimate=pl.CostEstimate(
            flops=2 * len(ks) * blk * rows * width, bytes_accessed=4 * rows * width, transcendentals=0
        ),
    )(embeddings, cluster.reshape(1, rows), rank.reshape(1, rows))


def compare_kernel(sizes, jobs, names, spots, starts, joined, has_prev, *refs):
    groups, halves, half, cap, blk = sizes
    array = dict(zip(names, refs))
    refs = refs[len(names) :]
    block = {piece: (array[name], at * blk) for piece, (name, at) in spots.items()}
    prev = None
    if has_prev:
        prev, refs = refs[0], refs[1:]
    outs, (key_col, turned, best) = refs[:-3], refs[-3:]
    rows = groups * blk
    per_tile = blk // TILES
    tile = rows // TILES
    cap_all = float(halves * half)

    side = halves // 2 // groups
    along = lax.axis_index("mem")

    def strip_of(piece):
        ref, at = block[piece]
        first = ref.shape[0] - LABEL_ROWS
        return ref[first : first + LABEL_ROWS, at : at + blk]

    def keys_of(piece):
        strip = strip_of(piece).astype(jnp.float32)
        return strip[0:1] + float(half) * strip[1:2]

    weight_row = lax.broadcasted_iota(jnp.int32, (LABEL_ROWS, 128), 0)
    weights = jnp.where(weight_row == 0, 1.0, jnp.where(weight_row == 1, float(half), 0.0))
    weights = weights.astype(jnp.bfloat16)
    needed = sorted({piece for *_, pieces in jobs for piece in pieces})
    key_at = {piece: n * blk for n, piece in enumerate(needed)}
    for piece in needed:
        key_col[pl.ds(key_at[piece], blk), :] = lax.dot_general(
            strip_of(piece), weights, TN, preferred_element_type=jnp.float32
        )
    lane = lax.div(lax.broadcasted_iota(jnp.int32, (1, tile), 1), per_tile)

    def floor_of(key):
        low = jnp.floor(key * (1.0 / cap_all)) * cap_all
        return jnp.where(low > 0.5, low, FAR)

    def lines_of(a, ks):
        keys = [keys_of((a, k)) if k in ks else jnp.zeros((1, blk), jnp.float32) for k in range(groups)]
        keys = [jnp.concatenate([key] * (tile // blk), axis=1) for key in keys]
        lines = []
        for t in range(TILES):
            line = jnp.zeros((1, tile), jnp.float32)
            for k in range(groups):
                turn = ((k - t) * per_tile) % tile
                moved = pltpu.roll(keys[k], turn, 1) if turn else keys[k]
                line = jnp.where(lane == k, moved, line)
            lines.append(line)
        return lines

    def rows_of(ref, base, first, last):
        return ref[base + first * per_tile : base + last * per_tile, :]

    best[...] = prev[...] if has_prev else jnp.full(best.shape, -1.0, jnp.float32)

    def search(a, row, queries, mine, pieces, last, spot):
        width = mine.shape[1]
        turned[spot, :, 0:width] = jnp.concatenate(queries, axis=0).T
        floor = floor_of(mine)
        acc = jnp.full((8, width), -1.0, jnp.float32)
        for at in range(0, len(pieces), groups):
            some = pieces[at : at + groups]
            theirs = [rows_of(key_col, key_at[piece], 0, last) for piece in some]
            theirs = jnp.concatenate(theirs, axis=0)
            theirs = jnp.concatenate([theirs] * (width // 128), axis=1)
            sims = jnp.dot(
                jnp.concatenate([rows_of(*block[piece], 0, last) for piece in some], axis=0),
                turned[spot, :, 0:width],
                preferred_element_type=jnp.float32,
            )
            keep = (theirs >= floor) & (theirs < mine)
            sims = jnp.where(keep, sims, -1.0)
            top = jnp.max(sims.reshape(sims.shape[0] // 8, 8, width), axis=0)
            acc = jnp.maximum(acc, top)
        best[a, row : row + 1, 0:width] = jnp.maximum(
            best[a, row : row + 1, 0:width], jnp.max(acc, axis=0, keepdims=True)
        )

    spot = 0
    for a, whole, ks, pieces in jobs:
        if whole:
            (k,) = ks
            queries = [rows_of(*block[a, k], 0, TILES)]
            search(a, TILES, queries, keys_of((a, k)), pieces, TILES, spot)
            spot += 1
            continue
        lines = lines_of(a, ks)
        for t in range(TILES):
            queries = [rows_of(*block[a, k if k in ks else ks[0]], t, t + 1) for k in range(groups)]
            search(a, t, queries, lines[t], pieces, t + 1, spot)
            spot += 1

    if not starts:
        outs[0][...] = best[...]
        return
    for o, a in enumerate(starts):
        found = best[a]
        for k in range(groups):
            total = jnp.full((1, tile), -1.0, jnp.float32)
            for t in range(TILES):
                turn = ((t - k) * per_tile) % tile
                moved = pltpu.roll(found, turn, 1) if turn else found
                total = jnp.where(lane == t, moved[t : t + 1], total)
            if any(a == e and whole and k in ks for e, whole, ks, _ in jobs):
                total = jnp.maximum(total, found[TILES : TILES + 1])
            at = (along // side) ^ k
            if joined:
                outs[0][pl.ds(at * joined + ((along % side) ^ a), 1), 0, :] = total[:, :blk]
            else:
                outs[o][pl.ds(at, 1), 0, :] = total[:, :blk]


def compare(blocks, jobs, prev, starts, joined, offsets, sizes):
    groups, halves, half, cap, blk = sizes
    n_sets = len(offsets)
    used = {piece for *_, pieces in jobs for piece in pieces}
    used |= {(a, k) for a, _, ks, _ in jobs for k in ks}
    searches = sum(1 if whole else TILES for _, whole, _, _ in jobs)
    spots = {}
    arrays = {}
    for piece in sorted(used):
        value, at = blocks[piece]
        name = next((n for n, v in arrays.items() if v is value), None)
        if name is None:
            name = len(arrays)
            arrays[name] = value
        spots[piece] = (name, at)
    names = list(arrays)
    width = arrays[0].shape[1]
    tile = groups * blk // TILES
    vmem = pl.BlockSpec(memory_space=pltpu.VMEM)
    work = blk * tile * width * sum(
        len(pieces) * (1.0 if whole else (TILES + 1) / 2 / TILES) for _, whole, _, pieces in jobs
    )
    if not starts:
        out_shape = [jax.ShapeDtypeStruct((n_sets, 8, tile), jnp.float32)]
    elif joined:
        out_shape = [jax.ShapeDtypeStruct((groups * joined, 1, blk), jnp.float32)]
    else:
        out_shape = [jax.ShapeDtypeStruct((groups, 1, blk), jnp.float32)] * len(starts)
    operands = list(arrays.values()) + ([] if prev is None else [prev])
    needed = {piece for *_, pieces in jobs for piece in pieces}
    return pl.pallas_call(
        functools.partial(
            compare_kernel, sizes, jobs, names, spots, starts, joined, prev is not None
        ),
        out_shape=out_shape,
        in_specs=[vmem] * len(operands),
        out_specs=[vmem] * len(out_shape),
        scratch_shapes=[
            pltpu.VMEM((len(needed) * blk, 128), jnp.float32),
            pltpu.VMEM((searches, width, tile), jnp.bfloat16),
            pltpu.VMEM((n_sets, 8, tile), jnp.float32),
        ],
        compiler_params=pltpu.CompilerParams(vmem_limit_bytes=COMPARE_VMEM),
        cost_estimate=pl.CostEstimate(
            flops=int(2 * work), bytes_accessed=2 * len(used) * blk * width, transcendentals=0
        ),
    )(*operands)


def join_kernel(*refs):
    out_ref, ins = refs[-1], refs[:-1]
    blk, width = ins[0].shape[0] - LABEL_ROWS, ins[0].shape[1]
    parts = []
    for n, ref in enumerate(ins):
        out_ref[n * blk : (n + 1) * blk, :] = ref[0:blk, :]
        parts.append(ref[blk : blk + LABEL_ROWS, 0:blk])
    parts.append(jnp.zeros((LABEL_ROWS, width - len(ins) * blk), jnp.bfloat16))
    out_ref[len(ins) * blk :, :] = jnp.concatenate(parts, axis=1)


def join(pieces, flops):
    rows, width = pieces[0].shape
    total = len(pieces) * (rows - LABEL_ROWS) + LABEL_ROWS
    vmem = pl.BlockSpec(memory_space=pltpu.VMEM)
    return pl.pallas_call(
        join_kernel,
        out_shape=jax.ShapeDtypeStruct((total, width), pieces[0].dtype),
        in_specs=[vmem] * len(pieces),
        out_specs=vmem,
        compiler_params=pltpu.CompilerParams(vmem_limit_bytes=COMPARE_VMEM),
        cost_estimate=pl.CostEstimate(flops=flops, bytes_accessed=0, transcendentals=0),
    )(*pieces)


def unpack_kernel(sizes, dest_ref, back_ref, out_ref):
    groups, halves, half, cap, blk = sizes
    side = back_ref.shape[0] // groups
    rows = dest_ref.shape[1]
    dest = dest_ref[...]
    slot = lax.broadcasted_iota(jnp.int32, (blk, rows), 0)
    field = lax.broadcasted_iota(jnp.int32, (LABEL_ROWS, blk), 0)
    total = jnp.zeros((LABEL_ROWS, rows), jnp.float32)
    for k in range(groups):
        value = back_ref[k * side]
        for more in range(1, side):
            value = jnp.maximum(value, back_ref[k * side + more])
        top = value.astype(jnp.bfloat16).astype(jnp.float32)
        rest = value - top
        mid = rest.astype(jnp.bfloat16).astype(jnp.float32)
        low = rest - mid
        stack = jnp.where(field == 0, top, jnp.where(field == 1, mid, jnp.where(field == 2, low, 0.0)))
        pick = (slot + k * blk == dest).astype(jnp.float32).astype(jnp.bfloat16)
        total = total + jnp.dot(stack.astype(jnp.bfloat16), pick, preferred_element_type=jnp.float32)
    value = (total[0:1] + total[1:2]) + total[2:3]
    out_ref[...] = jnp.where(dest >= 0, value, -1.0)


def unpack(dest, back, sizes):
    vmem = pl.BlockSpec(memory_space=pltpu.VMEM)
    return pl.pallas_call(
        functools.partial(unpack_kernel, sizes),
        out_shape=jax.ShapeDtypeStruct(dest.shape, jnp.float32),
        in_specs=[vmem] * 2,
        out_specs=vmem,
        compiler_params=pltpu.CompilerParams(vmem_limit_bytes=COMPARE_VMEM),
    )(dest, back)


def on_device(embeddings, cluster, rank):
    rows_dev, width = embeddings.shape
    groups = lax.axis_size("grp")
    members = lax.axis_size("mem")
    devices = groups * members
    halves = 2 * members
    half = rows_dev // CLUS_GRP // 2
    blk = rows_dev // groups
    cap = blk // halves
    sizes = (groups, halves, half, cap, blk)
    side = members // groups

    def swap(value, block_step, member_step):
        mask = member_step // side * members + block_step * side + member_step % side
        if mask == 0:
            return value
        return lax.ppermute(value, ("grp", "mem"), [(i, i ^ mask) for i in range(devices)])

    offsets, pairs = cover(members)
    sends = [None] * groups
    first = tuple(range(1, min(3, groups)))
    for k, value in zip(first, pack(embeddings, cluster, rank, first, False, sizes)):
        sends[k] = value
    rest = tuple(k for k in range(groups) if k not in first)
    cluster, sends[1] = lax.optimization_barrier((cluster, sends[1]))
    *packed, dest = pack(embeddings, cluster, rank, rest, True, sizes)
    for k, value in zip(rest, packed):
        sends[k] = value

    last = groups - 1
    far = [d for d in offsets if d & side and d != side and d ^ side in offsets]
    near = [d for d in offsets[1:] if d not in far]
    lead = far[0] ^ side if far else near[0]
    held = {0: [sends[0]]}
    for d in near:
        held[d] = [swap(sends[0], 0, d)]
    for d in far:
        held[d] = [swap(held[d ^ side][0], 0, side)]
    after = held[lead][0]
    for k in range(1, groups, 2):
        if k > 1:
            send, after = lax.optimization_barrier((sends[k], after))
        else:
            send = sends[k]
        mine = swap(send, k, 0)
        if k < last:
            also = swap(sends[k + 1], k + 1, 0)
            if k == 1:
                mine, also, *firsts = lax.optimization_barrier(
                    (mine, also, *(held[d][0] for d in near))
                )
                for d, value in zip(near, firsts):
                    held[d] = [value]
            mine = join([mine, also], 0)
            after = mine
        else:
            mine = join([mine], WANTED)
        held[0].append(mine)
        for d in near:
            held[d].append(swap(mine, 0, d))
    for spot in range(1, len(held[0]) - 1):
        held[0][spot + 1], *values = lax.optimization_barrier(
            (held[0][spot + 1], *(held[d][0] for d in far), *(held[d][spot] for d in near))
        )
        for d in far:
            held[d][0] = values.pop(0)
        for d, value in zip(near, values):
            held[d][spot] = value
    for d in far:
        for spot in range(1, len(held[0]) - 1):
            held[d].append(swap(held[d ^ side][spot], 0, side))

    index = {d: i for i, d in enumerate(offsets)}
    blocks = {}

    def note():
        for d in offsets:
            for spot, value in enumerate(held[d]):
                ks = [0] if spot == 0 else [k for k in (2 * spot - 1, 2 * spot) if k < groups]
                for at, k in enumerate(ks):
                    blocks[index[d], k] = (value, at)

    note()
    starts = sorted({a for a, _ in pairs.values()})
    every = tuple(range(groups))
    early, middle, late = [], [], []
    for a in starts:
        cols = [index[b] for _, (e, b) in sorted(pairs.items()) if e == a]
        pieces = [(b, k) for b in cols for k in every]
        soon = [(b, k) for b, k in pieces if k < last]
        if a == 0:
            slow = {(index[d], k) for d in far for k in range(1, last)} | {(index[side], last)}
            ready = [piece for piece in pieces if piece in soon or piece[0] == 0]
            early.append((0, False, every, [piece for piece in ready if piece not in slow]))
            middle.append((0, False, every, [piece for piece in pieces if piece in slow]))
            done = early[-1][-1] + middle[-1][-1]
            late.append((0, False, every, [piece for piece in pieces if piece not in done]))
        else:
            middle.append((index[a], False, every[:-1], soon))
            late.append((index[a], False, every, [piece for piece in pieces if piece not in soon]))
            late.append((index[a], True, (last,), soon))
    order = [index[a] for a in starts]
    joined = side if all(a < side for a in starts) else 0
    prev = compare(blocks, early, None, (), 0, offsets, sizes)[0]
    prev = compare(blocks, middle, prev, (), 0, offsets, sizes)[0]
    for d in far:
        piece, prev = lax.optimization_barrier((held[d ^ side][-1], prev))
        held[d].append(swap(piece, 0, side))
    note()
    found = compare(blocks, late, prev, order, joined, offsets, sizes)
    if joined:
        back = found[0]
    else:
        best = {}
        for a, value in zip(starts, found):
            near = a % side
            value = swap(value, 0, a - near)
            best[near] = jnp.maximum(best[near], value) if near in best else value
        none = jnp.full_like(found[0], -1.0)
        near_of = [best.get(near, none) for near in range(side)]
        rows_of = []
        for spot in range(side):
            value = near_of[spot]
            for mine in range(1, side):
                value = jnp.where(lax.axis_index("mem") % side == mine, near_of[spot ^ mine], value)
            rows_of.append(value)
        back = jnp.stack(rows_of, axis=1).reshape(groups * side, 1, blk)
    back = lax.all_to_all(back, "mem", split_axis=0, concat_axis=0, tiled=True)
    return unpack(dest, back, sizes).reshape(rows_dev)


def solution(mesh):
    in_specs = (P(("grp", "mem"), None), P(("grp", "mem")), P(("grp", "mem")))
    out_specs = P(("grp", "mem"))
    return jax.shard_map(
        on_device, mesh=mesh, in_specs=in_specs, out_specs=out_specs, check_vma=False
    )
```

```python
import functools

import jax
import jax.numpy as jnp
from jax import lax
from jax.experimental import pallas as pl
from jax.experimental.pallas import tpu as pltpu
from jax.sharding import PartitionSpec as P

CLUS_GRP = 2
TILES = 4
LABEL_ROWS = 16
FAR = 1.0e9
WANTED = 20_000_000_000
PACK_VMEM = 60 * 1024 * 1024
COMPARE_VMEM = 24 * 1024 * 1024
NT = (((1,), (1,)), ((), ()))
TN = (((0,), (0,)), ((), ()))


def cover(members):
    bits = [1 << i for i in range(members.bit_length() - 1)]
    offsets = [0] + bits

    def missing(held):
        return set(range(members)) - {a ^ b for a in held for b in held}

    while missing(offsets):
        offsets.append(
            min(
                (d for d in range(members) if d not in offsets),
                key=lambda d: (len(missing(offsets + [d])), bin(d).count("1"), -d),
            )
        )
    pairs = {}
    for delta in range(members):
        pairs[delta] = min(
            (a, a ^ delta) for a in offsets if a ^ delta in offsets
        )
    return offsets, pairs


def pack_kernel(sizes, ks, placed, emb_hbm, cluster_hbm, rank_hbm, *refs):
    groups, halves, half, cap, blk = sizes
    outs, refs = refs[: len(ks)], refs[len(ks) :]
    if placed:
        dest_ref, *refs = refs
    emb_ref, cluster_ref, rank_ref, stage, sems, out_sems = refs
    rows = emb_ref.shape[0]
    step = 256
    loads = [
        pltpu.make_async_copy(cluster_hbm, cluster_ref, sems.at[0]),
        pltpu.make_async_copy(rank_hbm, rank_ref, sems.at[1]),
    ]
    for j in range(rows // step):
        at = pl.ds(j * step, step)
        loads.append(pltpu.make_async_copy(emb_hbm.at[at], emb_ref.at[at], sems.at[2 + j]))
    for load in loads:
        load.start()
    for load in loads[:2]:
        load.wait()
    cluster = cluster_ref[...]
    rank = rank_ref[...]
    alive = cluster >= 0
    pair = lax.shift_right_logical(jnp.maximum(cluster, 0), 1)
    parity = jnp.maximum(cluster, 0) - 2 * pair
    safe_rank = jnp.maximum(rank, 0)
    which = safe_rank // half
    units = groups * halves
    unit_id = jnp.where(alive, pair * halves + which, -1)
    before_rows = lax.broadcasted_iota(jnp.int32, (step, step), 0)
    before_cols = lax.broadcasted_iota(jnp.int32, (step, step), 1)
    upper = (before_rows < before_cols).astype(jnp.float32).astype(jnp.bfloat16)
    unit_iota = lax.broadcasted_iota(jnp.int32, (units, step), 0)
    carry = jnp.zeros((units, 1), jnp.float32)
    places = []
    for j in range(rows // step):
        mine = unit_id[:, j * step : (j + 1) * step]
        hit = (unit_iota == mine).astype(jnp.float32)
        before = jnp.dot(hit.astype(jnp.bfloat16), upper, preferred_element_type=jnp.float32) + carry
        position = jnp.sum(hit * before, axis=0, keepdims=True)
        carry = carry + jnp.sum(hit, axis=1, keepdims=True)
        places.append(jnp.where(mine >= 0, mine * cap + position.astype(jnp.int32), -1))
    dest = jnp.concatenate(places, axis=1)
    if placed:
        dest_ref[...] = dest
    members = halves // 2
    side = members // groups
    here = lax.axis_index("mem") // side
    dest = jnp.where(dest >= 0, dest ^ (here * blk), -1)

    units_of = []
    for j in range(rows // step):
        loads[2 + j].wait()
        wide = emb_ref[j * step : (j + 1) * step, :].astype(jnp.float32)
        total = jnp.sum(wide * wide, axis=1, keepdims=True)
        units_of.append((wide * lax.rsqrt(total + 1e-06)).astype(jnp.bfloat16))
    unit = jnp.concatenate(units_of, axis=0)

    field = lax.broadcasted_iota(jnp.int32, (LABEL_ROWS, rows), 0)
    labels = jnp.where(
        field == 0, safe_rank - which * half, jnp.where(field == 1, parity + 1, 0)
    )
    labels = jnp.where(alive, labels, 0).astype(jnp.float32).astype(jnp.bfloat16)
    unit_of = lax.div(lax.broadcasted_iota(jnp.int32, (1, blk), 1), cap).astype(jnp.float32)
    slot = lax.broadcasted_iota(jnp.int32, (blk, rows), 0)
    line = lax.broadcasted_iota(jnp.int32, (LABEL_ROWS, blk), 0)
    width = emb_ref.shape[1]
    leaving = []
    for n, k in enumerate(ks):
        pick = (slot + k * blk == dest).astype(jnp.float32).astype(jnp.bfloat16)
        stage[n, 0:blk, :] = jnp.dot(pick, unit, preferred_element_type=jnp.float32).astype(
            jnp.bfloat16
        )
        mine = lax.dot_general(labels, pick, NT, preferred_element_type=jnp.float32)
        high = unit_of + float(halves) * mine[1:2]
        strip = jnp.where(line == 0, mine[0:1], jnp.where(line == 1, high, 0.0))
        strip = jnp.concatenate([strip, jnp.zeros((LABEL_ROWS, width - blk), jnp.float32)], axis=1)
        stage[n, blk : blk + LABEL_ROWS, :] = strip.astype(jnp.bfloat16)
        leaving.append(pltpu.make_async_copy(stage.at[n], outs[n], out_sems.at[n]))
        leaving[-1].start()
    for copy in leaving:
        copy.wait()


def pack(embeddings, cluster, rank, ks, placed, sizes):
    groups, halves, half, cap, blk = sizes
    rows, width = embeddings.shape
    hbm = pl.BlockSpec(memory_space=pltpu.HBM)
    vmem = pl.BlockSpec(memory_space=pltpu.VMEM)
    out_shape = [jax.ShapeDtypeStruct((blk + LABEL_ROWS, width), jnp.bfloat16)] * len(ks)
    out_specs = [hbm] * len(ks)
    if placed:
        out_shape.append(jax.ShapeDtypeStruct((1, rows), jnp.int32))
        out_specs.append(vmem)
    return pl.pallas_call(
        functools.partial(pack_kernel, sizes, ks, placed),
        out_shape=out_shape,
        in_specs=[hbm, hbm, hbm],
        out_specs=out_specs,
        scratch_shapes=[
            pltpu.VMEM((rows, width), jnp.bfloat16),
            pltpu.VMEM((1, rows), jnp.int32),
            pltpu.VMEM((1, rows), jnp.int32),
            pltpu.VMEM((len(ks), blk + LABEL_ROWS, width), jnp.bfloat16),
            pltpu.SemaphoreType.DMA((2 + rows // 256,)),
            pltpu.SemaphoreType.DMA((len(ks),)),
        ],
        compiler_params=pltpu.CompilerParams(vmem_limit_bytes=PACK_VMEM),
        cost_estimate=pl.CostEstimate(
            flops=2 * len(ks) * blk * rows * width, bytes_accessed=4 * rows * width, transcendentals=0
        ),
    )(embeddings, cluster.reshape(1, rows), rank.reshape(1, rows))


def compare_kernel(sizes, jobs, names, spots, starts, joined, has_prev, *refs):
    groups, halves, half, cap, blk = sizes
    array = dict(zip(names, refs))
    refs = refs[len(names) :]
    block = {piece: (array[name], at * blk) for piece, (name, at) in spots.items()}
    prev = None
    if has_prev:
        prev, refs = refs[0], refs[1:]
    outs, (key_col, turned, best) = refs[:-3], refs[-3:]
    rows = groups * blk
    per_tile = blk // TILES
    tile = rows // TILES
    cap_all = float(halves * half)

    side = halves // 2 // groups
    along = lax.axis_index("mem")

    def strip_of(piece):
        ref, at = block[piece]
        first = ref.shape[0] - LABEL_ROWS
        return ref[first : first + LABEL_ROWS, at : at + blk]

    def keys_of(piece):
        strip = strip_of(piece).astype(jnp.float32)
        return strip[0:1] + float(half) * strip[1:2]

    weight_row = lax.broadcasted_iota(jnp.int32, (LABEL_ROWS, 128), 0)
    weights = jnp.where(weight_row == 0, 1.0, jnp.where(weight_row == 1, float(half), 0.0))
    weights = weights.astype(jnp.bfloat16)
    needed = sorted({piece for *_, pieces in jobs for piece in pieces})
    key_at = {piece: n * blk for n, piece in enumerate(needed)}
    for piece in needed:
        key_col[pl.ds(key_at[piece], blk), :] = lax.dot_general(
            strip_of(piece), weights, TN, preferred_element_type=jnp.float32
        )
    lane = lax.div(lax.broadcasted_iota(jnp.int32, (1, tile), 1), per_tile)

    def floor_of(key):
        low = jnp.floor(key * (1.0 / cap_all)) * cap_all
        return jnp.where(low > 0.5, low, FAR)

    def lines_of(a, ks):
        keys = [keys_of((a, k)) if k in ks else jnp.zeros((1, blk), jnp.float32) for k in range(groups)]
        keys = [jnp.concatenate([key] * (tile // blk), axis=1) for key in keys]
        lines = []
        for t in range(TILES):
            line = jnp.zeros((1, tile), jnp.float32)
            for k in range(groups):
                turn = ((k - t) * per_tile) % tile
                moved = pltpu.roll(keys[k], turn, 1) if turn else keys[k]
                line = jnp.where(lane == k, moved, line)
            lines.append(line)
        return lines

    def rows_of(ref, base, first, last):
        return ref[base + first * per_tile : base + last * per_tile, :]

    best[...] = prev[...] if has_prev else jnp.full(best.shape, -1.0, jnp.float32)

    def search(a, row, queries, mine, pieces, last, spot):
        width = mine.shape[1]
        turned[spot, :, 0:width] = jnp.concatenate(queries, axis=0).T
        floor = floor_of(mine)
        acc = jnp.full((8, width), -1.0, jnp.float32)
        for at in range(0, len(pieces), groups):
            some = pieces[at : at + groups]
            theirs = [rows_of(key_col, key_at[piece], 0, last) for piece in some]
            theirs = jnp.concatenate(theirs, axis=0)
            theirs = jnp.concatenate([theirs] * (width // 128), axis=1)
            sims = jnp.dot(
                jnp.concatenate([rows_of(*block[piece], 0, last) for piece in some], axis=0),
                turned[spot, :, 0:width],
                preferred_element_type=jnp.float32,
            )
            keep = (theirs >= floor) & (theirs < mine)
            sims = jnp.where(keep, sims, -1.0)
            top = jnp.max(sims.reshape(sims.shape[0] // 8, 8, width), axis=0)
            acc = jnp.maximum(acc, top)
        best[a, row : row + 1, 0:width] = jnp.maximum(
            best[a, row : row + 1, 0:width], jnp.max(acc, axis=0, keepdims=True)
        )

    spot = 0
    for a, whole, ks, pieces in jobs:
        if whole:
            (k,) = ks
            queries = [rows_of(*block[a, k], 0, TILES)]
            search(a, TILES, queries, keys_of((a, k)), pieces, TILES, spot)
            spot += 1
            continue
        lines = lines_of(a, ks)
        for t in range(TILES):
            queries = [rows_of(*block[a, k if k in ks else ks[0]], t, t + 1) for k in range(groups)]
            search(a, t, queries, lines[t], pieces, t + 1, spot)
            spot += 1

    if not starts:
        outs[0][...] = best[...]
        return
    for o, a in enumerate(starts):
        found = best[a]
        for k in range(groups):
            total = jnp.full((1, tile), -1.0, jnp.float32)
            for t in range(TILES):
                turn = ((t - k) * per_tile) % tile
                moved = pltpu.roll(found, turn, 1) if turn else found
                total = jnp.where(lane == t, moved[t : t + 1], total)
            if any(a == e and whole and k in ks for e, whole, ks, _ in jobs):
                total = jnp.maximum(total, found[TILES : TILES + 1])
            at = (along // side) ^ k
            if joined:
                outs[0][pl.ds(at * joined + ((along % side) ^ a), 1), 0, :] = total[:, :blk]
            else:
                outs[o][pl.ds(at, 1), 0, :] = total[:, :blk]


def compare(blocks, jobs, prev, starts, joined, offsets, sizes):
    groups, halves, half, cap, blk = sizes
    n_sets = len(offsets)
    used = {piece for *_, pieces in jobs for piece in pieces}
    used |= {(a, k) for a, _, ks, _ in jobs for k in ks}
    searches = sum(1 if whole else TILES for _, whole, _, _ in jobs)
    spots = {}
    arrays = {}
    for piece in sorted(used):
        value, at = blocks[piece]
        name = next((n for n, v in arrays.items() if v is value), None)
        if name is None:
            name = len(arrays)
            arrays[name] = value
        spots[piece] = (name, at)
    names = list(arrays)
    width = arrays[0].shape[1]
    tile = groups * blk // TILES
    vmem = pl.BlockSpec(memory_space=pltpu.VMEM)
    work = blk * tile * width * sum(
        len(pieces) * (1.0 if whole else (TILES + 1) / 2 / TILES) for _, whole, _, pieces in jobs
    )
    if not starts:
        out_shape = [jax.ShapeDtypeStruct((n_sets, 8, tile), jnp.float32)]
    elif joined:
        out_shape = [jax.ShapeDtypeStruct((groups * joined, 1, blk), jnp.float32)]
    else:
        out_shape = [jax.ShapeDtypeStruct((groups, 1, blk), jnp.float32)] * len(starts)
    operands = list(arrays.values()) + ([] if prev is None else [prev])
    needed = {piece for *_, pieces in jobs for piece in pieces}
    return pl.pallas_call(
        functools.partial(
            compare_kernel, sizes, jobs, names, spots, starts, joined, prev is not None
        ),
        out_shape=out_shape,
        in_specs=[vmem] * len(operands),
        out_specs=[vmem] * len(out_shape),
        scratch_shapes=[
            pltpu.VMEM((len(needed) * blk, 128), jnp.float32),
            pltpu.VMEM((searches, width, tile), jnp.bfloat16),
            pltpu.VMEM((n_sets, 8, tile), jnp.float32),
        ],
        compiler_params=pltpu.CompilerParams(vmem_limit_bytes=COMPARE_VMEM),
        cost_estimate=pl.CostEstimate(
            flops=int(2 * work), bytes_accessed=2 * len(used) * blk * width, transcendentals=0
        ),
    )(*operands)


def join_kernel(*refs):
    out_ref, ins = refs[-1], refs[:-1]
    blk, width = ins[0].shape[0] - LABEL_ROWS, ins[0].shape[1]
    parts = []
    for n, ref in enumerate(ins):
        out_ref[n * blk : (n + 1) * blk, :] = ref[0:blk, :]
        parts.append(ref[blk : blk + LABEL_ROWS, 0:blk])
    parts.append(jnp.zeros((LABEL_ROWS, width - len(ins) * blk), jnp.bfloat16))
    out_ref[len(ins) * blk :, :] = jnp.concatenate(parts, axis=1)


def join(pieces, flops):
    rows, width = pieces[0].shape
    total = len(pieces) * (rows - LABEL_ROWS) + LABEL_ROWS
    vmem = pl.BlockSpec(memory_space=pltpu.VMEM)
    return pl.pallas_call(
        join_kernel,
        out_shape=jax.ShapeDtypeStruct((total, width), pieces[0].dtype),
        in_specs=[vmem] * len(pieces),
        out_specs=vmem,
        compiler_params=pltpu.CompilerParams(vmem_limit_bytes=COMPARE_VMEM),
        cost_estimate=pl.CostEstimate(flops=flops, bytes_accessed=0, transcendentals=0),
    )(*pieces)


def unpack_kernel(sizes, dest_ref, back_ref, out_ref):
    groups, halves, half, cap, blk = sizes
    side = back_ref.shape[0] // groups
    rows = dest_ref.shape[1]
    dest = dest_ref[...]
    slot = lax.broadcasted_iota(jnp.int32, (blk, rows), 0)
    field = lax.broadcasted_iota(jnp.int32, (LABEL_ROWS, blk), 0)
    total = jnp.zeros((LABEL_ROWS, rows), jnp.float32)
    for k in range(groups):
        value = back_ref[k * side]
        for more in range(1, side):
            value = jnp.maximum(value, back_ref[k * side + more])
        top = value.astype(jnp.bfloat16).astype(jnp.float32)
        rest = value - top
        mid = rest.astype(jnp.bfloat16).astype(jnp.float32)
        low = rest - mid
        stack = jnp.where(field == 0, top, jnp.where(field == 1, mid, jnp.where(field == 2, low, 0.0)))
        pick = (slot + k * blk == dest).astype(jnp.float32).astype(jnp.bfloat16)
        total = total + jnp.dot(stack.astype(jnp.bfloat16), pick, preferred_element_type=jnp.float32)
    value = (total[0:1] + total[1:2]) + total[2:3]
    out_ref[...] = jnp.where(dest >= 0, value, -1.0)


def unpack(dest, back, sizes):
    vmem = pl.BlockSpec(memory_space=pltpu.VMEM)
    return pl.pallas_call(
        functools.partial(unpack_kernel, sizes),
        out_shape=jax.ShapeDtypeStruct(dest.shape, jnp.float32),
        in_specs=[vmem] * 2,
        out_specs=vmem,
        compiler_params=pltpu.CompilerParams(vmem_limit_bytes=COMPARE_VMEM),
    )(dest, back)


def on_device(embeddings, cluster, rank):
    rows_dev, width = embeddings.shape
    groups = lax.axis_size("grp")
    members = lax.axis_size("mem")
    devices = groups * members
    halves = 2 * members
    half = rows_dev // CLUS_GRP // 2
    blk = rows_dev // groups
    cap = blk // halves
    sizes = (groups, halves, half, cap, blk)
    side = members // groups

    def swap(value, block_step, member_step):
        mask = member_step // side * members + block_step * side + member_step % side
        if mask == 0:
            return value
        return lax.ppermute(value, ("grp", "mem"), [(i, i ^ mask) for i in range(devices)])

    offsets, pairs = cover(members)
    sends = [None] * groups
    first = tuple(range(1, min(3, groups)))
    for k, value in zip(first, pack(embeddings, cluster, rank, first, False, sizes)):
        sends[k] = value
    rest = tuple(k for k in range(groups) if k not in first)
    cluster, sends[1] = lax.optimization_barrier((cluster, sends[1]))
    *packed, dest = pack(embeddings, cluster, rank, rest, True, sizes)
    for k, value in zip(rest, packed):
        sends[k] = value

    last = groups - 1
    far = [d for d in offsets if d & side and d != side and d ^ side in offsets]
    near = [d for d in offsets[1:] if d not in far]
    lead = far[0] ^ side if far else near[0]
    held = {0: [sends[0]]}
    for d in near:
        held[d] = [swap(sends[0], 0, d)]
    after = held[lead][0]
    for k in range(1, groups, 2):
        if k > 1:
            send, after = lax.optimization_barrier((sends[k], after))
        else:
            send = sends[k]
        mine = swap(send, k, 0)
        if k < last:
            also = swap(sends[k + 1], k + 1, 0)
            if k == 1:
                mine, also, *firsts = lax.optimization_barrier(
                    (mine, also, *(held[d][0] for d in near))
                )
                for d, value in zip(near, firsts):
                    held[d] = [value]
            mine = join([mine, also], 0)
            after = mine
        else:
            mine = join([mine], WANTED)
        held[0].append(mine)
    spots = len(held[0])
    for spot in range(1, spots):
        for d in near:
            if d != side:
                held[d].append(swap(held[0][spot], 0, d))
    end, side_hop = held[0][-1], held[near[0]]
    for spot in range(1, spots):
        piece, end = lax.optimization_barrier((held[0][spot], end))
        if spot == spots - 1:
            piece, side_hop[spot - 1] = lax.optimization_barrier((piece, side_hop[spot - 1]))
        held[side].append(swap(piece, 0, side))
    for d in far:
        held[d] = []
        for spot in range(spots - 1):
            piece, side_hop[spots - 2] = lax.optimization_barrier(
                (held[d ^ side][spot], side_hop[spots - 2])
            )
            held[d].append(swap(piece, 0, side))

    index = {d: i for i, d in enumerate(offsets)}
    blocks = {}

    def note():
        for d in offsets:
            for spot, value in enumerate(held[d]):
                ks = [0] if spot == 0 else [k for k in (2 * spot - 1, 2 * spot) if k < groups]
                for at, k in enumerate(ks):
                    blocks[index[d], k] = (value, at)

    note()
    starts = sorted({a for a, _ in pairs.values()})
    every = tuple(range(groups))
    early, middle, late = [], [], []
    for a in starts:
        cols = [index[b] for _, (e, b) in sorted(pairs.items()) if e == a]
        pieces = [(b, k) for b in cols for k in every]
        soon = [(b, k) for b, k in pieces if k < last]
        if a == 0:
            slow = {(index[d], k) for d in far for k in range(last)} | {(index[side], last)}
            ready = [piece for piece in pieces if piece in soon or piece[0] == 0]
            early.append((0, False, every, [piece for piece in ready if piece not in slow]))
            middle.append((0, False, every, [piece for piece in pieces if piece in slow]))
            done = early[-1][-1] + middle[-1][-1]
            late.append((0, False, every, [piece for piece in pieces if piece not in done]))
        else:
            middle.append((index[a], False, every[:-1], soon))
            late.append((index[a], False, every, [piece for piece in pieces if piece not in soon]))
            late.append((index[a], True, (last,), soon))
    order = [index[a] for a in starts]
    joined = side if all(a < side for a in starts) else 0
    prev = compare(blocks, early, None, (), 0, offsets, sizes)[0]
    prev = compare(blocks, middle, prev, (), 0, offsets, sizes)[0]
    for d in far:
        piece, prev = lax.optimization_barrier((held[d ^ side][-1], prev))
        held[d].append(swap(piece, 0, side))
    note()
    found = compare(blocks, late, prev, order, joined, offsets, sizes)
    if joined:
        back = found[0]
    else:
        best = {}
        for a, value in zip(starts, found):
            near = a % side
            value = swap(value, 0, a - near)
            best[near] = jnp.maximum(best[near], value) if near in best else value
        none = jnp.full_like(found[0], -1.0)
        near_of = [best.get(near, none) for near in range(side)]
        rows_of = []
        for spot in range(side):
            value = near_of[spot]
            for mine in range(1, side):
                value = jnp.where(lax.axis_index("mem") % side == mine, near_of[spot ^ mine], value)
            rows_of.append(value)
        back = jnp.stack(rows_of, axis=1).reshape(groups * side, 1, blk)
    back = lax.all_to_all(back, "mem", split_axis=0, concat_axis=0, tiled=True)
    return unpack(dest, back, sizes).reshape(rows_dev)


def solution(mesh):
    in_specs = (P(("grp", "mem"), None), P(("grp", "mem")), P(("grp", "mem")))
    out_specs = P(("grp", "mem"))
    return jax.shard_map(
        on_device, mesh=mesh, in_specs=in_specs, out_specs=out_specs, check_vma=False
    )
```

```python
import functools

import jax
import jax.numpy as jnp
from jax import lax
from jax.experimental import pallas as pl
from jax.experimental.pallas import tpu as pltpu
from jax.sharding import PartitionSpec as P

CLUS_GRP = 2
TILES = 4
LABEL_ROWS = 16
FAR = 1.0e9
PACK_VMEM = 60 * 1024 * 1024
COMPARE_VMEM = 24 * 1024 * 1024
NT = (((1,), (1,)), ((), ()))
TN = (((0,), (0,)), ((), ()))


def cover(members):
    bits = [1 << i for i in range(members.bit_length() - 1)]
    offsets = [0] + bits

    def missing(held):
        return set(range(members)) - {a ^ b for a in held for b in held}

    while missing(offsets):
        offsets.append(
            min(
                (d for d in range(members) if d not in offsets),
                key=lambda d: (len(missing(offsets + [d])), bin(d).count("1"), -d),
            )
        )
    pairs = {}
    for delta in range(members):
        pairs[delta] = min(
            (a, a ^ delta) for a in offsets if a ^ delta in offsets
        )
    return offsets, pairs


def pack_kernel(sizes, ks, placed, emb_hbm, cluster_hbm, rank_hbm, *refs):
    groups, halves, half, cap, blk = sizes
    outs, refs = refs[: len(ks)], refs[len(ks) :]
    if placed:
        dest_ref, *refs = refs
    emb_ref, cluster_ref, rank_ref, stage, sems, out_sems = refs
    rows = emb_ref.shape[0]
    step = 256
    loads = [
        pltpu.make_async_copy(cluster_hbm, cluster_ref, sems.at[0]),
        pltpu.make_async_copy(rank_hbm, rank_ref, sems.at[1]),
    ]
    for j in range(rows // step):
        at = pl.ds(j * step, step)
        loads.append(pltpu.make_async_copy(emb_hbm.at[at], emb_ref.at[at], sems.at[2 + j]))
    for load in loads:
        load.start()
    for load in loads[:2]:
        load.wait()
    cluster = cluster_ref[...]
    rank = rank_ref[...]
    alive = cluster >= 0
    pair = lax.shift_right_logical(jnp.maximum(cluster, 0), 1)
    parity = jnp.maximum(cluster, 0) - 2 * pair
    safe_rank = jnp.maximum(rank, 0)
    which = safe_rank // half
    units = groups * halves
    unit_id = jnp.where(alive, pair * halves + which, -1)
    before_rows = lax.broadcasted_iota(jnp.int32, (step, step), 0)
    before_cols = lax.broadcasted_iota(jnp.int32, (step, step), 1)
    upper = (before_rows < before_cols).astype(jnp.float32).astype(jnp.bfloat16)
    unit_iota = lax.broadcasted_iota(jnp.int32, (units, step), 0)
    carry = jnp.zeros((units, 1), jnp.float32)
    places = []
    for j in range(rows // step):
        mine = unit_id[:, j * step : (j + 1) * step]
        hit = (unit_iota == mine).astype(jnp.float32)
        before = jnp.dot(hit.astype(jnp.bfloat16), upper, preferred_element_type=jnp.float32) + carry
        position = jnp.sum(hit * before, axis=0, keepdims=True)
        carry = carry + jnp.sum(hit, axis=1, keepdims=True)
        places.append(jnp.where(mine >= 0, mine * cap + position.astype(jnp.int32), -1))
    dest = jnp.concatenate(places, axis=1)
    if placed:
        dest_ref[...] = dest
    members = halves // 2
    side = members // groups
    here = lax.axis_index("mem") // side
    dest = jnp.where(dest >= 0, dest ^ (here * blk), -1)

    units_of = []
    for j in range(rows // step):
        loads[2 + j].wait()
        wide = emb_ref[j * step : (j + 1) * step, :].astype(jnp.float32)
        total = jnp.sum(wide * wide, axis=1, keepdims=True)
        units_of.append((wide * lax.rsqrt(total + 1e-06)).astype(jnp.bfloat16))
    unit = jnp.concatenate(units_of, axis=0)

    field = lax.broadcasted_iota(jnp.int32, (LABEL_ROWS, rows), 0)
    labels = jnp.where(
        field == 0, safe_rank - which * half, jnp.where(field == 1, parity + 1, 0)
    )
    labels = jnp.where(alive, labels, 0).astype(jnp.float32).astype(jnp.bfloat16)
    unit_of = lax.div(lax.broadcasted_iota(jnp.int32, (1, blk), 1), cap).astype(jnp.float32)
    slot = lax.broadcasted_iota(jnp.int32, (blk, rows), 0)
    line = lax.broadcasted_iota(jnp.int32, (LABEL_ROWS, blk), 0)
    width = emb_ref.shape[1]
    leaving = []
    for n, k in enumerate(ks):
        pick = (slot + k * blk == dest).astype(jnp.float32).astype(jnp.bfloat16)
        stage[n, 0:blk, :] = jnp.dot(pick, unit, preferred_element_type=jnp.float32).astype(
            jnp.bfloat16
        )
        mine = lax.dot_general(labels, pick, NT, preferred_element_type=jnp.float32)
        high = unit_of + float(halves) * mine[1:2]
        strip = jnp.where(line == 0, mine[0:1], jnp.where(line == 1, high, 0.0))
        strip = jnp.concatenate([strip, jnp.zeros((LABEL_ROWS, width - blk), jnp.float32)], axis=1)
        stage[n, blk : blk + LABEL_ROWS, :] = strip.astype(jnp.bfloat16)
        leaving.append(pltpu.make_async_copy(stage.at[n], outs[n], out_sems.at[n]))
        leaving[-1].start()
    for copy in leaving:
        copy.wait()


def pack(embeddings, cluster, rank, ks, placed, sizes):
    groups, halves, half, cap, blk = sizes
    rows, width = embeddings.shape
    hbm = pl.BlockSpec(memory_space=pltpu.HBM)
    vmem = pl.BlockSpec(memory_space=pltpu.VMEM)
    out_shape = [jax.ShapeDtypeStruct((blk + LABEL_ROWS, width), jnp.bfloat16)] * len(ks)
    out_specs = [hbm] * len(ks)
    if placed:
        out_shape.append(jax.ShapeDtypeStruct((1, rows), jnp.int32))
        out_specs.append(vmem)
    return pl.pallas_call(
        functools.partial(pack_kernel, sizes, ks, placed),
        out_shape=out_shape,
        in_specs=[hbm, hbm, hbm],
        out_specs=out_specs,
        scratch_shapes=[
            pltpu.VMEM((rows, width), jnp.bfloat16),
            pltpu.VMEM((1, rows), jnp.int32),
            pltpu.VMEM((1, rows), jnp.int32),
            pltpu.VMEM((len(ks), blk + LABEL_ROWS, width), jnp.bfloat16),
            pltpu.SemaphoreType.DMA((2 + rows // 256,)),
            pltpu.SemaphoreType.DMA((len(ks),)),
        ],
        compiler_params=pltpu.CompilerParams(vmem_limit_bytes=PACK_VMEM),
        cost_estimate=pl.CostEstimate(
            flops=2 * len(ks) * blk * rows * width, bytes_accessed=4 * rows * width, transcendentals=0
        ),
    )(embeddings, cluster.reshape(1, rows), rank.reshape(1, rows))


def compare_kernel(sizes, jobs, names, spots, starts, joined, has_prev, *refs):
    groups, halves, half, cap, blk = sizes
    array = dict(zip(names, refs))
    refs = refs[len(names) :]
    block = {piece: (array[name], row) for piece, (name, row, _, _) in spots.items()}
    prev = None
    if has_prev:
        prev, refs = refs[0], refs[1:]
    outs, (key_col, turned, best) = refs[:-3], refs[-3:]
    rows = groups * blk
    per_tile = blk // TILES
    tile = rows // TILES
    cap_all = float(halves * half)

    side = halves // 2 // groups
    along = lax.axis_index("mem")

    def strip_of(piece):
        name, _, first, left = spots[piece]
        return array[name][first : first + LABEL_ROWS, left : left + blk]

    def keys_of(piece):
        strip = strip_of(piece).astype(jnp.float32)
        return strip[0:1] + float(half) * strip[1:2]

    weight_row = lax.broadcasted_iota(jnp.int32, (LABEL_ROWS, 128), 0)
    weights = jnp.where(weight_row == 0, 1.0, jnp.where(weight_row == 1, float(half), 0.0))
    weights = weights.astype(jnp.bfloat16)
    needed = sorted({piece for *_, pieces in jobs for piece in pieces})
    key_at = {piece: n * blk for n, piece in enumerate(needed)}
    for piece in needed:
        key_col[pl.ds(key_at[piece], blk), :] = lax.dot_general(
            strip_of(piece), weights, TN, preferred_element_type=jnp.float32
        )
    lane = lax.div(lax.broadcasted_iota(jnp.int32, (1, tile), 1), per_tile)

    def floor_of(key):
        low = jnp.floor(key * (1.0 / cap_all)) * cap_all
        return jnp.where(low > 0.5, low, FAR)

    def lines_of(a, ks):
        keys = [keys_of((a, k)) if k in ks else jnp.zeros((1, blk), jnp.float32) for k in range(groups)]
        keys = [jnp.concatenate([key] * (tile // blk), axis=1) for key in keys]
        lines = []
        for t in range(TILES):
            line = jnp.zeros((1, tile), jnp.float32)
            for k in range(groups):
                turn = ((k - t) * per_tile) % tile
                moved = pltpu.roll(keys[k], turn, 1) if turn else keys[k]
                line = jnp.where(lane == k, moved, line)
            lines.append(line)
        return lines

    def rows_of(ref, base, first, last):
        return ref[base + first * per_tile : base + last * per_tile, :]

    best[...] = prev[...] if has_prev else jnp.full(best.shape, -1.0, jnp.float32)

    def search(a, row, queries, mine, pieces, last, spot):
        width = mine.shape[1]
        turned[spot, :, 0:width] = jnp.concatenate(queries, axis=0).T
        floor = floor_of(mine)
        acc = jnp.full((8, width), -1.0, jnp.float32)
        for at in range(0, len(pieces), groups):
            some = pieces[at : at + groups]
            theirs = [rows_of(key_col, key_at[piece], 0, last) for piece in some]
            theirs = jnp.concatenate(theirs, axis=0)
            theirs = jnp.concatenate([theirs] * (width // 128), axis=1)
            sims = jnp.dot(
                jnp.concatenate([rows_of(*block[piece], 0, last) for piece in some], axis=0),
                turned[spot, :, 0:width],
                preferred_element_type=jnp.float32,
            )
            keep = (theirs >= floor) & (theirs < mine)
            sims = jnp.where(keep, sims, -1.0)
            top = jnp.max(sims.reshape(sims.shape[0] // 8, 8, width), axis=0)
            acc = jnp.maximum(acc, top)
        best[a, row : row + 1, 0:width] = jnp.maximum(
            best[a, row : row + 1, 0:width], jnp.max(acc, axis=0, keepdims=True)
        )

    spot = 0
    for a, whole, ks, pieces in jobs:
        if whole:
            (k,) = ks
            queries = [rows_of(*block[a, k], 0, TILES)]
            search(a, TILES, queries, keys_of((a, k)), pieces, TILES, spot)
            spot += 1
            continue
        lines = lines_of(a, ks)
        for t in range(TILES):
            queries = [rows_of(*block[a, k if k in ks else ks[0]], t, t + 1) for k in range(groups)]
            search(a, t, queries, lines[t], pieces, t + 1, spot)
            spot += 1

    if not starts:
        outs[0][...] = best[...]
        return
    for o, a in enumerate(starts):
        found = best[a]
        for k in range(groups):
            total = jnp.full((1, tile), -1.0, jnp.float32)
            for t in range(TILES):
                turn = ((t - k) * per_tile) % tile
                moved = pltpu.roll(found, turn, 1) if turn else found
                total = jnp.where(lane == t, moved[t : t + 1], total)
            if any(a == e and whole and k in ks for e, whole, ks, _ in jobs):
                total = jnp.maximum(total, found[TILES : TILES + 1])
            at = (along // side) ^ k
            if joined:
                outs[0][pl.ds(at * joined + ((along % side) ^ a), 1), 0, :] = total[:, :blk]
            else:
                outs[o][pl.ds(at, 1), 0, :] = total[:, :blk]


def compare(blocks, jobs, prev, starts, joined, offsets, sizes):
    groups, halves, half, cap, blk = sizes
    n_sets = len(offsets)
    used = {piece for *_, pieces in jobs for piece in pieces}
    used |= {(a, k) for a, _, ks, _ in jobs for k in ks}
    searches = sum(1 if whole else TILES for _, whole, _, _ in jobs)
    spots = {}
    arrays = {}
    for piece in sorted(used):
        value, *where = blocks[piece]
        name = next((n for n, v in arrays.items() if v is value), None)
        if name is None:
            name = len(arrays)
            arrays[name] = value
        spots[piece] = (name, *where)
    names = list(arrays)
    width = arrays[0].shape[1]
    tile = groups * blk // TILES
    vmem = pl.BlockSpec(memory_space=pltpu.VMEM)
    work = blk * tile * width * sum(
        len(pieces) * (1.0 if whole else (TILES + 1) / 2 / TILES) for _, whole, _, pieces in jobs
    )
    if not starts:
        out_shape = [jax.ShapeDtypeStruct((n_sets, 8, tile), jnp.float32)]
    elif joined:
        out_shape = [jax.ShapeDtypeStruct((groups * joined, 1, blk), jnp.float32)]
    else:
        out_shape = [jax.ShapeDtypeStruct((groups, 1, blk), jnp.float32)] * len(starts)
    operands = list(arrays.values()) + ([] if prev is None else [prev])
    needed = {piece for *_, pieces in jobs for piece in pieces}
    return pl.pallas_call(
        functools.partial(
            compare_kernel, sizes, jobs, names, spots, starts, joined, prev is not None
        ),
        out_shape=out_shape,
        in_specs=[vmem] * len(operands),
        out_specs=[vmem] * len(out_shape),
        scratch_shapes=[
            pltpu.VMEM((len(needed) * blk, 128), jnp.float32),
            pltpu.VMEM((searches, width, tile), jnp.bfloat16),
            pltpu.VMEM((n_sets, 8, tile), jnp.float32),
        ],
        compiler_params=pltpu.CompilerParams(vmem_limit_bytes=COMPARE_VMEM),
        cost_estimate=pl.CostEstimate(
            flops=int(2 * work), bytes_accessed=2 * len(used) * blk * width, transcendentals=0
        ),
    )(*operands)


def pair_kernel(*refs):
    out_ref, ins = refs[-1], refs[:-1]
    blk, width = ins[0].shape[0] - LABEL_ROWS, ins[0].shape[1]
    parts = []
    for n, ref in enumerate(ins):
        out_ref[n * blk : (n + 1) * blk, :] = ref[0:blk, :]
        parts.append(ref[blk : blk + LABEL_ROWS, 0:blk])
    parts.append(jnp.zeros((LABEL_ROWS, width - len(ins) * blk), jnp.bfloat16))
    out_ref[len(ins) * blk :, :] = jnp.concatenate(parts, axis=1)


def pile_kernel(*refs):
    out_ref, ins = refs[-1], refs[:-1]
    row, strip = 0, out_ref.shape[0] - LABEL_ROWS * len(ins)
    for ref in ins:
        rows = ref.shape[0] - LABEL_ROWS
        out_ref[row : row + rows, :] = ref[0:rows, :]
        out_ref[strip : strip + LABEL_ROWS, :] = ref[rows : rows + LABEL_ROWS, :]
        row, strip = row + rows, strip + LABEL_ROWS


def join(kernel, pieces, rows):
    vmem = pl.BlockSpec(memory_space=pltpu.VMEM)
    return pl.pallas_call(
        kernel,
        out_shape=jax.ShapeDtypeStruct((rows, pieces[0].shape[1]), pieces[0].dtype),
        in_specs=[vmem] * len(pieces),
        out_specs=vmem,
        compiler_params=pltpu.CompilerParams(vmem_limit_bytes=COMPARE_VMEM),
    )(*pieces)


def unpack_kernel(sizes, dest_ref, back_ref, out_ref):
    groups, halves, half, cap, blk = sizes
    side = back_ref.shape[0] // groups
    rows = dest_ref.shape[1]
    dest = dest_ref[...]
    slot = lax.broadcasted_iota(jnp.int32, (blk, rows), 0)
    field = lax.broadcasted_iota(jnp.int32, (LABEL_ROWS, blk), 0)
    total = jnp.zeros((LABEL_ROWS, rows), jnp.float32)
    for k in range(groups):
        value = back_ref[k * side]
        for more in range(1, side):
            value = jnp.maximum(value, back_ref[k * side + more])
        top = value.astype(jnp.bfloat16).astype(jnp.float32)
        rest = value - top
        mid = rest.astype(jnp.bfloat16).astype(jnp.float32)
        low = rest - mid
        stack = jnp.where(field == 0, top, jnp.where(field == 1, mid, jnp.where(field == 2, low, 0.0)))
        pick = (slot + k * blk == dest).astype(jnp.float32).astype(jnp.bfloat16)
        total = total + jnp.dot(stack.astype(jnp.bfloat16), pick, preferred_element_type=jnp.float32)
    value = (total[0:1] + total[1:2]) + total[2:3]
    out_ref[...] = jnp.where(dest >= 0, value, -1.0)


def unpack(dest, back, sizes):
    vmem = pl.BlockSpec(memory_space=pltpu.VMEM)
    return pl.pallas_call(
        functools.partial(unpack_kernel, sizes),
        out_shape=jax.ShapeDtypeStruct(dest.shape, jnp.float32),
        in_specs=[vmem] * 2,
        out_specs=vmem,
        compiler_params=pltpu.CompilerParams(vmem_limit_bytes=COMPARE_VMEM),
    )(dest, back)


def on_device(embeddings, cluster, rank):
    rows_dev, width = embeddings.shape
    groups = lax.axis_size("grp")
    members = lax.axis_size("mem")
    devices = groups * members
    halves = 2 * members
    half = rows_dev // CLUS_GRP // 2
    blk = rows_dev // groups
    cap = blk // halves
    sizes = (groups, halves, half, cap, blk)
    side = members // groups

    def swap(value, block_step, member_step):
        mask = member_step // side * members + block_step * side + member_step % side
        if mask == 0:
            return value
        return lax.ppermute(value, ("grp", "mem"), [(i, i ^ mask) for i in range(devices)])

    offsets, pairs = cover(members)
    sends = [None] * groups
    first = tuple(range(1, min(3, groups)))
    for k, value in zip(first, pack(embeddings, cluster, rank, first, False, sizes)):
        sends[k] = value
    rest = tuple(k for k in range(groups) if k not in first)
    cluster, sends[1] = lax.optimization_barrier((cluster, sends[1]))
    *packed, dest = pack(embeddings, cluster, rank, rest, True, sizes)
    for k, value in zip(rest, packed):
        sends[k] = value

    last = groups - 1
    far = [d for d in offsets if d & side and d != side and d ^ side in offsets]
    near = [d for d in offsets[1:] if d not in far]
    lead = far[0] ^ side if far else near[0]
    held = {0: [sends[0]]}
    for d in near:
        held[d] = [swap(sends[0], 0, d)]
    after = held[lead][0]
    for k in range(1, groups, 2):
        if k > 1:
            send, after = lax.optimization_barrier((sends[k], after))
        else:
            send = sends[k]
        mine = swap(send, k, 0)
        if k < last:
            also = swap(sends[k + 1], k + 1, 0)
            mine = join(pair_kernel, [mine, also], 2 * blk + LABEL_ROWS)
            if k == 1:
                mine, *firsts = lax.optimization_barrier((mine, *(held[d][0] for d in near)))
                for d, value in zip(near, firsts):
                    held[d] = [value]
            after = mine
        held[0].append(mine)
    spots = len(held[0])
    for spot in range(1, spots):
        for d in near:
            if d != side:
                held[d].append(swap(held[0][spot], 0, d))

    index = {d: i for i, d in enumerate(offsets)}
    blocks = {}

    def ks_of(spot):
        return [0] if spot == 0 else [k for k in (2 * spot - 1, 2 * spot) if k < groups]

    def note(d, spot):
        value = held[d][spot]
        first = value.shape[0] - LABEL_ROWS
        for at, k in enumerate(ks_of(spot)):
            blocks[index[d], k] = (value, at * blk, first, at * blk)

    for d in held:
        for spot in range(len(held[d])):
            note(d, spot)
    pile = [(side, spot) for spot in range(1, spots)]
    pile += [(d, spot) for d in far for spot in range(spots - 1)]
    hops = [d for d in near if d != side and d not in [e ^ side for e in far]]
    values = [held[d][spots - 2] for d in hops]
    held[0][-1], *values = lax.optimization_barrier((held[0][-1], *values))
    for d, value in zip(hops, values):
        held[d][spots - 2] = value
        note(d, spots - 2)
    note(0, spots - 1)
    parts = [held[d ^ side][spot] for d, spot in pile]
    data = sum(part.shape[0] - LABEL_ROWS for part in parts)
    moved = swap(join(pile_kernel, parts, data + LABEL_ROWS * len(parts)), 0, side)
    row = 0
    for n, (d, spot) in enumerate(pile):
        for at, k in enumerate(ks_of(spot)):
            blocks[index[d], k] = (moved, row + at * blk, data + LABEL_ROWS * n, at * blk)
        row += parts[n].shape[0] - LABEL_ROWS
    slow = {(index[d], k) for d, spot in pile for k in ks_of(spot)}

    starts = sorted({a for a, _ in pairs.values()})
    every = tuple(range(groups))
    early, middle, late = [], [], []
    for a in starts:
        cols = [index[b] for _, (e, b) in sorted(pairs.items()) if e == a]
        pieces = [(b, k) for b in cols for k in every]
        soon = [(b, k) for b, k in pieces if k < last]
        if a == 0:
            ready = [piece for piece in pieces if piece in soon or piece[0] == 0]
            early.append((0, False, every, [piece for piece in ready if piece not in slow]))
            middle.append((0, False, every, [piece for piece in pieces if piece in slow]))
            done = early[-1][-1] + middle[-1][-1]
            late.append((0, False, every, [piece for piece in pieces if piece not in done]))
        else:
            middle.append((index[a], False, every[:-1], soon))
            late.append((index[a], False, every, [piece for piece in pieces if piece not in soon]))
            late.append((index[a], True, (last,), soon))
    order = [index[a] for a in starts]
    joined = side if all(a < side for a in starts) else 0
    prev = compare(blocks, early, None, (), 0, offsets, sizes)[0]
    prev = compare(blocks, middle, prev, (), 0, offsets, sizes)[0]
    for d in far:
        piece, prev = lax.optimization_barrier((held[d ^ side][-1], prev))
        held[d] = {spots - 1: swap(piece, 0, side)}
        note(d, spots - 1)
    found = compare(blocks, late, prev, order, joined, offsets, sizes)
    if joined:
        back = found[0]
    else:
        best = {}
        for a, value in zip(starts, found):
            near = a % side
            value = swap(value, 0, a - near)
            best[near] = jnp.maximum(best[near], value) if near in best else value
        none = jnp.full_like(found[0], -1.0)
        near_of = [best.get(near, none) for near in range(side)]
        rows_of = []
        for spot in range(side):
            value = near_of[spot]
            for mine in range(1, side):
                value = jnp.where(lax.axis_index("mem") % side == mine, near_of[spot ^ mine], value)
            rows_of.append(value)
        back = jnp.stack(rows_of, axis=1).reshape(groups * side, 1, blk)
    back = lax.all_to_all(back, "mem", split_axis=0, concat_axis=0, tiled=True)
    return unpack(dest, back, sizes).reshape(rows_dev)


def solution(mesh):
    in_specs = (P(("grp", "mem"), None), P(("grp", "mem")), P(("grp", "mem")))
    out_specs = P(("grp", "mem"))
    return jax.shard_map(
        on_device, mesh=mesh, in_specs=in_specs, out_specs=out_specs, check_vma=False
    )
```

```python
import functools

import jax
import jax.numpy as jnp
from jax import lax
from jax.experimental import pallas as pl
from jax.experimental.pallas import tpu as pltpu
from jax.sharding import PartitionSpec as P

CLUS_GRP = 2
TILES = 4
LABEL_ROWS = 16
FAR = 1.0e9
PACK_VMEM = 60 * 1024 * 1024
COMPARE_VMEM = 24 * 1024 * 1024
NT = (((1,), (1,)), ((), ()))
TN = (((0,), (0,)), ((), ()))


def cover(members):
    bits = [1 << i for i in range(members.bit_length() - 1)]
    offsets = [0] + bits

    def missing(held):
        return set(range(members)) - {a ^ b for a in held for b in held}

    while missing(offsets):
        offsets.append(
            min(
                (d for d in range(members) if d not in offsets),
                key=lambda d: (len(missing(offsets + [d])), bin(d).count("1"), -d),
            )
        )
    pairs = {}
    for delta in range(members):
        pairs[delta] = min(
            (a, a ^ delta) for a in offsets if a ^ delta in offsets
        )
    return offsets, pairs


def pack_kernel(sizes, ks, placed, emb_hbm, cluster_hbm, rank_hbm, *refs):
    groups, halves, half, cap, blk = sizes
    outs, refs = refs[: len(ks)], refs[len(ks) :]
    if placed:
        dest_ref, *refs = refs
    emb_ref, cluster_ref, rank_ref, stage, sems, out_sems = refs
    rows = emb_ref.shape[0]
    step = 256
    loads = [
        pltpu.make_async_copy(cluster_hbm, cluster_ref, sems.at[0]),
        pltpu.make_async_copy(rank_hbm, rank_ref, sems.at[1]),
    ]
    for j in range(rows // step):
        at = pl.ds(j * step, step)
        loads.append(pltpu.make_async_copy(emb_hbm.at[at], emb_ref.at[at], sems.at[2 + j]))
    for load in loads:
        load.start()
    for load in loads[:2]:
        load.wait()
    cluster = cluster_ref[...]
    rank = rank_ref[...]
    alive = cluster >= 0
    pair = lax.shift_right_logical(jnp.maximum(cluster, 0), 1)
    parity = jnp.maximum(cluster, 0) - 2 * pair
    safe_rank = jnp.maximum(rank, 0)
    which = safe_rank // half
    units = groups * halves
    unit_id = jnp.where(alive, pair * halves + which, -1)
    before_rows = lax.broadcasted_iota(jnp.int32, (step, step), 0)
    before_cols = lax.broadcasted_iota(jnp.int32, (step, step), 1)
    upper = (before_rows < before_cols).astype(jnp.float32).astype(jnp.bfloat16)
    unit_iota = lax.broadcasted_iota(jnp.int32, (units, step), 0)
    carry = jnp.zeros((units, 1), jnp.float32)
    places = []
    for j in range(rows // step):
        mine = unit_id[:, j * step : (j + 1) * step]
        hit = (unit_iota == mine).astype(jnp.float32)
        before = jnp.dot(hit.astype(jnp.bfloat16), upper, preferred_element_type=jnp.float32) + carry
        position = jnp.sum(hit * before, axis=0, keepdims=True)
        carry = carry + jnp.sum(hit, axis=1, keepdims=True)
        places.append(jnp.where(mine >= 0, mine * cap + position.astype(jnp.int32), -1))
    dest = jnp.concatenate(places, axis=1)
    if placed:
        dest_ref[...] = dest
    members = halves // 2
    side = members // groups
    here = lax.axis_index("mem") // side
    dest = jnp.where(dest >= 0, dest ^ (here * blk), -1)

    field = lax.broadcasted_iota(jnp.int32, (LABEL_ROWS, rows), 0)
    labels = jnp.where(
        field == 0, safe_rank - which * half, jnp.where(field == 1, parity + 1, 0)
    )
    labels = jnp.where(alive, labels, 0).astype(jnp.float32).astype(jnp.bfloat16)
    unit_of = lax.div(lax.broadcasted_iota(jnp.int32, (1, blk), 1), cap).astype(jnp.float32)
    slot = lax.broadcasted_iota(jnp.int32, (blk, rows), 0)
    line = lax.broadcasted_iota(jnp.int32, (LABEL_ROWS, blk), 0)
    width = emb_ref.shape[1]
    leaving = []
    for n, k in enumerate(ks):
        pick = (slot + k * blk == dest).astype(jnp.float32).astype(jnp.bfloat16)
        if n == 0:
            for load in loads[2:]:
                load.wait()
        wide = jnp.dot(pick, emb_ref[...], preferred_element_type=jnp.float32)
        total = jnp.sum(wide * wide, axis=1, keepdims=True)
        stage[n, 0:blk, :] = (wide * lax.rsqrt(total + 1e-06)).astype(jnp.bfloat16)
        mine = lax.dot_general(labels, pick, NT, preferred_element_type=jnp.float32)
        high = unit_of + float(halves) * mine[1:2]
        strip = jnp.where(line == 0, mine[0:1], jnp.where(line == 1, high, 0.0))
        strip = jnp.concatenate([strip, jnp.zeros((LABEL_ROWS, width - blk), jnp.float32)], axis=1)
        stage[n, blk : blk + LABEL_ROWS, :] = strip.astype(jnp.bfloat16)
        leaving.append(pltpu.make_async_copy(stage.at[n], outs[n], out_sems.at[n]))
        leaving[-1].start()
    for copy in leaving:
        copy.wait()


def pack(embeddings, cluster, rank, ks, placed, sizes):
    groups, halves, half, cap, blk = sizes
    rows, width = embeddings.shape
    hbm = pl.BlockSpec(memory_space=pltpu.HBM)
    vmem = pl.BlockSpec(memory_space=pltpu.VMEM)
    out_shape = [jax.ShapeDtypeStruct((blk + LABEL_ROWS, width), jnp.bfloat16)] * len(ks)
    out_specs = [hbm] * len(ks)
    if placed:
        out_shape.append(jax.ShapeDtypeStruct((1, rows), jnp.int32))
        out_specs.append(vmem)
    return pl.pallas_call(
        functools.partial(pack_kernel, sizes, ks, placed),
        out_shape=out_shape,
        in_specs=[hbm, hbm, hbm],
        out_specs=out_specs,
        scratch_shapes=[
            pltpu.VMEM((rows, width), jnp.bfloat16),
            pltpu.VMEM((1, rows), jnp.int32),
            pltpu.VMEM((1, rows), jnp.int32),
            pltpu.VMEM((len(ks), blk + LABEL_ROWS, width), jnp.bfloat16),
            pltpu.SemaphoreType.DMA((2 + rows // 256,)),
            pltpu.SemaphoreType.DMA((len(ks),)),
        ],
        compiler_params=pltpu.CompilerParams(vmem_limit_bytes=PACK_VMEM),
        cost_estimate=pl.CostEstimate(
            flops=2 * len(ks) * blk * rows * width, bytes_accessed=4 * rows * width, transcendentals=0
        ),
    )(embeddings, cluster.reshape(1, rows), rank.reshape(1, rows))


def compare_kernel(sizes, jobs, names, spots, starts, wholes, joined, has_prev, keep, reuse, *refs):
    groups, halves, half, cap, blk = sizes
    array = dict(zip(names, refs))
    refs = refs[len(names) :]
    block = {piece: (array[name], row) for piece, (name, row, _, _) in spots.items()}
    prev = None
    if has_prev:
        prev, refs = refs[0], refs[1:]
    if reuse:
        turned, *refs = refs
        *outs, key_col, best = refs
    elif keep:
        *outs, turned, key_col, best = refs
    else:
        *outs, key_col, best, turned = refs
    rows = groups * blk
    per_tile = blk // TILES
    tile = rows // TILES
    cap_all = float(halves * half)

    side = halves // 2 // groups
    along = lax.axis_index("mem")

    def strip_of(piece):
        name, _, first, left = spots[piece]
        return array[name][first : first + LABEL_ROWS, left : left + blk]

    def keys_of(piece):
        strip = strip_of(piece).astype(jnp.float32)
        return strip[0:1] + float(half) * strip[1:2]

    weight_row = lax.broadcasted_iota(jnp.int32, (LABEL_ROWS, 128), 0)
    weights = jnp.where(weight_row == 0, 1.0, jnp.where(weight_row == 1, float(half), 0.0))
    weights = weights.astype(jnp.bfloat16)
    needed = sorted({piece for *_, pieces in jobs for piece in pieces})
    key_at = {piece: n * blk for n, piece in enumerate(needed)}
    for piece in needed:
        key_col[pl.ds(key_at[piece], blk), :] = lax.dot_general(
            strip_of(piece), weights, TN, preferred_element_type=jnp.float32
        )
    lane = lax.div(lax.broadcasted_iota(jnp.int32, (1, tile), 1), per_tile)

    def floor_of(key):
        low = jnp.floor(key * (1.0 / cap_all)) * cap_all
        return jnp.where(low > 0.5, low, FAR)

    def lines_of(a, ks):
        keys = [keys_of((a, k)) if k in ks else jnp.zeros((1, blk), jnp.float32) for k in range(groups)]
        keys = [jnp.concatenate([key] * (tile // blk), axis=1) for key in keys]
        lines = []
        for t in range(TILES):
            line = jnp.zeros((1, tile), jnp.float32)
            for k in range(groups):
                turn = ((k - t) * per_tile) % tile
                moved = pltpu.roll(keys[k], turn, 1) if turn else keys[k]
                line = jnp.where(lane == k, moved, line)
            lines.append(line)
        return lines

    def rows_of(ref, base, first, last):
        return ref[base + first * per_tile : base + last * per_tile, :]

    best[...] = prev[...] if has_prev else jnp.full(best.shape, -1.0, jnp.float32)

    def search(a, row, queries, mine, pieces, last, spot):
        width = mine.shape[1]
        if not reuse:
            turned[spot, :, 0:width] = jnp.concatenate(queries, axis=0).T
        floor = floor_of(mine)
        acc = jnp.full((8, width), -1.0, jnp.float32)
        for at in range(0, len(pieces), groups):
            some = pieces[at : at + groups]
            theirs = [rows_of(key_col, key_at[piece], 0, last) for piece in some]
            theirs = jnp.concatenate(theirs, axis=0)
            theirs = jnp.concatenate([theirs] * (width // 128), axis=1)
            sims = jnp.dot(
                jnp.concatenate([rows_of(*block[piece], 0, last) for piece in some], axis=0),
                turned[spot, :, 0:width],
                preferred_element_type=jnp.float32,
            )
            keep = (theirs >= floor) & (theirs < mine)
            sims = jnp.where(keep, sims, -1.0)
            top = jnp.max(sims.reshape(sims.shape[0] // 8, 8, width), axis=0)
            acc = jnp.maximum(acc, top)
        best[a, row : row + 1, 0:width] = jnp.maximum(
            best[a, row : row + 1, 0:width], jnp.max(acc, axis=0, keepdims=True)
        )

    spot = 0
    for a, whole, ks, pieces in jobs:
        if whole:
            (k,) = ks
            queries = [rows_of(*block[a, k], 0, TILES)]
            search(a, TILES, queries, keys_of((a, k)), pieces, TILES, spot)
            spot += 1
            continue
        lines = lines_of(a, ks)
        for t in range(TILES):
            queries = [rows_of(*block[a, k if k in ks else ks[0]], t, t + 1) for k in range(groups)]
            search(a, t, queries, lines[t], pieces, t + 1, spot)
            spot += 1

    if not starts:
        outs[0][...] = best[...]
        return
    for o, a in enumerate(starts):
        found = best[a]
        for k in range(groups):
            total = jnp.full((1, tile), -1.0, jnp.float32)
            for t in range(TILES):
                turn = ((t - k) * per_tile) % tile
                moved = pltpu.roll(found, turn, 1) if turn else found
                total = jnp.where(lane == t, moved[t : t + 1], total)
            if (a, k) in wholes:
                total = jnp.maximum(total, found[TILES : TILES + 1])
            at = (along // side) ^ k
            if joined:
                outs[0][pl.ds(at * joined + ((along % side) ^ a), 1), 0, :] = total[:, :blk]
            else:
                outs[o][pl.ds(at, 1), 0, :] = total[:, :blk]


def compare(blocks, jobs, prev, starts, wholes, joined, offsets, sizes, keep=False, cache=None):
    groups, halves, half, cap, blk = sizes
    n_sets = len(offsets)
    used = {piece for *_, pieces in jobs for piece in pieces}
    used |= {(a, k) for a, _, ks, _ in jobs for k in ks}
    searches = sum(1 if whole else TILES for _, whole, _, _ in jobs)
    spots = {}
    arrays = {}
    for piece in sorted(used):
        value, *where = blocks[piece]
        name = next((n for n, v in arrays.items() if v is value), None)
        if name is None:
            name = len(arrays)
            arrays[name] = value
        spots[piece] = (name, *where)
    names = list(arrays)
    width = arrays[0].shape[1]
    tile = groups * blk // TILES
    vmem = pl.BlockSpec(memory_space=pltpu.VMEM)
    work = blk * tile * width * sum(
        len(pieces) * (1.0 if whole else (TILES + 1) / 2 / TILES) for _, whole, _, pieces in jobs
    )
    if not starts:
        out_shape = [jax.ShapeDtypeStruct((n_sets, 8, tile), jnp.float32)]
    elif joined:
        out_shape = [jax.ShapeDtypeStruct((groups * joined, 1, blk), jnp.float32)]
    else:
        out_shape = [jax.ShapeDtypeStruct((groups, 1, blk), jnp.float32)] * len(starts)
    operands = list(arrays.values()) + ([] if prev is None else [prev])
    scratch = []
    shape = (searches, width, tile)
    if cache is not None:
        operands.append(cache)
    elif keep:
        out_shape.append(jax.ShapeDtypeStruct(shape, jnp.bfloat16))
    else:
        scratch.append(pltpu.VMEM(shape, jnp.bfloat16))
    needed = {piece for *_, pieces in jobs for piece in pieces}
    return pl.pallas_call(
        functools.partial(
            compare_kernel,
            sizes,
            jobs,
            names,
            spots,
            starts,
            wholes,
            joined,
            prev is not None,
            keep,
            cache is not None,
        ),
        out_shape=out_shape,
        in_specs=[vmem] * len(operands),
        out_specs=[vmem] * len(out_shape),
        scratch_shapes=[
            pltpu.VMEM((len(needed) * blk, 128), jnp.float32),
            pltpu.VMEM((n_sets, 8, tile), jnp.float32),
            *scratch,
        ],
        compiler_params=pltpu.CompilerParams(vmem_limit_bytes=COMPARE_VMEM),
        cost_estimate=pl.CostEstimate(
            flops=int(2 * work), bytes_accessed=2 * len(used) * blk * width, transcendentals=0
        ),
    )(*operands)


def pair_kernel(*refs):
    out_ref, ins = refs[-1], refs[:-1]
    blk, width = ins[0].shape[0] - LABEL_ROWS, ins[0].shape[1]
    parts = []
    for n, ref in enumerate(ins):
        out_ref[n * blk : (n + 1) * blk, :] = ref[0:blk, :]
        parts.append(ref[blk : blk + LABEL_ROWS, 0:blk])
    parts.append(jnp.zeros((LABEL_ROWS, width - len(ins) * blk), jnp.bfloat16))
    out_ref[len(ins) * blk :, :] = jnp.concatenate(parts, axis=1)


def pile_kernel(*refs):
    out_ref, ins = refs[-1], refs[:-1]
    row, strip = 0, out_ref.shape[0] - LABEL_ROWS * len(ins)
    for ref in ins:
        rows = ref.shape[0] - LABEL_ROWS
        out_ref[row : row + rows, :] = ref[0:rows, :]
        out_ref[strip : strip + LABEL_ROWS, :] = ref[rows : rows + LABEL_ROWS, :]
        row, strip = row + rows, strip + LABEL_ROWS


def join(kernel, pieces, rows):
    vmem = pl.BlockSpec(memory_space=pltpu.VMEM)
    return pl.pallas_call(
        kernel,
        out_shape=jax.ShapeDtypeStruct((rows, pieces[0].shape[1]), pieces[0].dtype),
        in_specs=[vmem] * len(pieces),
        out_specs=vmem,
        compiler_params=pltpu.CompilerParams(vmem_limit_bytes=COMPARE_VMEM),
    )(*pieces)


def unpack_kernel(sizes, dest_ref, back_ref, out_ref):
    groups, halves, half, cap, blk = sizes
    side = back_ref.shape[0] // groups
    rows = dest_ref.shape[1]
    dest = dest_ref[...]
    slot = lax.broadcasted_iota(jnp.int32, (blk, rows), 0)
    field = lax.broadcasted_iota(jnp.int32, (LABEL_ROWS, blk), 0)
    total = jnp.zeros((LABEL_ROWS, rows), jnp.float32)
    for k in range(groups):
        value = back_ref[k * side]
        for more in range(1, side):
            value = jnp.maximum(value, back_ref[k * side + more])
        top = value.astype(jnp.bfloat16).astype(jnp.float32)
        rest = value - top
        mid = rest.astype(jnp.bfloat16).astype(jnp.float32)
        low = rest - mid
        stack = jnp.where(field == 0, top, jnp.where(field == 1, mid, jnp.where(field == 2, low, 0.0)))
        pick = (slot + k * blk == dest).astype(jnp.float32).astype(jnp.bfloat16)
        total = total + jnp.dot(stack.astype(jnp.bfloat16), pick, preferred_element_type=jnp.float32)
    value = (total[0:1] + total[1:2]) + total[2:3]
    out_ref[...] = jnp.where(dest >= 0, value, -1.0)


def unpack(dest, back, sizes):
    vmem = pl.BlockSpec(memory_space=pltpu.VMEM)
    return pl.pallas_call(
        functools.partial(unpack_kernel, sizes),
        out_shape=jax.ShapeDtypeStruct(dest.shape, jnp.float32),
        in_specs=[vmem] * 2,
        out_specs=vmem,
        compiler_params=pltpu.CompilerParams(vmem_limit_bytes=COMPARE_VMEM),
    )(dest, back)


def on_device(embeddings, cluster, rank):
    rows_dev, width = embeddings.shape
    groups = lax.axis_size("grp")
    members = lax.axis_size("mem")
    devices = groups * members
    halves = 2 * members
    half = rows_dev // CLUS_GRP // 2
    blk = rows_dev // groups
    cap = blk // halves
    sizes = (groups, halves, half, cap, blk)
    side = members // groups

    def swap(value, block_step, member_step):
        mask = member_step // side * members + block_step * side + member_step % side
        if mask == 0:
            return value
        return lax.ppermute(value, ("grp", "mem"), [(i, i ^ mask) for i in range(devices)])

    offsets, pairs = cover(members)
    sends = [None] * groups
    first = tuple(range(1, min(3, groups)))
    for k, value in zip(first, pack(embeddings, cluster, rank, first, False, sizes)):
        sends[k] = value
    rest = tuple(k for k in range(groups) if k not in first)
    cluster, sends[1] = lax.optimization_barrier((cluster, sends[1]))
    *packed, dest = pack(embeddings, cluster, rank, rest, True, sizes)
    for k, value in zip(rest, packed):
        sends[k] = value

    last = groups - 1
    far = [d for d in offsets if d & side and d != side and d ^ side in offsets]
    near = [d for d in offsets[1:] if d not in far]
    lead = far[0] ^ side if far else near[0]
    held = {0: [sends[0]]}
    for d in near:
        held[d] = [swap(sends[0], 0, d)]
    after = held[lead][0]
    for k in range(1, groups, 2):
        if k > 1:
            send, after = lax.optimization_barrier((sends[k], after))
        else:
            send = sends[k]
        mine = swap(send, k, 0)
        if k < last:
            also = swap(sends[k + 1], k + 1, 0)
            mine = join(pair_kernel, [mine, also], 2 * blk + LABEL_ROWS)
            if k == 1:
                mine, *firsts = lax.optimization_barrier((mine, *(held[d][0] for d in near)))
                for d, value in zip(near, firsts):
                    held[d] = [value]
            after = mine
        held[0].append(mine)
    spots = len(held[0])
    for spot in range(1, spots):
        for d in near:
            if d != side:
                held[d].append(swap(held[0][spot], 0, d))

    index = {d: i for i, d in enumerate(offsets)}
    blocks = {}

    def ks_of(spot):
        return [0] if spot == 0 else [k for k in (2 * spot - 1, 2 * spot) if k < groups]

    def note(d, spot):
        value = held[d][spot]
        first = value.shape[0] - LABEL_ROWS
        for at, k in enumerate(ks_of(spot)):
            blocks[index[d], k] = (value, at * blk, first, at * blk)

    for d in held:
        for spot in range(len(held[d])):
            note(d, spot)
    pile = [(side, spot) for spot in range(1, spots)]
    pile += [(d, spot) for d in far for spot in range(spots - 1)]
    hops = [d for d in near if d != side and d not in [e ^ side for e in far]]
    values = [held[d][spots - 2] for d in hops]
    held[0][-1], *values = lax.optimization_barrier((held[0][-1], *values))
    for d, value in zip(hops, values):
        held[d][spots - 2] = value
        note(d, spots - 2)
    note(0, spots - 1)
    parts = [held[d ^ side][spot] for d, spot in pile]
    data = sum(part.shape[0] - LABEL_ROWS for part in parts)
    moved = swap(join(pile_kernel, parts, data + LABEL_ROWS * len(parts)), 0, side)
    row = 0
    for n, (d, spot) in enumerate(pile):
        for at, k in enumerate(ks_of(spot)):
            blocks[index[d], k] = (moved, row + at * blk, data + LABEL_ROWS * n, at * blk)
        row += parts[n].shape[0] - LABEL_ROWS
    slow = {(index[d], k) for d, spot in pile for k in ks_of(spot)}

    starts = sorted({a for a, _ in pairs.values()})
    every = tuple(range(groups))
    early, middle, late = [], [], []
    for a in starts:
        cols = [index[b] for _, (e, b) in sorted(pairs.items()) if e == a]
        pieces = [(b, k) for b in cols for k in every]
        soon = [(b, k) for b, k in pieces if k < last]
        if a == 0:
            ready = [piece for piece in pieces if piece in soon or piece[0] == 0]
            early.append((0, False, every, [piece for piece in ready if piece not in slow]))
            middle.append((0, False, every, [piece for piece in pieces if piece in slow]))
            done = early[-1][-1] + middle[-1][-1]
            late.append((0, False, every, [piece for piece in pieces if piece not in done]))
        else:
            middle.append((index[a], False, every[:-1], soon))
            late.append((index[a], False, every, [piece for piece in pieces if piece not in soon]))
            late.append((index[a], True, (last,), soon))
    order = [index[a] for a in starts]
    joined = side if all(a < side for a in starts) else 0
    prev = compare(blocks, early, None, (), (), 0, offsets, sizes)[0]
    prev = compare(blocks, middle, prev, (), (), 0, offsets, sizes)[0]
    wholes = [(a, k) for a, whole, ks, _ in late if whole for k in ks]
    if far:
        final = {(index[d], last) for d in far}
        before = [(*job, [p for p in pieces if p not in final]) for *job, pieces in late]
        late = [(*job, [p for p in pieces if p in final]) for *job, pieces in late]
        late = [job for job in late if job[-1]]
        for d in far:
            piece, prev = lax.optimization_barrier((held[d ^ side][-1], prev))
            held[d] = {spots - 1: swap(piece, 0, side)}
            note(d, spots - 1)
        prev, turned = compare(blocks, before, prev, (), (), 0, offsets, sizes, keep=True)
        found = compare(blocks, late, prev, order, wholes, joined, offsets, sizes, cache=turned)
    else:
        found = compare(blocks, late, prev, order, wholes, joined, offsets, sizes)
    if joined:
        back = found[0]
    else:
        best = {}
        for a, value in zip(starts, found):
            near = a % side
            value = swap(value, 0, a - near)
            best[near] = jnp.maximum(best[near], value) if near in best else value
        none = jnp.full_like(found[0], -1.0)
        near_of = [best.get(near, none) for near in range(side)]
        rows_of = []
        for spot in range(side):
            value = near_of[spot]
            for mine in range(1, side):
                value = jnp.where(lax.axis_index("mem") % side == mine, near_of[spot ^ mine], value)
            rows_of.append(value)
        back = jnp.stack(rows_of, axis=1).reshape(groups * side, 1, blk)
    back = lax.all_to_all(back, "mem", split_axis=0, concat_axis=0, tiled=True)
    return unpack(dest, back, sizes).reshape(rows_dev)


def solution(mesh):
    in_specs = (P(("grp", "mem"), None), P(("grp", "mem")), P(("grp", "mem")))
    out_specs = P(("grp", "mem"))
    return jax.shard_map(
        on_device, mesh=mesh, in_specs=in_specs, out_specs=out_specs, check_vma=False
    )
```

```python
import functools

import jax
import jax.numpy as jnp
from jax import lax
from jax.experimental import pallas as pl
from jax.experimental.pallas import tpu as pltpu
from jax.sharding import PartitionSpec as P

CLUS_GRP = 2
TILES = 4
LABEL_ROWS = 16
FAR = 1.0e9
LONG = 20_000_000_000
PACK_VMEM = 60 * 1024 * 1024
COMPARE_VMEM = 24 * 1024 * 1024
NT = (((1,), (1,)), ((), ()))
TN = (((0,), (0,)), ((), ()))


def cover(members):
    bits = [1 << i for i in range(members.bit_length() - 1)]
    offsets = [0] + bits

    def missing(held):
        return set(range(members)) - {a ^ b for a in held for b in held}

    while missing(offsets):
        offsets.append(
            min(
                (d for d in range(members) if d not in offsets),
                key=lambda d: (len(missing(offsets + [d])), bin(d).count("1"), -d),
            )
        )
    pairs = {}
    for delta in range(members):
        pairs[delta] = min(
            (a, a ^ delta) for a in offsets if a ^ delta in offsets
        )
    return offsets, pairs


def pack_kernel(sizes, ks, placed, emb_hbm, cluster_hbm, rank_hbm, *refs):
    groups, halves, half, cap, blk = sizes
    outs, refs = refs[: len(ks)], refs[len(ks) :]
    if placed:
        dest_ref, *refs = refs
    emb_ref, cluster_ref, rank_ref, stage, sems, out_sems = refs
    rows = emb_ref.shape[0]
    step = 256
    loads = [
        pltpu.make_async_copy(cluster_hbm, cluster_ref, sems.at[0]),
        pltpu.make_async_copy(rank_hbm, rank_ref, sems.at[1]),
    ]
    for j in range(rows // step):
        at = pl.ds(j * step, step)
        loads.append(pltpu.make_async_copy(emb_hbm.at[at], emb_ref.at[at], sems.at[2 + j]))
    for load in loads:
        load.start()
    for load in loads[:2]:
        load.wait()
    cluster = cluster_ref[...]
    rank = rank_ref[...]
    alive = cluster >= 0
    pair = lax.shift_right_logical(jnp.maximum(cluster, 0), 1)
    parity = jnp.maximum(cluster, 0) - 2 * pair
    safe_rank = jnp.maximum(rank, 0)
    which = safe_rank // half
    units = groups * halves
    unit_id = jnp.where(alive, pair * halves + which, -1)
    before_rows = lax.broadcasted_iota(jnp.int32, (step, step), 0)
    before_cols = lax.broadcasted_iota(jnp.int32, (step, step), 1)
    upper = (before_rows < before_cols).astype(jnp.float32).astype(jnp.bfloat16)
    unit_iota = lax.broadcasted_iota(jnp.int32, (units, step), 0)
    carry = jnp.zeros((units, 1), jnp.float32)
    places = []
    for j in range(rows // step):
        mine = unit_id[:, j * step : (j + 1) * step]
        hit = (unit_iota == mine).astype(jnp.float32)
        before = jnp.dot(hit.astype(jnp.bfloat16), upper, preferred_element_type=jnp.float32) + carry
        position = jnp.sum(hit * before, axis=0, keepdims=True)
        carry = carry + jnp.sum(hit, axis=1, keepdims=True)
        places.append(jnp.where(mine >= 0, mine * cap + position.astype(jnp.int32), -1))
    dest = jnp.concatenate(places, axis=1)
    if placed:
        dest_ref[...] = dest
    members = halves // 2
    side = members // groups
    here = lax.axis_index("mem") // side
    dest = jnp.where(dest >= 0, dest ^ (here * blk), -1)

    field = lax.broadcasted_iota(jnp.int32, (LABEL_ROWS, rows), 0)
    labels = jnp.where(
        field == 0, safe_rank - which * half, jnp.where(field == 1, parity + 1, 0)
    )
    labels = jnp.where(alive, labels, 0).astype(jnp.float32).astype(jnp.bfloat16)
    unit_of = lax.div(lax.broadcasted_iota(jnp.int32, (1, blk), 1), cap).astype(jnp.float32)
    slot = lax.broadcasted_iota(jnp.int32, (blk, rows), 0)
    line = lax.broadcasted_iota(jnp.int32, (LABEL_ROWS, blk), 0)
    width = emb_ref.shape[1]
    leaving = []
    for n, k in enumerate(ks):
        pick = (slot + k * blk == dest).astype(jnp.float32).astype(jnp.bfloat16)
        if n == 0:
            for load in loads[2:]:
                load.wait()
        wide = jnp.dot(pick, emb_ref[...], preferred_element_type=jnp.float32)
        total = jnp.sum(wide * wide, axis=1, keepdims=True)
        stage[n, 0:blk, :] = (wide * lax.rsqrt(total + 1e-06)).astype(jnp.bfloat16)
        mine = lax.dot_general(labels, pick, NT, preferred_element_type=jnp.float32)
        high = unit_of + float(halves) * mine[1:2]
        strip = jnp.where(line == 0, mine[0:1], jnp.where(line == 1, high, 0.0))
        strip = jnp.concatenate([strip, jnp.zeros((LABEL_ROWS, width - blk), jnp.float32)], axis=1)
        stage[n, blk : blk + LABEL_ROWS, :] = strip.astype(jnp.bfloat16)
        leaving.append(pltpu.make_async_copy(stage.at[n], outs[n], out_sems.at[n]))
        leaving[-1].start()
    for copy in leaving:
        copy.wait()


def pack(embeddings, cluster, rank, ks, placed, sizes):
    groups, halves, half, cap, blk = sizes
    rows, width = embeddings.shape
    hbm = pl.BlockSpec(memory_space=pltpu.HBM)
    vmem = pl.BlockSpec(memory_space=pltpu.VMEM)
    out_shape = [jax.ShapeDtypeStruct((blk + LABEL_ROWS, width), jnp.bfloat16)] * len(ks)
    out_specs = [hbm] * len(ks)
    if placed:
        out_shape.append(jax.ShapeDtypeStruct((1, rows), jnp.int32))
        out_specs.append(vmem)
    return pl.pallas_call(
        functools.partial(pack_kernel, sizes, ks, placed),
        out_shape=out_shape,
        in_specs=[hbm, hbm, hbm],
        out_specs=out_specs,
        scratch_shapes=[
            pltpu.VMEM((rows, width), jnp.bfloat16),
            pltpu.VMEM((1, rows), jnp.int32),
            pltpu.VMEM((1, rows), jnp.int32),
            pltpu.VMEM((len(ks), blk + LABEL_ROWS, width), jnp.bfloat16),
            pltpu.SemaphoreType.DMA((2 + rows // 256,)),
            pltpu.SemaphoreType.DMA((len(ks),)),
        ],
        compiler_params=pltpu.CompilerParams(vmem_limit_bytes=PACK_VMEM),
        cost_estimate=pl.CostEstimate(
            flops=LONG if placed else 0, bytes_accessed=4 * rows * width, transcendentals=0
        ),
    )(embeddings, cluster.reshape(1, rows), rank.reshape(1, rows))


def compare_kernel(sizes, jobs, names, spots, starts, wholes, joined, has_prev, keep, reuse, *refs):
    groups, halves, half, cap, blk = sizes
    array = dict(zip(names, refs))
    refs = refs[len(names) :]
    block = {piece: (array[name], row) for piece, (name, row, _, _) in spots.items()}
    prev = None
    if has_prev:
        prev, refs = refs[0], refs[1:]
    if reuse:
        turned, *refs = refs
        *outs, key_col, best = refs
    elif keep:
        *outs, turned, key_col, best = refs
    else:
        *outs, key_col, best, turned = refs
    rows = groups * blk
    per_tile = blk // TILES
    tile = rows // TILES
    cap_all = float(halves * half)

    side = halves // 2 // groups
    along = lax.axis_index("mem")

    def strip_of(piece):
        name, _, first, left = spots[piece]
        return array[name][first : first + LABEL_ROWS, left : left + blk]

    def keys_of(piece):
        strip = strip_of(piece).astype(jnp.float32)
        return strip[0:1] + float(half) * strip[1:2]

    weight_row = lax.broadcasted_iota(jnp.int32, (LABEL_ROWS, 128), 0)
    weights = jnp.where(weight_row == 0, 1.0, jnp.where(weight_row == 1, float(half), 0.0))
    weights = weights.astype(jnp.bfloat16)
    needed = sorted({piece for *_, pieces in jobs for piece in pieces})
    key_at = {piece: n * blk for n, piece in enumerate(needed)}
    for piece in needed:
        key_col[pl.ds(key_at[piece], blk), :] = lax.dot_general(
            strip_of(piece), weights, TN, preferred_element_type=jnp.float32
        )
    lane = lax.div(lax.broadcasted_iota(jnp.int32, (1, tile), 1), per_tile)

    def floor_of(key):
        low = jnp.floor(key * (1.0 / cap_all)) * cap_all
        return jnp.where(low > 0.5, low, FAR)

    def lines_of(a, ks):
        keys = [keys_of((a, k)) if k in ks else jnp.zeros((1, blk), jnp.float32) for k in range(groups)]
        keys = [jnp.concatenate([key] * (tile // blk), axis=1) for key in keys]
        lines = []
        for t in range(TILES):
            line = jnp.zeros((1, tile), jnp.float32)
            for k in range(groups):
                turn = ((k - t) * per_tile) % tile
                moved = pltpu.roll(keys[k], turn, 1) if turn else keys[k]
                line = jnp.where(lane == k, moved, line)
            lines.append(line)
        return lines

    def rows_of(ref, base, first, last):
        return ref[base + first * per_tile : base + last * per_tile, :]

    best[...] = prev[...] if has_prev else jnp.full(best.shape, -1.0, jnp.float32)

    def search(a, row, queries, mine, pieces, last, spot):
        width = mine.shape[1]
        if not reuse:
            turned[spot, :, 0:width] = jnp.concatenate(queries, axis=0).T
        floor = floor_of(mine)
        acc = jnp.full((8, width), -1.0, jnp.float32)
        for at in range(0, len(pieces), groups):
            some = pieces[at : at + groups]
            theirs = [rows_of(key_col, key_at[piece], 0, last) for piece in some]
            theirs = jnp.concatenate(theirs, axis=0)
            theirs = jnp.concatenate([theirs] * (width // 128), axis=1)
            sims = jnp.dot(
                jnp.concatenate([rows_of(*block[piece], 0, last) for piece in some], axis=0),
                turned[spot, :, 0:width],
                preferred_element_type=jnp.float32,
            )
            keep = (theirs >= floor) & (theirs < mine)
            sims = jnp.where(keep, sims, -1.0)
            top = jnp.max(sims.reshape(sims.shape[0] // 8, 8, width), axis=0)
            acc = jnp.maximum(acc, top)
        best[a, row : row + 1, 0:width] = jnp.maximum(
            best[a, row : row + 1, 0:width], jnp.max(acc, axis=0, keepdims=True)
        )

    spot = 0
    for a, whole, ks, pieces in jobs:
        if whole:
            (k,) = ks
            queries = [rows_of(*block[a, k], 0, TILES)]
            search(a, TILES, queries, keys_of((a, k)), pieces, TILES, spot)
            spot += 1
            continue
        lines = lines_of(a, ks)
        for t in range(TILES):
            queries = [rows_of(*block[a, k if k in ks else ks[0]], t, t + 1) for k in range(groups)]
            search(a, t, queries, lines[t], pieces, t + 1, spot)
            spot += 1

    if not starts:
        outs[0][...] = best[...]
        return
    for o, a in enumerate(starts):
        found = best[a]
        for k in range(groups):
            total = jnp.full((1, tile), -1.0, jnp.float32)
            for t in range(TILES):
                turn = ((t - k) * per_tile) % tile
                moved = pltpu.roll(found, turn, 1) if turn else found
                total = jnp.where(lane == t, moved[t : t + 1], total)
            if (a, k) in wholes:
                total = jnp.maximum(total, found[TILES : TILES + 1])
            at = (along // side) ^ k
            if joined:
                outs[0][pl.ds(at * joined + ((along % side) ^ a), 1), 0, :] = total[:, :blk]
            else:
                outs[o][pl.ds(at, 1), 0, :] = total[:, :blk]


def compare(blocks, jobs, prev, starts, wholes, joined, offsets, sizes, keep=False, cache=None):
    groups, halves, half, cap, blk = sizes
    n_sets = len(offsets)
    used = {piece for *_, pieces in jobs for piece in pieces}
    used |= {(a, k) for a, _, ks, _ in jobs for k in ks}
    searches = sum(1 if whole else TILES for _, whole, _, _ in jobs)
    spots = {}
    arrays = {}
    for piece in sorted(used):
        value, *where = blocks[piece]
        name = next((n for n, v in arrays.items() if v is value), None)
        if name is None:
            name = len(arrays)
            arrays[name] = value
        spots[piece] = (name, *where)
    names = list(arrays)
    width = arrays[0].shape[1]
    tile = groups * blk // TILES
    vmem = pl.BlockSpec(memory_space=pltpu.VMEM)
    work = blk * tile * width * sum(
        len(pieces) * (1.0 if whole else (TILES + 1) / 2 / TILES) for _, whole, _, pieces in jobs
    )
    if not starts:
        out_shape = [jax.ShapeDtypeStruct((n_sets, 8, tile), jnp.float32)]
    elif joined:
        out_shape = [jax.ShapeDtypeStruct((groups * joined, 1, blk), jnp.float32)]
    else:
        out_shape = [jax.ShapeDtypeStruct((groups, 1, blk), jnp.float32)] * len(starts)
    operands = list(arrays.values()) + ([] if prev is None else [prev])
    scratch = []
    shape = (searches, width, tile)
    if cache is not None:
        operands.append(cache)
    elif keep:
        out_shape.append(jax.ShapeDtypeStruct(shape, jnp.bfloat16))
    else:
        scratch.append(pltpu.VMEM(shape, jnp.bfloat16))
    needed = {piece for *_, pieces in jobs for piece in pieces}
    return pl.pallas_call(
        functools.partial(
            compare_kernel,
            sizes,
            jobs,
            names,
            spots,
            starts,
            wholes,
            joined,
            prev is not None,
            keep,
            cache is not None,
        ),
        out_shape=out_shape,
        in_specs=[vmem] * len(operands),
        out_specs=[vmem] * len(out_shape),
        scratch_shapes=[
            pltpu.VMEM((len(needed) * blk, 128), jnp.float32),
            pltpu.VMEM((n_sets, 8, tile), jnp.float32),
            *scratch,
        ],
        compiler_params=pltpu.CompilerParams(vmem_limit_bytes=COMPARE_VMEM),
        cost_estimate=pl.CostEstimate(
            flops=int(2 * work), bytes_accessed=2 * len(used) * blk * width, transcendentals=0
        ),
    )(*operands)


def pair_kernel(*refs):
    out_ref, ins = refs[-1], refs[:-1]
    blk, width = ins[0].shape[0] - LABEL_ROWS, ins[0].shape[1]
    parts = []
    for n, ref in enumerate(ins):
        out_ref[n * blk : (n + 1) * blk, :] = ref[0:blk, :]
        parts.append(ref[blk : blk + LABEL_ROWS, 0:blk])
    parts.append(jnp.zeros((LABEL_ROWS, width - len(ins) * blk), jnp.bfloat16))
    out_ref[len(ins) * blk :, :] = jnp.concatenate(parts, axis=1)


def pile_kernel(*refs):
    out_ref, ins = refs[-1], refs[:-1]
    row, strip = 0, out_ref.shape[0] - LABEL_ROWS * len(ins)
    for ref in ins:
        rows = ref.shape[0] - LABEL_ROWS
        out_ref[row : row + rows, :] = ref[0:rows, :]
        out_ref[strip : strip + LABEL_ROWS, :] = ref[rows : rows + LABEL_ROWS, :]
        row, strip = row + rows, strip + LABEL_ROWS


def join(kernel, pieces, rows):
    vmem = pl.BlockSpec(memory_space=pltpu.VMEM)
    return pl.pallas_call(
        kernel,
        out_shape=jax.ShapeDtypeStruct((rows, pieces[0].shape[1]), pieces[0].dtype),
        in_specs=[vmem] * len(pieces),
        out_specs=vmem,
        compiler_params=pltpu.CompilerParams(vmem_limit_bytes=COMPARE_VMEM),
    )(*pieces)


def unpack_kernel(sizes, dest_ref, back_ref, out_ref):
    groups, halves, half, cap, blk = sizes
    side = back_ref.shape[0] // groups
    rows = dest_ref.shape[1]
    dest = dest_ref[...]
    slot = lax.broadcasted_iota(jnp.int32, (blk, rows), 0)
    field = lax.broadcasted_iota(jnp.int32, (LABEL_ROWS, blk), 0)
    total = jnp.zeros((LABEL_ROWS, rows), jnp.float32)
    for k in range(groups):
        value = back_ref[k * side]
        for more in range(1, side):
            value = jnp.maximum(value, back_ref[k * side + more])
        top = value.astype(jnp.bfloat16).astype(jnp.float32)
        rest = value - top
        mid = rest.astype(jnp.bfloat16).astype(jnp.float32)
        low = rest - mid
        stack = jnp.where(field == 0, top, jnp.where(field == 1, mid, jnp.where(field == 2, low, 0.0)))
        pick = (slot + k * blk == dest).astype(jnp.float32).astype(jnp.bfloat16)
        total = total + jnp.dot(stack.astype(jnp.bfloat16), pick, preferred_element_type=jnp.float32)
    value = (total[0:1] + total[1:2]) + total[2:3]
    out_ref[...] = jnp.where(dest >= 0, value, -1.0)


def unpack(dest, back, sizes):
    vmem = pl.BlockSpec(memory_space=pltpu.VMEM)
    return pl.pallas_call(
        functools.partial(unpack_kernel, sizes),
        out_shape=jax.ShapeDtypeStruct(dest.shape, jnp.float32),
        in_specs=[vmem] * 2,
        out_specs=vmem,
        compiler_params=pltpu.CompilerParams(vmem_limit_bytes=COMPARE_VMEM),
    )(dest, back)


def on_device(embeddings, cluster, rank):
    rows_dev, width = embeddings.shape
    groups = lax.axis_size("grp")
    members = lax.axis_size("mem")
    devices = groups * members
    halves = 2 * members
    half = rows_dev // CLUS_GRP // 2
    blk = rows_dev // groups
    cap = blk // halves
    sizes = (groups, halves, half, cap, blk)
    side = members // groups

    def swap(value, block_step, member_step):
        mask = member_step // side * members + block_step * side + member_step % side
        if mask == 0:
            return value
        return lax.ppermute(value, ("grp", "mem"), [(i, i ^ mask) for i in range(devices)])

    offsets, pairs = cover(members)
    sends = [None] * groups
    first = (2,)
    for k, value in zip(first, pack(embeddings, cluster, rank, first, False, sizes)):
        sends[k] = value
    rest = (1, 0, *range(3, groups))
    cluster, sends[2] = lax.optimization_barrier((cluster, sends[2]))
    *packed, dest = pack(embeddings, cluster, rank, rest, True, sizes)
    for k, value in zip(rest, packed):
        sends[k] = value

    last = groups - 1
    far = [d for d in offsets if d & side and d != side and d ^ side in offsets]
    near = [d for d in offsets[1:] if d not in far]
    lead = far[0] ^ side if far else near[0]
    held = {0: [sends[0]]}
    for d in near:
        held[d] = [swap(sends[0], 0, d)]
    after = held[lead][0]
    for k in range(1, groups, 2):
        if k > 1:
            send, after = lax.optimization_barrier((sends[k], after))
        else:
            send = sends[k]
        mine = swap(send, k, 0)
        if k < last:
            also = swap(sends[k + 1], k + 1, 0)
            mine = join(pair_kernel, [mine, also], 2 * blk + LABEL_ROWS)
            if k == 1:
                mine, *firsts = lax.optimization_barrier((mine, *(held[d][0] for d in near)))
                for d, value in zip(near, firsts):
                    held[d] = [value]
            after = mine
        held[0].append(mine)
    spots = len(held[0])
    for spot in range(1, spots):
        for d in near:
            if d != side:
                held[d].append(swap(held[0][spot], 0, d))

    index = {d: i for i, d in enumerate(offsets)}
    blocks = {}

    def ks_of(spot):
        return [0] if spot == 0 else [k for k in (2 * spot - 1, 2 * spot) if k < groups]

    def note(d, spot):
        value = held[d][spot]
        first = value.shape[0] - LABEL_ROWS
        for at, k in enumerate(ks_of(spot)):
            blocks[index[d], k] = (value, at * blk, first, at * blk)

    for d in held:
        for spot in range(len(held[d])):
            note(d, spot)
    pile = [(side, spot) for spot in range(1, spots)]
    pile += [(d, spot) for d in far for spot in range(spots - 1)]
    hops = [d for d in near if d != side and d not in [e ^ side for e in far]]
    values = [held[d][spots - 2] for d in hops]
    held[0][-1], *values = lax.optimization_barrier((held[0][-1], *values))
    for d, value in zip(hops, values):
        held[d][spots - 2] = value
        note(d, spots - 2)
    note(0, spots - 1)
    parts = [held[d ^ side][spot] for d, spot in pile]
    data = sum(part.shape[0] - LABEL_ROWS for part in parts)
    moved = swap(join(pile_kernel, parts, data + LABEL_ROWS * len(parts)), 0, side)
    row = 0
    for n, (d, spot) in enumerate(pile):
        for at, k in enumerate(ks_of(spot)):
            blocks[index[d], k] = (moved, row + at * blk, data + LABEL_ROWS * n, at * blk)
        row += parts[n].shape[0] - LABEL_ROWS
    slow = {(index[d], k) for d, spot in pile for k in ks_of(spot)}

    starts = sorted({a for a, _ in pairs.values()})
    every = tuple(range(groups))
    early, middle, late = [], [], []
    for a in starts:
        cols = [index[b] for _, (e, b) in sorted(pairs.items()) if e == a]
        pieces = [(b, k) for b in cols for k in every]
        soon = [(b, k) for b, k in pieces if k < last]
        if a == 0:
            ready = [piece for piece in pieces if piece in soon or piece[0] == 0]
            early.append((0, False, every, [piece for piece in ready if piece not in slow]))
            middle.append((0, False, every, [piece for piece in pieces if piece in slow]))
            done = early[-1][-1] + middle[-1][-1]
            late.append((0, False, every, [piece for piece in pieces if piece not in done]))
        else:
            middle.append((index[a], False, every[:-1], soon))
            late.append((index[a], False, every, [piece for piece in pieces if piece not in soon]))
            late.append((index[a], True, (last,), soon))
    order = [index[a] for a in starts]
    joined = side if all(a < side for a in starts) else 0
    prev = compare(blocks, early, None, (), (), 0, offsets, sizes)[0]
    prev = compare(blocks, middle, prev, (), (), 0, offsets, sizes)[0]
    wholes = [(a, k) for a, whole, ks, _ in late if whole for k in ks]
    if far:
        final = {(index[d], last) for d in far}
        before = [(*job, [p for p in pieces if p not in final]) for *job, pieces in late]
        late = [(*job, [p for p in pieces if p in final]) for *job, pieces in late]
        late = [job for job in late if job[-1]]
        for d in far:
            piece, prev = lax.optimization_barrier((held[d ^ side][-1], prev))
            held[d] = {spots - 1: swap(piece, 0, side)}
            note(d, spots - 1)
        prev, turned = compare(blocks, before, prev, (), (), 0, offsets, sizes, keep=True)
        found = compare(blocks, late, prev, order, wholes, joined, offsets, sizes, cache=turned)
    else:
        found = compare(blocks, late, prev, order, wholes, joined, offsets, sizes)
    if joined:
        back = found[0]
    else:
        best = {}
        for a, value in zip(starts, found):
            near = a % side
            value = swap(value, 0, a - near)
            best[near] = jnp.maximum(best[near], value) if near in best else value
        none = jnp.full_like(found[0], -1.0)
        near_of = [best.get(near, none) for near in range(side)]
        rows_of = []
        for spot in range(side):
            value = near_of[spot]
            for mine in range(1, side):
                value = jnp.where(lax.axis_index("mem") % side == mine, near_of[spot ^ mine], value)
            rows_of.append(value)
        back = jnp.stack(rows_of, axis=1).reshape(groups * side, 1, blk)
    back = lax.all_to_all(back, "mem", split_axis=0, concat_axis=0, tiled=True)
    return unpack(dest, back, sizes).reshape(rows_dev)


def solution(mesh):
    in_specs = (P(("grp", "mem"), None), P(("grp", "mem")), P(("grp", "mem")))
    out_specs = P(("grp", "mem"))
    return jax.shard_map(
        on_device, mesh=mesh, in_specs=in_specs, out_specs=out_specs, check_vma=False
    )
```

```python
import functools

import jax
import jax.numpy as jnp
from jax import lax
from jax.experimental import pallas as pl
from jax.experimental.pallas import tpu as pltpu
from jax.sharding import PartitionSpec as P

CLUS_GRP = 2
TILES = 4
LABEL_ROWS = 16
FAR = 1.0e9
PACK_VMEM = 60 * 1024 * 1024
COMPARE_VMEM = 24 * 1024 * 1024
NT = (((1,), (1,)), ((), ()))
TN = (((0,), (0,)), ((), ()))


def cover(members):
    bits = [1 << i for i in range(members.bit_length() - 1)]
    offsets = [0] + bits

    def missing(held):
        return set(range(members)) - {a ^ b for a in held for b in held}

    while missing(offsets):
        offsets.append(
            min(
                (d for d in range(members) if d not in offsets),
                key=lambda d: (len(missing(offsets + [d])), bin(d).count("1"), -d),
            )
        )
    pairs = {}
    for delta in range(members):
        pairs[delta] = min(
            (a, a ^ delta) for a in offsets if a ^ delta in offsets
        )
    return offsets, pairs


def pack_kernel(sizes, ks, placed, emb_hbm, cluster_hbm, rank_hbm, *refs):
    groups, halves, half, cap, blk = sizes
    outs, refs = refs[: len(ks)], refs[len(ks) :]
    if placed:
        dest_ref, *refs = refs
    emb_ref, cluster_ref, rank_ref, stage, sems, out_sems = refs
    rows = emb_ref.shape[0]
    step = 256
    loads = [
        pltpu.make_async_copy(cluster_hbm, cluster_ref, sems.at[0]),
        pltpu.make_async_copy(rank_hbm, rank_ref, sems.at[1]),
    ]
    for j in range(rows // step):
        at = pl.ds(j * step, step)
        loads.append(pltpu.make_async_copy(emb_hbm.at[at], emb_ref.at[at], sems.at[2 + j]))
    for load in loads:
        load.start()
    for load in loads[:2]:
        load.wait()
    cluster = cluster_ref[...]
    rank = rank_ref[...]
    alive = cluster >= 0
    pair = lax.shift_right_logical(jnp.maximum(cluster, 0), 1)
    parity = jnp.maximum(cluster, 0) - 2 * pair
    safe_rank = jnp.maximum(rank, 0)
    which = safe_rank // half
    units = groups * halves
    unit_id = jnp.where(alive, pair * halves + which, -1)
    before_rows = lax.broadcasted_iota(jnp.int32, (step, step), 0)
    before_cols = lax.broadcasted_iota(jnp.int32, (step, step), 1)
    upper = (before_rows < before_cols).astype(jnp.float32).astype(jnp.bfloat16)
    unit_iota = lax.broadcasted_iota(jnp.int32, (units, step), 0)
    carry = jnp.zeros((units, 1), jnp.float32)
    places = []
    for j in range(rows // step):
        mine = unit_id[:, j * step : (j + 1) * step]
        hit = (unit_iota == mine).astype(jnp.float32)
        before = jnp.dot(hit.astype(jnp.bfloat16), upper, preferred_element_type=jnp.float32) + carry
        position = jnp.sum(hit * before, axis=0, keepdims=True)
        carry = carry + jnp.sum(hit, axis=1, keepdims=True)
        places.append(jnp.where(mine >= 0, mine * cap + position.astype(jnp.int32), -1))
    dest = jnp.concatenate(places, axis=1)
    if placed:
        dest_ref[...] = dest
    members = halves // 2
    side = members // groups
    here = lax.axis_index("mem") // side
    dest = jnp.where(dest >= 0, dest ^ (here * blk), -1)

    field = lax.broadcasted_iota(jnp.int32, (LABEL_ROWS, rows), 0)
    labels = jnp.where(
        field == 0, safe_rank - which * half, jnp.where(field == 1, parity + 1, 0)
    )
    labels = jnp.where(alive, labels, 0).astype(jnp.float32).astype(jnp.bfloat16)
    unit_of = lax.div(lax.broadcasted_iota(jnp.int32, (1, blk), 1), cap).astype(jnp.float32)
    slot = lax.broadcasted_iota(jnp.int32, (blk, rows), 0)
    line = lax.broadcasted_iota(jnp.int32, (LABEL_ROWS, blk), 0)
    width = emb_ref.shape[1]
    leaving = []
    for n, k in enumerate(ks):
        pick = (slot + k * blk == dest).astype(jnp.float32).astype(jnp.bfloat16)
        if n == 0:
            for load in loads[2:]:
                load.wait()
        wide = jnp.dot(pick, emb_ref[...], preferred_element_type=jnp.float32)
        total = jnp.sum(wide * wide, axis=1, keepdims=True)
        stage[n, 0:blk, :] = (wide * lax.rsqrt(total + 1e-06)).astype(jnp.bfloat16)
        mine = lax.dot_general(labels, pick, NT, preferred_element_type=jnp.float32)
        high = unit_of + float(halves) * mine[1:2]
        strip = jnp.where(line == 0, mine[0:1], jnp.where(line == 1, high, 0.0))
        strip = jnp.concatenate([strip, jnp.zeros((LABEL_ROWS, width - blk), jnp.float32)], axis=1)
        stage[n, blk : blk + LABEL_ROWS, :] = strip.astype(jnp.bfloat16)
        leaving.append(pltpu.make_async_copy(stage.at[n], outs[n], out_sems.at[n]))
        leaving[-1].start()
    for copy in leaving:
        copy.wait()


def pack(embeddings, cluster, rank, ks, placed, sizes):
    groups, halves, half, cap, blk = sizes
    rows, width = embeddings.shape
    hbm = pl.BlockSpec(memory_space=pltpu.HBM)
    vmem = pl.BlockSpec(memory_space=pltpu.VMEM)
    out_shape = [jax.ShapeDtypeStruct((blk + LABEL_ROWS, width), jnp.bfloat16)] * len(ks)
    out_specs = [hbm] * len(ks)
    if placed:
        out_shape.append(jax.ShapeDtypeStruct((1, rows), jnp.int32))
        out_specs.append(vmem)
    return pl.pallas_call(
        functools.partial(pack_kernel, sizes, ks, placed),
        out_shape=out_shape,
        in_specs=[hbm, hbm, hbm],
        out_specs=out_specs,
        scratch_shapes=[
            pltpu.VMEM((rows, width), jnp.bfloat16),
            pltpu.VMEM((1, rows), jnp.int32),
            pltpu.VMEM((1, rows), jnp.int32),
            pltpu.VMEM((len(ks), blk + LABEL_ROWS, width), jnp.bfloat16),
            pltpu.SemaphoreType.DMA((2 + rows // 256,)),
            pltpu.SemaphoreType.DMA((len(ks),)),
        ],
        compiler_params=pltpu.CompilerParams(vmem_limit_bytes=PACK_VMEM),
        cost_estimate=pl.CostEstimate(
            flops=2 * len(ks) * blk * rows * width, bytes_accessed=4 * rows * width, transcendentals=0
        ),
    )(embeddings, cluster.reshape(1, rows), rank.reshape(1, rows))


def compare_kernel(sizes, jobs, names, spots, starts, wholes, joined, has_prev, keep, reuse, *refs):
    groups, halves, half, cap, blk = sizes
    array = dict(zip(names, refs))
    refs = refs[len(names) :]
    block = {piece: (array[name], row) for piece, (name, row, _, _) in spots.items()}
    prev = None
    if has_prev:
        prev, refs = refs[0], refs[1:]
    if reuse:
        turned, *refs = refs
        *outs, key_col, best = refs
    elif keep:
        *outs, turned, key_col, best = refs
    else:
        *outs, key_col, best, turned = refs
    rows = groups * blk
    per_tile = blk // TILES
    tile = rows // TILES
    cap_all = float(halves * half)

    side = halves // 2 // groups
    along = lax.axis_index("mem")

    def strip_of(piece):
        name, _, first, left = spots[piece]
        return array[name][first : first + LABEL_ROWS, left : left + blk]

    def keys_of(piece):
        strip = strip_of(piece).astype(jnp.float32)
        return strip[0:1] + float(half) * strip[1:2]

    weight_row = lax.broadcasted_iota(jnp.int32, (LABEL_ROWS, 128), 0)
    weights = jnp.where(weight_row == 0, 1.0, jnp.where(weight_row == 1, float(half), 0.0))
    weights = weights.astype(jnp.bfloat16)
    needed = sorted({piece for *_, pieces in jobs for piece in pieces})
    key_at = {piece: n * blk for n, piece in enumerate(needed)}
    for piece in needed:
        key_col[pl.ds(key_at[piece], blk), :] = lax.dot_general(
            strip_of(piece), weights, TN, preferred_element_type=jnp.float32
        )
    lane = lax.div(lax.broadcasted_iota(jnp.int32, (1, tile), 1), per_tile)

    def floor_of(key):
        low = jnp.floor(key * (1.0 / cap_all)) * cap_all
        return jnp.where(low > 0.5, low, FAR)

    def lines_of(a, ks):
        keys = [keys_of((a, k)) if k in ks else jnp.zeros((1, blk), jnp.float32) for k in range(groups)]
        keys = [jnp.concatenate([key] * (tile // blk), axis=1) for key in keys]
        lines = []
        for t in range(TILES):
            line = jnp.zeros((1, tile), jnp.float32)
            for k in range(groups):
                turn = ((k - t) * per_tile) % tile
                moved = pltpu.roll(keys[k], turn, 1) if turn else keys[k]
                line = jnp.where(lane == k, moved, line)
            lines.append(line)
        return lines

    def rows_of(ref, base, first, last):
        return ref[base + first * per_tile : base + last * per_tile, :]

    best[...] = prev[...] if has_prev else jnp.full(best.shape, -1.0, jnp.float32)

    def search(a, row, queries, mine, pieces, last, spot):
        width = mine.shape[1]
        if not reuse:
            turned[spot, :, 0:width] = jnp.concatenate(queries, axis=0).T
        floor = floor_of(mine)
        acc = jnp.full((8, width), -1.0, jnp.float32)
        for at in range(0, len(pieces), groups):
            some = pieces[at : at + groups]
            theirs = [rows_of(key_col, key_at[piece], 0, last) for piece in some]
            theirs = jnp.concatenate(theirs, axis=0)
            theirs = jnp.concatenate([theirs] * (width // 128), axis=1)
            sims = jnp.dot(
                jnp.concatenate([rows_of(*block[piece], 0, last) for piece in some], axis=0),
                turned[spot, :, 0:width],
                preferred_element_type=jnp.float32,
            )
            keep = (theirs >= floor) & (theirs < mine)
            sims = jnp.where(keep, sims, -1.0)
            top = jnp.max(sims.reshape(sims.shape[0] // 8, 8, width), axis=0)
            acc = jnp.maximum(acc, top)
        best[a, row : row + 1, 0:width] = jnp.maximum(
            best[a, row : row + 1, 0:width], jnp.max(acc, axis=0, keepdims=True)
        )

    spot = 0
    for a, whole, ks, pieces in jobs:
        if whole:
            (k,) = ks
            queries = [rows_of(*block[a, k], 0, TILES)]
            search(a, TILES, queries, keys_of((a, k)), pieces, TILES, spot)
            spot += 1
            continue
        lines = lines_of(a, ks)
        for t in range(TILES):
            queries = [rows_of(*block[a, k if k in ks else ks[0]], t, t + 1) for k in range(groups)]
            search(a, t, queries, lines[t], pieces, t + 1, spot)
            spot += 1

    if not starts:
        outs[0][...] = best[...]
        return
    for o, a in enumerate(starts):
        found = best[a]
        for k in range(groups):
            total = jnp.full((1, tile), -1.0, jnp.float32)
            for t in range(TILES):
                turn = ((t - k) * per_tile) % tile
                moved = pltpu.roll(found, turn, 1) if turn else found
                total = jnp.where(lane == t, moved[t : t + 1], total)
            if (a, k) in wholes:
                total = jnp.maximum(total, found[TILES : TILES + 1])
            at = (along // side) ^ k
            if joined:
                outs[0][pl.ds(at * joined + ((along % side) ^ a), 1), 0, :] = total[:, :blk]
            else:
                outs[o][pl.ds(at, 1), 0, :] = total[:, :blk]


def compare(blocks, jobs, prev, starts, wholes, joined, offsets, sizes, keep=False, cache=None):
    groups, halves, half, cap, blk = sizes
    n_sets = len(offsets)
    used = {piece for *_, pieces in jobs for piece in pieces}
    used |= {(a, k) for a, _, ks, _ in jobs for k in ks}
    searches = sum(1 if whole else TILES for _, whole, _, _ in jobs)
    spots = {}
    arrays = {}
    for piece in sorted(used):
        value, *where = blocks[piece]
        name = next((n for n, v in arrays.items() if v is value), None)
        if name is None:
            name = len(arrays)
            arrays[name] = value
        spots[piece] = (name, *where)
    names = list(arrays)
    width = arrays[0].shape[1]
    tile = groups * blk // TILES
    vmem = pl.BlockSpec(memory_space=pltpu.VMEM)
    work = blk * tile * width * sum(
        len(pieces) * (1.0 if whole else (TILES + 1) / 2 / TILES) for _, whole, _, pieces in jobs
    )
    if not starts:
        out_shape = [jax.ShapeDtypeStruct((n_sets, 8, tile), jnp.float32)]
    elif joined:
        out_shape = [jax.ShapeDtypeStruct((groups * joined, 1, blk), jnp.float32)]
    else:
        out_shape = [jax.ShapeDtypeStruct((groups, 1, blk), jnp.float32)] * len(starts)
    operands = list(arrays.values()) + ([] if prev is None else [prev])
    scratch = []
    shape = (searches, width, tile)
    if cache is not None:
        operands.append(cache)
    elif keep:
        out_shape.append(jax.ShapeDtypeStruct(shape, jnp.bfloat16))
    else:
        scratch.append(pltpu.VMEM(shape, jnp.bfloat16))
    needed = {piece for *_, pieces in jobs for piece in pieces}
    return pl.pallas_call(
        functools.partial(
            compare_kernel,
            sizes,
            jobs,
            names,
            spots,
            starts,
            wholes,
            joined,
            prev is not None,
            keep,
            cache is not None,
        ),
        out_shape=out_shape,
        in_specs=[vmem] * len(operands),
        out_specs=[vmem] * len(out_shape),
        scratch_shapes=[
            pltpu.VMEM((len(needed) * blk, 128), jnp.float32),
            pltpu.VMEM((n_sets, 8, tile), jnp.float32),
            *scratch,
        ],
        compiler_params=pltpu.CompilerParams(vmem_limit_bytes=COMPARE_VMEM),
        cost_estimate=pl.CostEstimate(
            flops=int(2 * work), bytes_accessed=2 * len(used) * blk * width, transcendentals=0
        ),
    )(*operands)


def pair_kernel(*refs):
    out_ref, ins = refs[-1], refs[:-1]
    blk, width = ins[0].shape[0] - LABEL_ROWS, ins[0].shape[1]
    parts = []
    for n, ref in enumerate(ins):
        out_ref[n * blk : (n + 1) * blk, :] = ref[0:blk, :]
        parts.append(ref[blk : blk + LABEL_ROWS, 0:blk])
    parts.append(jnp.zeros((LABEL_ROWS, width - len(ins) * blk), jnp.bfloat16))
    out_ref[len(ins) * blk :, :] = jnp.concatenate(parts, axis=1)


def pile_kernel(*refs):
    out_ref, ins = refs[-1], refs[:-1]
    row, strip = 0, out_ref.shape[0] - LABEL_ROWS * len(ins)
    for ref in ins:
        rows = ref.shape[0] - LABEL_ROWS
        out_ref[row : row + rows, :] = ref[0:rows, :]
        out_ref[strip : strip + LABEL_ROWS, :] = ref[rows : rows + LABEL_ROWS, :]
        row, strip = row + rows, strip + LABEL_ROWS


def join(kernel, pieces, rows):
    vmem = pl.BlockSpec(memory_space=pltpu.VMEM)
    return pl.pallas_call(
        kernel,
        out_shape=jax.ShapeDtypeStruct((rows, pieces[0].shape[1]), pieces[0].dtype),
        in_specs=[vmem] * len(pieces),
        out_specs=vmem,
        compiler_params=pltpu.CompilerParams(vmem_limit_bytes=COMPARE_VMEM),
    )(*pieces)


def unpack_kernel(sizes, dest_ref, back_ref, out_ref):
    groups, halves, half, cap, blk = sizes
    side = back_ref.shape[0] // groups
    rows = dest_ref.shape[1]
    dest = dest_ref[...]
    slot = lax.broadcasted_iota(jnp.int32, (blk, rows), 0)
    field = lax.broadcasted_iota(jnp.int32, (LABEL_ROWS, blk), 0)
    total = jnp.zeros((LABEL_ROWS, rows), jnp.float32)
    for k in range(groups):
        value = back_ref[k * side]
        for more in range(1, side):
            value = jnp.maximum(value, back_ref[k * side + more])
        top = value.astype(jnp.bfloat16).astype(jnp.float32)
        rest = value - top
        mid = rest.astype(jnp.bfloat16).astype(jnp.float32)
        low = rest - mid
        stack = jnp.where(field == 0, top, jnp.where(field == 1, mid, jnp.where(field == 2, low, 0.0)))
        pick = (slot + k * blk == dest).astype(jnp.float32).astype(jnp.bfloat16)
        total = total + jnp.dot(stack.astype(jnp.bfloat16), pick, preferred_element_type=jnp.float32)
    value = (total[0:1] + total[1:2]) + total[2:3]
    out_ref[...] = jnp.where(dest >= 0, value, -1.0)


def unpack(dest, back, sizes):
    vmem = pl.BlockSpec(memory_space=pltpu.VMEM)
    return pl.pallas_call(
        functools.partial(unpack_kernel, sizes),
        out_shape=jax.ShapeDtypeStruct(dest.shape, jnp.float32),
        in_specs=[vmem] * 2,
        out_specs=vmem,
        compiler_params=pltpu.CompilerParams(vmem_limit_bytes=COMPARE_VMEM),
    )(dest, back)


def on_device(embeddings, cluster, rank):
    rows_dev, width = embeddings.shape
    groups = lax.axis_size("grp")
    members = lax.axis_size("mem")
    devices = groups * members
    halves = 2 * members
    half = rows_dev // CLUS_GRP // 2
    blk = rows_dev // groups
    cap = blk // halves
    sizes = (groups, halves, half, cap, blk)
    side = members // groups

    def swap(value, block_step, member_step):
        mask = member_step // side * members + block_step * side + member_step % side
        if mask == 0:
            return value
        return lax.ppermute(value, ("grp", "mem"), [(i, i ^ mask) for i in range(devices)])

    offsets, pairs = cover(members)
    sends = [None] * groups
    first = tuple(range(1, min(3, groups)))
    for k, value in zip(first, pack(embeddings, cluster, rank, first, False, sizes)):
        sends[k] = value
    rest = tuple(k for k in range(groups) if k not in first)
    cluster, sends[1] = lax.optimization_barrier((cluster, sends[1]))
    *packed, dest = pack(embeddings, cluster, rank, rest, True, sizes)
    for k, value in zip(rest, packed):
        sends[k] = value

    last = groups - 1
    far = [d for d in offsets if d & side and d != side and d ^ side in offsets]
    near = [d for d in offsets[1:] if d not in far]
    lead = far[0] ^ side if far else near[0]
    held = {0: [sends[0]]}
    for d in near:
        held[d] = [swap(sends[0], 0, d)]
    after = held[lead][0]
    for k in range(1, groups, 2):
        if k > 1:
            send, after = lax.optimization_barrier((sends[k], after))
        else:
            send = sends[k]
        mine = swap(send, k, 0)
        if k < last:
            also = swap(sends[k + 1], k + 1, 0)
            mine = join(pair_kernel, [mine, also], 2 * blk + LABEL_ROWS)
            if k == 1:
                mine, *firsts = lax.optimization_barrier((mine, *(held[d][0] for d in near)))
                for d, value in zip(near, firsts):
                    held[d] = [value]
            after = mine
        held[0].append(mine)
    spots = len(held[0])
    for spot in range(1, spots):
        for d in near:
            if d != side:
                held[d].append(swap(held[0][spot], 0, d))

    index = {d: i for i, d in enumerate(offsets)}
    blocks = {}

    def ks_of(spot):
        return [0] if spot == 0 else [k for k in (2 * spot - 1, 2 * spot) if k < groups]

    def note(d, spot):
        value = held[d][spot]
        first = value.shape[0] - LABEL_ROWS
        for at, k in enumerate(ks_of(spot)):
            blocks[index[d], k] = (value, at * blk, first, at * blk)

    for d in held:
        for spot in range(len(held[d])):
            note(d, spot)
    pile = [(side, spot) for spot in range(1, spots)]
    pile += [(d, spot) for d in far for spot in range(spots - 1)]
    hops = [d for d in near if d != side and d not in [e ^ side for e in far]]
    values = [held[d][spots - 2] for d in hops]
    held[0][-1], *values = lax.optimization_barrier((held[0][-1], *values))
    for d, value in zip(hops, values):
        held[d][spots - 2] = value
        note(d, spots - 2)
    note(0, spots - 1)
    ahead = [(d, spot) for d, spot in pile if spot < (spots - 1 if d == side else 1)]
    behind = [item for item in pile if item not in ahead] + [(d, spots - 1) for d in far]

    def cross(some, after):
        parts = [held[d ^ side][spot] for d, spot in some]
        parts[0], *after = lax.optimization_barrier((parts[0], *after))
        data = sum(part.shape[0] - LABEL_ROWS for part in parts)
        moved = swap(join(pile_kernel, parts, data + LABEL_ROWS * len(parts)), 0, side)
        row = 0
        for n, (d, spot) in enumerate(some):
            for at, k in enumerate(ks_of(spot)):
                blocks[index[d], k] = (moved, row + at * blk, data + LABEL_ROWS * n, at * blk)
            row += parts[n].shape[0] - LABEL_ROWS
        return after

    cross(ahead, [])
    final = {(index[d], k) for d, spot in behind for k in ks_of(spot)}

    starts = sorted({a for a, _ in pairs.values()})
    every = tuple(range(groups))
    early, middle, late = [], [], []
    for a in starts:
        cols = [index[b] for _, (e, b) in sorted(pairs.items()) if e == a]
        pieces = [(b, k) for b in cols for k in every]
        soon = [(b, k) for b, k in pieces if k < last]
        soon = [piece for piece in soon if piece not in final]
        if a == 0:
            done = [p for p in pieces if p in soon or p[0] == 0]
            early.append((0, False, every, done))
            late.append((0, False, every, [p for p in pieces if p not in done]))
        else:
            middle.append((index[a], False, every[:-1], soon))
            late.append((index[a], False, every, [p for p in pieces if p not in soon]))
            late.append((index[a], True, (last,), soon))
    order = [index[a] for a in starts]
    joined = side if all(a < side for a in starts) else 0
    prev = compare(blocks, early, None, (), (), 0, offsets, sizes)[0]
    prev = compare(blocks, middle, prev, (), (), 0, offsets, sizes)[0]
    wholes = [(a, k) for a, whole, ks, _ in late if whole for k in ks]
    before = [(*job, [p for p in pieces if p not in final]) for *job, pieces in late]
    late = [(*job, [p for p in pieces if p in final]) for *job, pieces in late]
    late = [job for job in late if job[-1]]
    hops = [d for d in near if d != side]
    prev, *values = cross(behind, [prev, *(held[d][-1] for d in hops)])
    for d, value in zip(hops, values):
        blocks[index[d], last] = (value, *blocks[index[d], last][1:])
    prev, turned = compare(blocks, before, prev, (), (), 0, offsets, sizes, keep=True)
    found = compare(blocks, late, prev, order, wholes, joined, offsets, sizes, cache=turned)
    if joined:
        back = found[0]
    else:
        best = {}
        for a, value in zip(starts, found):
            near = a % side
            value = swap(value, 0, a - near)
            best[near] = jnp.maximum(best[near], value) if near in best else value
        none = jnp.full_like(found[0], -1.0)
        near_of = [best.get(near, none) for near in range(side)]
        rows_of = []
        for spot in range(side):
            value = near_of[spot]
            for mine in range(1, side):
                value = jnp.where(lax.axis_index("mem") % side == mine, near_of[spot ^ mine], value)
            rows_of.append(value)
        back = jnp.stack(rows_of, axis=1).reshape(groups * side, 1, blk)
    back = lax.all_to_all(back, "mem", split_axis=0, concat_axis=0, tiled=True)
    return unpack(dest, back, sizes).reshape(rows_dev)


def solution(mesh):
    in_specs = (P(("grp", "mem"), None), P(("grp", "mem")), P(("grp", "mem")))
    out_specs = P(("grp", "mem"))
    return jax.shard_map(
        on_device, mesh=mesh, in_specs=in_specs, out_specs=out_specs, check_vma=False
    )
```
